256 devices in a mesh: blk: 32 (over x, z_hi, y), sub: 8 (over z_lo, core).
Axes of the slice: x: 4, y: 4, z: 8 (z_hi: 2, z_lo: 4; z = z_hi * 4 + z_lo), core: 2. Of those that a mesh axis runs over, the one named last changes fastest.
Arguments:
- features: bfloat16 [131072, 256], P(('blk', 'sub')), may hold values from -8 to 8
- w_query: bfloat16 [256, 256], replicated, may hold values from -0.3984375 to 0.3984375
- key_weight: bfloat16 [256, 256], replicated, may hold values from -0.3984375 to 0.3984375
- value_weight: bfloat16 [256, 256], replicated, may hold values from -0.375 to 0.375
- w_output: bfloat16 [256, 256], replicated, may hold values from -0.375 to 0.375
- virtual_node: bfloat16 [256], replicated, may hold values from -4 to 4
- cotangent: bfloat16 [131072, 256], P(('blk', 'sub')), may hold values from -8 to 8
- local_mask: int32 [131072, 512], P(('blk', 'sub')), may hold values 0 or 1
- counts: int32 [256], P(('blk', 'sub')), may hold values from 128 to 512, as said below
- shifts: int32 [4], replicated, may hold values from 1 to 31, as said below
Outputs:
- layer_out: bfloat16 [131072, 256], P(('blk', 'sub'))
- grad_features: bfloat16 [131072, 256], P(('blk', 'sub'))
- grad_query: float32 [256, 256], replicated
- key_weight_gradient: float32 [256, 256], replicated
- grad_value: float32 [256, 256], replicated
- grad_output: float32 [256, 256], replicated
- grad_virtual: float32 [256], replicated
The draws below stay inside these ranges and needn't reach their ends.
Inputs may be any that keep to these rules, and one draw needn't show every extreme that they name: `counts`: at least one block has 512 live slots and at least one has 128. `shifts`: the 4 values are distinct; 1 and the largest are among them.
All inputs are finite; a program needn't handle non-finite values. No bound on the sum of `local_mask` on one device may be relied on, other than what follows from the above.
Results may differ from the reference program's by a relative error of at most 0.02.
Values may be sent and summed in bfloat16 or wider, within the bound.
No kernel may reach another device: no remote copies, remote signals or barrier semaphores. Data moves between devices by JAX's collectives and lax.ppermute only.
A program may use at most 128 MiB of HBM per device.

```python
import math
import jax
import jax.numpy as jnp
from jax import lax

D = 256
HEADS = 8
MATCHINGS = 4
BN = 512
NODES = 131072
N_BLK = 32
N_SUB = 8


def block_spike(key, factor):
    blocks = NODES // BN
    order = jax.random.permutation(key, D).astype(jnp.int32)
    chosen = order[jnp.arange(blocks, dtype=jnp.int32) % D]
    hit = (jnp.arange(D, dtype=jnp.int32)[None, :] == chosen[:, None]).astype(jnp.float32)
    return jnp.repeat(1.0 + (factor - 1.0) * hit, BN, axis=0)


def draw_features(key, part):
    key = jax.random.fold_in(key, 11)
    noise_key, mean_key, spike_key = jax.random.split(key, 3)
    position = jnp.arange(NODES, dtype=jnp.float32)[:, None] / NODES
    noise = 0.9 * jax.random.truncated_normal(noise_key, -2.5, 2.5, (NODES, D), jnp.float32)
    column_mean = 0.35 * jax.random.truncated_normal(mean_key, -2.0, 2.0, (1, D), jnp.float32)
    ramp = 0.3 + 1.2 * position
    return (noise * block_spike(spike_key, 3.0) + column_mean * ramp).astype(jnp.bfloat16)


def draw_cotangent(key, part):
    key = jax.random.fold_in(key, 14)
    noise_key, spike_key = jax.random.split(key)
    position = jnp.arange(NODES, dtype=jnp.float32)[:, None] / NODES
    noise = 0.4 * jax.random.truncated_normal(noise_key, -2.5, 2.5, (NODES, D), jnp.float32)
    ramp = 0.4 + 1.2 * position
    return (noise * ramp * block_spike(spike_key, 2.5)).astype(jnp.bfloat16)


def draw_counts(key, part):
    key = jax.random.fold_in(key, 12)
    count_key, spot_key = jax.random.split(key)
    blocks = NODES // BN
    values = jax.random.randint(count_key, (blocks,), BN // 4, BN + 1, jnp.int32)
    chosen_spot = jax.random.randint(spot_key, (), 0, blocks, jnp.int32)
    values = values.at[chosen_spot].set(BN)
    values = values.at[(chosen_spot + blocks // 2) % blocks].set(BN // 4)
    return values.astype(jnp.int32)


def draw_shifts(key, part):
    key = jax.random.fold_in(key, 13)
    pick_key, order_key = jax.random.split(key)
    middle = jax.random.permutation(pick_key, N_BLK - 3)[:2].astype(jnp.int32) + 2
    values = jnp.concatenate([jnp.array([1, N_BLK - 1], jnp.int32), middle])
    return jax.random.permutation(order_key, values).astype(jnp.int32)


def place_ends(values, key, smallest, high):
    dims = values.shape
    place = [jax.random.randint(jax.random.fold_in(key, axis), (), 0, dims[axis]) for axis in range(len(dims))]
    values = values.at[tuple(place)].set(smallest)
    longest = dims.index(max(dims))
    place[longest] = (place[longest] + 1) % dims[longest]
    return values.at[tuple(place)].set(high)


def scatter_about(own_key, extent, deviation, most, kind=jnp.bfloat16):
    result = deviation * jax.random.normal(own_key, extent, jnp.float32)
    return jnp.clip(result, min=-most, max=most).astype(kind)


def setup_inputs(seed: int = 0) -> dict:
    streams_of = jax.random.split(jax.random.key(seed), 11)
    return {
        "features": draw_features(jax.random.fold_in(streams_of[10], 71), 0),
        "w_query": scatter_about(streams_of[1], (D, D), 0.1, 0.3984375),
        "key_weight": scatter_about(streams_of[2], (D, D), 0.1, 0.3984375),
        "value_weight": scatter_about(streams_of[3], (D, D), D ** -0.5, 0.375),
        "w_output": scatter_about(streams_of[4], (D, D), D ** -0.5, 0.375),
        "virtual_node": scatter_about(streams_of[5], (D,), 1.0, 4.0),
        "cotangent": draw_cotangent(jax.random.fold_in(streams_of[10], 71), 0),
        "local_mask": place_ends((jax.random.randint(streams_of[7], (NODES, BN), 0, 2) < 1).astype(jnp.int32), jax.random.fold_in(streams_of[7], 1), 0, 1),
        "counts": draw_counts(jax.random.fold_in(streams_of[10], 71), 0),
        "shifts": draw_shifts(jax.random.fold_in(streams_of[10], 71), 0),
    }


NEG_FILL = -1000000000.0

def split_heads(matrix):
    return matrix.reshape(matrix.shape[0], HEADS, -1).transpose(1, 0, 2)

def join_heads(stacked):
    return stacked.transpose(1, 0, 2).reshape(stacked.shape[1], -1)

def build_bias(mask_tile, own_count, far_counts, block_rows):
    column = lax.broadcasted_iota(jnp.int32, (block_rows, block_rows), 1)
    row_index = lax.broadcasted_iota(jnp.int32, (block_rows, block_rows), 0)
    local_ok = ((mask_tile != 0) | (row_index == column)) & (column < own_count)
    pieces = [jnp.where(local_ok, 0.0, NEG_FILL).astype(jnp.float32)]
    for match_no in range(MATCHINGS):
        pieces.append(jnp.where(column < far_counts[match_no], 0.0, NEG_FILL).astype(jnp.float32))
    pieces.append(jnp.full((block_rows, 1), math.log(block_rows), jnp.float32))
    return jnp.concatenate(pieces, axis=1)

def attend_forward(queries, key_table, value_table, score_bias):
    score_scale = 1.0 / math.sqrt(D // HEADS)

    def one_head(packed):
        head_query, head_key, head_value = packed
        scores = jnp.einsum('qd,kd->qk', head_query.astype(jnp.float32), head_key.astype(jnp.float32)) * score_scale + score_bias
        row_top = lax.optimization_barrier(jnp.max(scores, axis=1, keepdims=True))
        weights = jnp.exp(scores - row_top)
        row_total = lax.optimization_barrier(jnp.sum(weights, axis=1, keepdims=True))
        probs = (weights / row_total).astype(jnp.bfloat16)
        head_out = jnp.einsum('qk,kd->qd', probs.astype(jnp.float32), head_value.astype(jnp.float32))
        return (head_out, (row_top + jnp.log(row_total))[:, 0])
    outputs, log_norms = lax.map(one_head, (split_heads(queries), split_heads(key_table), split_heads(value_table)))
    return (join_heads(outputs).astype(jnp.bfloat16), log_norms)

def attend_backward(queries, key_table, value_table, grad_attn, log_norms, score_bias, attn_out):
    score_scale = 1.0 / math.sqrt(D // HEADS)
    row_delta = lax.optimization_barrier(jnp.sum(split_heads(grad_attn).astype(jnp.float32) * split_heads(attn_out).astype(jnp.float32), axis=2))

    def one_head(packed):
        head_query, head_key, head_value, head_grad, log_norm, delta_row = packed
        scores = jnp.einsum('qd,kd->qk', head_query.astype(jnp.float32), head_key.astype(jnp.float32)) * score_scale + score_bias
        probs = jnp.exp(scores - log_norm[:, None])
        grad_probs = jnp.einsum('qd,kd->qk', head_grad.astype(jnp.float32), head_value.astype(jnp.float32))
        dscore = (probs * (grad_probs - delta_row[:, None]) * score_scale).astype(jnp.bfloat16)
        probs_low = probs.astype(jnp.bfloat16)
        dquery = jnp.einsum('qk,kd->qd', dscore.astype(jnp.float32), head_key.astype(jnp.float32))
        key_gradient = jnp.einsum('qk,qd->kd', dscore.astype(jnp.float32), head_query.astype(jnp.float32))
        dvalue = jnp.einsum('qk,qd->kd', probs_low.astype(jnp.float32), head_grad.astype(jnp.float32))
        return (dquery, key_gradient, dvalue)
    dquery, key_gradient, dvalue = lax.map(one_head, (split_heads(queries), split_heads(key_table), split_heads(value_table), split_heads(grad_attn), log_norms, row_delta))
    return (join_heads(dquery), join_heads(key_gradient), join_heads(dvalue))

def reference(features, w_query, key_weight, value_weight, w_output, virtual_node, cotangent, local_mask, counts, shifts):
    block_rows = BN
    block_count = NODES // BN
    queries = jnp.dot(features, w_query, preferred_element_type=jnp.float32).astype(jnp.bfloat16)
    key_rows = jnp.dot(features, key_weight, preferred_element_type=jnp.float32).astype(jnp.bfloat16)
    value_rows = jnp.dot(features, value_weight, preferred_element_type=jnp.float32).astype(jnp.bfloat16)
    virtual_key = jnp.dot(virtual_node[None, :], key_weight, preferred_element_type=jnp.float32).astype(jnp.bfloat16)
    virtual_value = jnp.dot(virtual_node[None, :], value_weight, preferred_element_type=jnp.float32).astype(jnp.bfloat16)
    query_blocks = queries.reshape(N_BLK, N_SUB, block_rows, D)
    key_blocks = key_rows.reshape(N_BLK, N_SUB, block_rows, D)
    value_blocks = value_rows.reshape(N_BLK, N_SUB, block_rows, D)
    mask_blocks = local_mask.reshape(N_BLK, N_SUB, block_rows, block_rows)
    count_blocks = counts.reshape(N_BLK, N_SUB)

    def gather_side(block_id):
        major = block_id // N_SUB
        minor = block_id % N_SUB
        partners = jnp.bitwise_xor(major, shifts)
        key_table = jnp.concatenate([key_blocks[major, minor]] + [key_blocks[partners[m_no], minor] for m_no in range(MATCHINGS)] + [virtual_key], axis=0)
        value_table = jnp.concatenate([value_blocks[major, minor]] + [value_blocks[partners[m_no], minor] for m_no in range(MATCHINGS)] + [virtual_value], axis=0)
        far_counts = [count_blocks[partners[m_no], minor] for m_no in range(MATCHINGS)]
        score_bias = build_bias(mask_blocks[major, minor], count_blocks[major, minor], far_counts, block_rows)
        return (query_blocks[major, minor], key_table, value_table, score_bias)

    def forward_one(block_id):
        block_query, key_table, value_table, score_bias = gather_side(block_id)
        return attend_forward(block_query, key_table, value_table, score_bias)
    block_ids = jnp.arange(block_count, dtype=jnp.int32)
    attn_blocks, norm_blocks = lax.map(forward_one, block_ids)
    attn = attn_blocks.reshape(NODES, D)
    layer_out = (features.astype(jnp.float32) + jnp.dot(attn, w_output, preferred_element_type=jnp.float32)).astype(jnp.bfloat16)
    grad_attn = jnp.dot(cotangent, w_output.T, preferred_element_type=jnp.float32).astype(jnp.bfloat16)
    grad_output = jnp.dot(attn.T, cotangent, preferred_element_type=jnp.float32)
    grad_blocks = grad_attn.reshape(block_count, block_rows, D)

    def backward_one(block_id):
        block_query, key_table, value_table, score_bias = gather_side(block_id)
        dquery, key_gradient_table, dvalue_table = attend_backward(block_query, key_table, value_table, grad_blocks[block_id], norm_blocks[block_id], score_bias, attn_blocks[block_id])
        remote_endpoint = block_rows * (MATCHINGS + 1)
        return (dquery.astype(jnp.bfloat16), key_gradient_table[:block_rows], key_gradient_table[block_rows:remote_endpoint].reshape(MATCHINGS, block_rows, D).astype(jnp.bfloat16), key_gradient_table[remote_endpoint], dvalue_table[:block_rows], dvalue_table[block_rows:remote_endpoint].reshape(MATCHINGS, block_rows, D).astype(jnp.bfloat16), dvalue_table[remote_endpoint])
    dquery, dkey_own, dkey_far, virtual_key_gradient, dvalue_own, dvalue_far, dvalue_virt = lax.map(backward_one, block_ids)
    dkey_far = dkey_far.reshape(N_BLK, N_SUB, MATCHINGS, block_rows, D)
    dvalue_far = dvalue_far.reshape(N_BLK, N_SUB, MATCHINGS, block_rows, D)
    dkey_sum = dkey_own.reshape(N_BLK, N_SUB, block_rows, D)
    dvalue_sum = dvalue_own.reshape(N_BLK, N_SUB, block_rows, D)
    block_index = jnp.arange(N_BLK, dtype=jnp.int32)
    for match_no in range(MATCHINGS):
        senders = jnp.bitwise_xor(block_index, shifts[match_no])
        dkey_sum = dkey_sum + jnp.take(dkey_far[:, :, match_no], senders, axis=0).astype(jnp.float32)
        dvalue_sum = dvalue_sum + jnp.take(dvalue_far[:, :, match_no], senders, axis=0).astype(jnp.float32)
    key_gradient = dkey_sum.reshape(NODES, D).astype(jnp.bfloat16)
    dvalue = dvalue_sum.reshape(NODES, D).astype(jnp.bfloat16)
    dquery = dquery.reshape(NODES, D)
    virtual_node_key = lax.optimization_barrier(jnp.sum(virtual_key_gradient, axis=0))
    virtual_node_value = lax.optimization_barrier(jnp.sum(dvalue_virt, axis=0))
    grad_virtual = (jnp.dot(virtual_node_key[None, :], key_weight.astype(jnp.float32).T, precision=lax.Precision.HIGHEST) + jnp.dot(virtual_node_value[None, :], value_weight.astype(jnp.float32).T, precision=lax.Precision.HIGHEST))[0]
    grad_features = (cotangent.astype(jnp.float32) + jnp.dot(dquery, w_query.T, preferred_element_type=jnp.float32) + jnp.dot(key_gradient, key_weight.T, preferred_element_type=jnp.float32) + jnp.dot(dvalue, value_weight.T, preferred_element_type=jnp.float32)).astype(jnp.bfloat16)
    virtual_broadcast = virtual_node.astype(jnp.float32)
    grad_query = jnp.dot(features.T, dquery, preferred_element_type=jnp.float32)
    key_weight_gradient = jnp.dot(features.T, key_gradient, preferred_element_type=jnp.float32) + virtual_broadcast[:, None] * virtual_node_key[None, :]
    grad_value = jnp.dot(features.T, dvalue, preferred_element_type=jnp.float32) + virtual_broadcast[:, None] * virtual_node_value[None, :]
    return (layer_out, grad_features, grad_query, key_weight_gradient, grad_value, grad_output, grad_virtual)
```

```python
import functools
import math

import jax
import jax.numpy as jnp
from jax import lax
from jax.experimental import pallas as pl
from jax.experimental.pallas import tpu as pltpu
from jax.sharding import PartitionSpec as P

D = 256
HEADS = 8
HD = D // HEADS
GROUP = 128 // HD
CHUNKS = 5
BN = 512
KEYS = CHUNKS * BN
SENT = BN + 16
NEG_FILL = -1000000000.0
SCALE = 1.0 / math.sqrt(HD)
LOG2E = 1.0 / math.log(2.0)
LN2 = math.log(2.0)
TILE = 256
BF = jnp.bfloat16
F32 = jnp.float32


def dot(a, b):
    return jnp.dot(a, b, preferred_element_type=F32)


def dot_nt(a, b):
    return lax.dot_general(a, b, (((1,), (1,)), ((), ())), preferred_element_type=F32)


def dot_nt_exact(a, b):
    return lax.dot_general(
        a, b.astype(F32), (((1,), (1,)), ((), ())), precision=lax.Precision.HIGHEST,
        preferred_element_type=F32,
    )


def attend_kernel(
    count_ref, x_ref, p0_ref, p1_ref, p2_ref, p3_ref, wq_ref, wk_ref, wv_ref, wo_ref, vn_ref,
    cot_ref, mask_ref,
    layer_ref, own_ref, b0_ref, b1_ref, b2_ref, b3_ref, weight_ref, virt_ref,
    qmt, qm, gt, ks, vs, vta, k0t, xt, bias, s_buf, p_buf, dk_acc, dv_acc, attn_t, dq_t,
    sv, dpv, dsv, pvn,
):
    parts = (x_ref, p0_ref, p1_ref, p2_ref, p3_ref)
    x = x_ref[...]
    wq, wk, wv, wo = wq_ref[...], wk_ref[...], wv_ref[...], wo_ref[...]
    vn = jnp.broadcast_to(vn_ref[...], (16, D))
    vk = dot(vn, wk).astype(BF)
    vv = dot(vn, wv).astype(BF)

    q32 = dot(x, wq) * (SCALE * LOG2E)
    qs = q32.astype(BF)
    qt = q32.T.astype(BF)
    cot = cot_ref[...]
    g32 = dot_nt(cot, wo)
    g = g32.astype(BF)
    gt_all = g32.T.astype(BF)
    gt[...] = gt_all.reshape(HEADS, HD, BN)
    qmt[...] = jnp.zeros_like(qmt)
    lane_head = lax.broadcasted_iota(jnp.int32, (BN, 128), 1) // HD
    for h in range(HEADS):
        r = h % GROUP
        lo = (h // GROUP) * 128
        qmt[h, r * HD:(r + 1) * HD, :] = qt[h * HD:(h + 1) * HD]
        qm[h] = jnp.where(lane_head == r, qs[:, lo:lo + 128], jnp.zeros((), BF))

    head_of = lax.broadcasted_iota(jnp.int32, (16, D), 1) // HD
    diag = head_of == lax.broadcasted_iota(jnp.int32, (16, D), 0)
    sv[...] = dot(jnp.where(diag, vk, jnp.zeros((), BF)), qt)[:HEADS].reshape(HEADS, 1, BN) + math.log2(BN)
    dpv[...] = dot(jnp.where(diag, vv, jnp.zeros((), BF)), gt_all)[:HEADS].reshape(HEADS, 1, BN)
    vkt = jnp.broadcast_to(vk[:1].astype(F32), (128, D)).T
    vvt = jnp.broadcast_to(vv[:1].astype(F32), (128, D)).T

    key_row = lax.broadcasted_iota(jnp.int32, (BN, BN), 0)
    query_col = lax.broadcasted_iota(jnp.int32, (BN, BN), 1)
    linked = mask_ref[...].astype(F32).T
    ok = ((linked != 0.0) | (key_row == query_col)) & (key_row < count_ref[0])
    bias[...] = jnp.where(ok, 0.0, NEG_FILL)

    row_no = lax.broadcasted_iota(jnp.int32, (BN, D), 0).astype(F32)
    lane_no = lax.broadcasted_iota(jnp.int32, (16, BN), 1).astype(F32)
    for c in range(CHUNKS):
        rows = slice(c * BN, (c + 1) * BN)
        xc = parts[c][:BN, :]
        k32 = dot(xc, wk)
        v32 = dot(xc, wv)
        k = k32.astype(BF)
        live_row = jnp.ones((16, BN), BF)
        if c:
            tail = parts[c][BN:, :].astype(F32)
            count = tail[0:1, 0:1] + 256.0 * tail[1:2, 0:1]
            live = row_no < count
            k = jnp.where(live, k, jnp.broadcast_to(vk[:1], (BN, D)))
            k32 = jnp.where(live, k32, 0.0)
            v32 = jnp.where(live, v32, 0.0)
            live_row = jnp.where(lane_no < count, 1.0, 0.0).astype(BF)
        v = v32.astype(BF)
        for gi in range(2):
            ks[gi, rows, :] = k[:, gi * 128:(gi + 1) * 128]
            vs[gi, rows, :] = v[:, gi * 128:(gi + 1) * 128]
        vt = v32.T.astype(BF)
        k0t[:, :, rows] = k32.T.astype(BF).reshape(HEADS, HD, BN)
        xt[c] = xc.astype(F32).T.astype(BF)
        for h in range(HEADS):
            vta[h, :HD, rows] = vt[h * HD:(h + 1) * HD]
            vta[h, HD:, rows] = live_row

    dk_acc[...] = jnp.zeros_like(dk_acc)
    dv_acc[...] = jnp.zeros_like(dv_acc)
    row_head = lax.broadcasted_iota(jnp.int32, (128, BN), 0) // HD
    vk_cols = vkt[:, :1].reshape(HEADS, HD, 1)
    vv_cols = vvt[:, :1].reshape(HEADS, HD, 1)

    for h in range(HEADS):
        gi = h // GROUP
        top = sv[h]
        peak = jnp.full((8, BN), -jnp.inf, F32)
        for t in range(KEYS // TILE):
            rows = pl.ds(t * TILE, TILE)
            s = dot(ks[gi, rows, :], qmt[h])
            if (t + 1) * TILE <= BN:
                s = s + bias[rows, :]
            s_buf[rows, :] = s
            peak = jnp.maximum(peak, jnp.max(s.reshape(TILE // 8, 8, BN), axis=0))
        top = jnp.maximum(top, jnp.max(peak, axis=0, keepdims=True))
        out = jnp.zeros((HD + 16, BN), F32)
        for t in range(KEYS // TILE):
            rows = pl.ds(t * TILE, TILE)
            p = jnp.exp2(s_buf[rows, :] - top).astype(BF)
            p_buf[rows, :] = p
            out = out + dot(vta[h, :, rows], p)
        pv = jnp.exp2(sv[h] - top)
        inv = 1.0 / (out[HD:HD + 1] + pv)
        attn_h = ((out[:HD] + vv_cols[h] * pv) * inv).astype(BF)
        attn_t[h] = attn_h
        g_h = gt[h].astype(F32)
        delta = jnp.sum(g_h * attn_h.astype(F32), axis=0, keepdims=True) * inv
        g_n = g_h * inv
        gmt32 = jnp.where(
            row_head == h % GROUP, jnp.concatenate([g_n] * GROUP, axis=0), 0.0
        )
        gmt = gmt32.astype(BF)
        gm = gmt32.T.astype(BF)
        dsv_h = pv * (dpv[h] * inv - delta)
        dsv[h] = dsv_h
        pvn[h] = pv * inv
        dq = vk_cols[h] * dsv_h
        for t in range(KEYS // TILE):
            rows = pl.ds(t * TILE, TILE)
            p = p_buf[rows, :]
            ds = (dot(vs[gi, rows, :], gmt) - delta).astype(BF) * p
            dq = dq + dot(k0t[h, :, rows], ds)
            dk_acc[gi, rows, :] += dot(ds, qm[h])
            dv_acc[gi, rows, :] += dot(p, gm)
        dq_t[h] = (dq * SCALE).astype(BF)

    at = attn_t[...].reshape(D, BN)
    attn = at.astype(F32).T.astype(BF)
    layer_ref[...] = (x.astype(F32) + dot(attn, wo)).astype(BF)
    dqt = dq_t[...].reshape(D, BN)
    dqm = dqt.astype(F32).T.astype(BF)

    grad_query = dot(xt[0], dqm)
    grad_output = dot(at, cot)
    keep = diag[:HEADS]
    dsv_all = dsv[...].reshape(HEADS, BN)
    pvn_all = pvn[...].reshape(HEADS, BN)
    vkey = jnp.sum(jnp.where(keep, dot(dsv_all.astype(BF), qs), 0.0), axis=0, keepdims=True) * LN2
    vvalue = jnp.sum(jnp.where(keep, dot(pvn_all.astype(BF), g), 0.0), axis=0, keepdims=True)
    vn_col = jnp.broadcast_to(vn_ref[...].astype(F32), (128, D)).T[:, :1]
    grad_key = vn_col * vkey
    grad_value = vn_col * vvalue
    backs = (None, b0_ref, b1_ref, b2_ref, b3_ref)
    for c in range(CHUNKS):
        rows = slice(c * BN, (c + 1) * BN)
        dk = jnp.concatenate([dk_acc[0, rows, :], dk_acc[1, rows, :]], axis=1) * LN2
        dv = jnp.concatenate([dv_acc[0, rows, :], dv_acc[1, rows, :]], axis=1)
        if c:
            tail = parts[c][BN:, :].astype(F32)
            live = row_no < tail[0:1, 0:1] + 256.0 * tail[1:2, 0:1]
            dk = jnp.where(live, dk, 0.0)
            dv = jnp.where(live, dv, 0.0)
        dk = dk.astype(BF)
        dv = dv.astype(BF)
        grad_key = grad_key + dot(xt[c], dk)
        grad_value = grad_value + dot(xt[c], dv)
        back = dot_nt(dk, wk) + dot_nt(dv, wv)
        if c:
            backs[c][...] = back.astype(BF)
        else:
            own_ref[...] = back + dot_nt(dqm, wq) + cot.astype(F32)
    for n, grad in enumerate((grad_query, grad_key, grad_value, grad_output)):
        for j in range(2):
            weight_ref[n * 32:(n + 1) * 32, j] = grad[:, j * 128:(j + 1) * 128].reshape(32, 8, 128)
    virt = dot_nt_exact(jnp.broadcast_to(vkey, (8, D)), wk) + dot_nt_exact(
        jnp.broadcast_to(vvalue, (8, D)), wv
    )
    virt_ref[...] = virt


def attend(count, x, partners, wq, wk, wv, wo, vn, cot, mask):
    vmem = pl.BlockSpec(memory_space=pltpu.VMEM)
    sds = jax.ShapeDtypeStruct
    return pl.pallas_call(
        attend_kernel,
        out_shape=(
            sds((BN, D), BF), sds((BN, D), F32), sds((BN, D), BF), sds((BN, D), BF),
            sds((BN, D), BF), sds((BN, D), BF), sds((128, 2, 8, 128), F32), sds((8, D), F32),
        ),
        in_specs=[pl.BlockSpec(memory_space=pltpu.SMEM)] + [vmem] * 12,
        out_specs=[vmem] * 8,
        scratch_shapes=[
            pltpu.VMEM((HEADS, 128, BN), BF),
            pltpu.VMEM((HEADS, BN, 128), BF),
            pltpu.VMEM((HEADS, HD, BN), BF),
            pltpu.VMEM((2, KEYS, 128), BF),
            pltpu.VMEM((2, KEYS, 128), BF),
            pltpu.VMEM((HEADS, HD + 16, KEYS), BF),
            pltpu.VMEM((HEADS, HD, KEYS), BF),
            pltpu.VMEM((CHUNKS, D, BN), BF),
            pltpu.VMEM((BN, BN), F32),
            pltpu.VMEM((KEYS, BN), F32),
            pltpu.VMEM((KEYS, BN), BF),
            pltpu.VMEM((2, KEYS, 128), F32),
            pltpu.VMEM((2, KEYS, 128), F32),
            pltpu.VMEM((HEADS, HD, BN), BF),
            pltpu.VMEM((HEADS, HD, BN), BF),
            pltpu.VMEM((HEADS, 1, BN), F32),
            pltpu.VMEM((HEADS, 1, BN), F32),
            pltpu.VMEM((HEADS, 1, BN), F32),
            pltpu.VMEM((HEADS, 1, BN), F32),
        ],
        compiler_params=pltpu.CompilerParams(vmem_limit_bytes=56 * 1024 * 1024),
        cost_estimate=pl.CostEstimate(flops=8 * 10**9, bytes_accessed=4 * 10**6, transcendentals=10**7),
        name="attend",
    )(count, x, *partners, wq, wk, wv, wo, vn, cot, mask)


def exchange(array, distance):
    return lax.ppermute(array, "blk", [(i, i ^ distance) for i in range(lax.axis_size("blk"))])


def exchange_by(array, distance):
    size = lax.axis_size("blk")
    branches = [functools.partial(exchange, distance=d) for d in range(2, size - 1)]
    return lax.switch(distance - 2, branches, array)


def body(
    features, w_query, key_weight, value_weight, w_output, virtual_node, cotangent, local_mask,
    counts, shifts,
):
    largest = lax.axis_size("blk") - 1
    low = jnp.min(jnp.where(shifts == 1, largest + 1, shifts))
    high = jnp.max(jnp.where(shifts == largest, 0, shifts))
    own = counts[0]
    halves = jnp.stack([own & 255, own >> 8]).astype(BF)
    tail = jnp.zeros((SENT - BN, D), BF).at[:2].set(jnp.broadcast_to(halves[:, None], (2, D)))
    sent = jnp.concatenate([features, tail], axis=0)
    partners = [exchange(sent, largest), exchange(sent, 1), exchange_by(sent, low), exchange_by(sent, high)]
    layer_out, own_grad, back_far, back_near, back_low, back_high, weights, virt = attend(
        counts, features, partners, w_query, key_weight, value_weight, w_output,
        virtual_node[None, :], cotangent, local_mask,
    )
    everyone = ("blk", "sub")
    scattered = lax.all_to_all(weights.reshape(256, 8, 128), everyone, 0, 0)
    chunk = jnp.sum(scattered, axis=0)
    summed = lax.all_to_all(jnp.broadcast_to(chunk, (256, 8, 128)), everyone, 0, 0)
    summed = summed.reshape(128, 2, 8, 128).transpose(0, 2, 1, 3).reshape(4, D, D)
    grad_virtual = jnp.sum(lax.all_gather(virt[0], everyone), axis=0)
    returned = [exchange(back_far, largest), exchange(back_near, 1), exchange_by(back_low, low), exchange_by(back_high, high)]
    total = own_grad
    for part in returned:
        total = total + part.astype(F32)
    return (
        layer_out, total.astype(BF), summed[0], summed[1], summed[2], summed[3], grad_virtual,
    )


def solution(mesh):
    return jax.shard_map(
        body,
        mesh=mesh,
        in_specs=(
            P(("blk", "sub"), None), P(), P(), P(), P(), P(), P(("blk", "sub"), None),
            P(("blk", "sub"), None), P(("blk", "sub")), P(),
        ),
        out_specs=(P(("blk", "sub"), None), P(("blk", "sub"), None), P(), P(), P(), P(), P()),
        check_vma=False,
    )
```

```python
import functools
import math

import jax
import jax.numpy as jnp
from jax import lax
from jax.experimental import pallas as pl
from jax.experimental.pallas import tpu as pltpu
from jax.sharding import PartitionSpec as P

D = 256
HEADS = 8
HD = D // HEADS
GROUP = 128 // HD
CHUNKS = 5
BN = 512
KEYS = CHUNKS * BN
SENT = BN + 16
NEG_FILL = -1000000000.0
SCALE = 1.0 / math.sqrt(HD)
LOG2E = 1.0 / math.log(2.0)
LN2 = math.log(2.0)
TILE = 512
BF = jnp.bfloat16
F32 = jnp.float32


def dot(a, b):
    return jnp.dot(a, b, preferred_element_type=F32)


def dot_nt(a, b):
    return lax.dot_general(a, b, (((1,), (1,)), ((), ())), preferred_element_type=F32)


def dot_nt_exact(a, b):
    return lax.dot_general(
        a, b.astype(F32), (((1,), (1,)), ((), ())), precision=lax.Precision.HIGHEST,
        preferred_element_type=F32,
    )


def attend_kernel(
    count_ref, core_ref, x_ref, p0_ref, p1_ref, p2_ref, p3_ref, wq_ref, wk_ref, wv_ref, wo_ref, vn_ref,
    cot_ref, mask_ref,
    layer_ref, own_ref, b0_ref, b1_ref, b2_ref, b3_ref, weight_ref, virt_ref,
    qmt, qm, gt, ks, vs, vta, k0t, xt, bias, s_even, s_odd, p_even, p_odd, gmt_even, gmt_odd,
    gm_even, gm_odd, dk_acc, dv_acc, attn_t, dq_t, sv, dpv, dsv, pvn, tops, deltas, vk_cols, vv_cols,
):
    parts = (x_ref, p0_ref, p1_ref, p2_ref, p3_ref)
    x = x_ref[...]
    wq, wk, wv, wo = wq_ref[...], wk_ref[...], wv_ref[...], wo_ref[...]
    vn = jnp.broadcast_to(vn_ref[...], (16, D))
    vk = dot(vn, wk).astype(BF)
    vv = dot(vn, wv).astype(BF)

    q32 = dot(x, wq) * (SCALE * LOG2E)
    qs = q32.astype(BF)
    qt = q32.T.astype(BF)
    cot = cot_ref[...]
    g32 = dot_nt(cot, wo)
    g = g32.astype(BF)
    gt_all = g32.T.astype(BF)
    gt[...] = gt_all.reshape(HEADS, HD, BN)
    qmt[...] = jnp.zeros_like(qmt)
    lane_head = lax.broadcasted_iota(jnp.int32, (BN, 128), 1) // HD
    for h in range(HEADS):
        r = h % GROUP
        lo = (h // GROUP) * 128
        qmt[h, r * HD:(r + 1) * HD, :] = qt[h * HD:(h + 1) * HD]
        qm[h] = jnp.where(lane_head == r, qs[:, lo:lo + 128], jnp.zeros((), BF))

    head_of = lax.broadcasted_iota(jnp.int32, (16, D), 1) // HD
    diag = head_of == lax.broadcasted_iota(jnp.int32, (16, D), 0)
    sv[...] = dot(jnp.where(diag, vk, jnp.zeros((), BF)), qt)[:HEADS].reshape(HEADS, 1, BN) + math.log2(BN)
    dpv[...] = dot(jnp.where(diag, vv, jnp.zeros((), BF)), gt_all)[:HEADS].reshape(HEADS, 1, BN)
    vk_cols[...] = jnp.broadcast_to(vk[:1].astype(F32), (128, D)).T.reshape(HEADS, HD, 128)
    vv_cols[...] = jnp.broadcast_to(vv[:1].astype(F32), (128, D)).T.reshape(HEADS, HD, 128)

    key_row = lax.broadcasted_iota(jnp.int32, (BN, BN), 0)
    query_col = lax.broadcasted_iota(jnp.int32, (BN, BN), 1)
    linked = mask_ref[...].astype(F32).T
    ok = ((linked != 0.0) | (key_row == query_col)) & (key_row < count_ref[0])
    bias[...] = jnp.where(ok, 0.0, NEG_FILL)

    row_no = lax.broadcasted_iota(jnp.int32, (BN, D), 0).astype(F32)
    lane_no = lax.broadcasted_iota(jnp.int32, (16, BN), 1).astype(F32)
    for c in range(CHUNKS):
        rows = slice(c * BN, (c + 1) * BN)
        xc = parts[c][:BN, :]
        k32 = dot(xc, wk)
        v32 = dot(xc, wv)
        k = k32.astype(BF)
        live_row = jnp.ones((16, BN), BF)
        if c:
            tail = parts[c][BN:, :].astype(F32)
            count = tail[0:1, 0:1] + 256.0 * tail[1:2, 0:1]
            live = row_no < count
            k = jnp.where(live, k, jnp.broadcast_to(vk[:1], (BN, D)))
            k32 = jnp.where(live, k32, 0.0)
            v32 = jnp.where(live, v32, 0.0)
            live_row = jnp.where(lane_no < count, 1.0, 0.0).astype(BF)
        v = v32.astype(BF)
        for gi in range(2):
            ks[gi, rows, :] = k[:, gi * 128:(gi + 1) * 128]
            vs[gi, rows, :] = v[:, gi * 128:(gi + 1) * 128]
        vt = v32.T.astype(BF)
        k0t[:, :, rows] = k32.T.astype(BF).reshape(HEADS, HD, BN)
        xt[c] = xc.astype(F32).T.astype(BF)
        for h in range(HEADS):
            vta[h, :HD, rows] = vt[h * HD:(h + 1) * HD]
            vta[h, HD:, rows] = live_row

    dk_acc[...] = jnp.zeros_like(dk_acc)
    dv_acc[...] = jnp.zeros_like(dv_acc)
    row_head = lax.broadcasted_iota(jnp.int32, (128, BN), 0) // HD
    s_bufs, p_bufs = (s_even, s_odd), (p_even, p_odd)
    gmt_bufs, gm_bufs = (gmt_even, gmt_odd), (gm_even, gm_odd)

    def step(first, second, third, parity):
        peak = jnp.full((8, BN), -jnp.inf, F32)
        out = jnp.zeros((HD + 16, BN), F32)
        if second is not None:
            top2 = tops[second]
        if third is not None:
            delta3 = deltas[third]
            gi3 = third // GROUP
            dq = vk_cols[third][:, :1] * dsv[third]
        for t in range(KEYS // TILE):
            rows = pl.ds(t * TILE, TILE)
            if first is not None:
                s = dot(ks[first // GROUP, rows, :], qmt[first])
                if (t + 1) * TILE <= BN:
                    s = s + bias[rows, :]
                s_bufs[parity][rows, :] = s
                peak = jnp.maximum(peak, jnp.max(s.reshape(TILE // 8, 8, BN), axis=0))
            if third is not None:
                p3 = p_bufs[parity][rows, :]
                ds = (dot(vs[gi3, rows, :], gmt_bufs[parity][...]) - delta3).astype(BF) * p3
            if second is not None:
                p = jnp.exp2(s_bufs[1 - parity][rows, :] - top2).astype(BF)
                p_bufs[1 - parity][rows, :] = p
                out = out + dot(vta[second, :, rows], p)
            if third is not None:
                dv_acc[gi3, rows, :] += dot(p3, gm_bufs[parity][...])
                dk_acc[gi3, rows, :] += dot(ds, qm[third])
                dq = dq + dot(k0t[third, :, rows], ds)
        if first is not None:
            tops[first] = jnp.maximum(sv[first], jnp.max(peak, axis=0, keepdims=True))
        if second is not None:
            pv = jnp.exp2(sv[second] - top2)
            inv = 1.0 / (out[HD:HD + 1] + pv)
            attn_h = ((out[:HD] + vv_cols[second][:, :1] * pv) * inv).astype(BF)
            attn_t[second] = attn_h
            g_h = gt[second].astype(F32)
            delta = jnp.sum(g_h * attn_h.astype(F32), axis=0, keepdims=True) * inv
            deltas[second] = delta
            g_n = g_h * inv
            gmt32 = jnp.where(
                row_head == second % GROUP, jnp.concatenate([g_n] * GROUP, axis=0), 0.0
            )
            gmt_bufs[1 - parity][...] = gmt32.astype(BF)
            gm_bufs[1 - parity][...] = gmt32.T.astype(BF)
            dsv[second] = pv * (dpv[second] * inv - delta)
            pvn[second] = pv * inv
        if third is not None:
            dq_t[third] = (dq * SCALE).astype(BF)

    step(0, None, None, 0)
    step(1, 0, None, 1)

    @pl.loop(1, HEADS // 2)
    def _(pair):
        h = 2 * pair
        step(h, h - 1, h - 2, 0)
        step(h + 1, h, h - 1, 1)

    step(None, HEADS - 1, HEADS - 2, 0)
    step(None, None, HEADS - 1, 1)

    at = attn_t[...].reshape(D, BN)
    attn = at.astype(F32).T.astype(BF)
    layer_ref[...] = (x.astype(F32) + dot(attn, wo)).astype(BF)
    dqt = dq_t[...].reshape(D, BN)
    dqm = dqt.astype(F32).T.astype(BF)

    grad_query = dot(xt[0], dqm)
    grad_output = dot(at, cot)
    keep = diag[:HEADS]
    dsv_all = dsv[...].reshape(HEADS, BN)
    pvn_all = pvn[...].reshape(HEADS, BN)
    vkey = jnp.sum(jnp.where(keep, dot(dsv_all.astype(BF), qs), 0.0), axis=0, keepdims=True) * LN2
    vvalue = jnp.sum(jnp.where(keep, dot(pvn_all.astype(BF), g), 0.0), axis=0, keepdims=True)
    vn_col = jnp.broadcast_to(vn_ref[...].astype(F32), (128, D)).T[:, :1]
    grad_key = vn_col * vkey
    grad_value = vn_col * vvalue
    backs = (None, b0_ref, b1_ref, b2_ref, b3_ref)
    for c in range(CHUNKS):
        rows = slice(c * BN, (c + 1) * BN)
        dk = jnp.concatenate([dk_acc[0, rows, :], dk_acc[1, rows, :]], axis=1) * LN2
        dv = jnp.concatenate([dv_acc[0, rows, :], dv_acc[1, rows, :]], axis=1)
        if c:
            tail = parts[c][BN:, :].astype(F32)
            live = row_no < tail[0:1, 0:1] + 256.0 * tail[1:2, 0:1]
            dk = jnp.where(live, dk, 0.0)
            dv = jnp.where(live, dv, 0.0)
        dk = dk.astype(BF)
        dv = dv.astype(BF)
        grad_key = grad_key + dot(xt[c], dk)
        grad_value = grad_value + dot(xt[c], dv)
        back = dot_nt(dk, wk) + dot_nt(dv, wv)
        if c:
            backs[c][...] = back.astype(BF)
        else:
            own_ref[...] = back + dot_nt(dqm, wq) + cot.astype(F32)
    for n, grad in enumerate((grad_query, grad_key, grad_value, grad_output)):
        for j in range(2):
            weight_ref[(j + core_ref[0]) % 2, n * 32:(n + 1) * 32] = (
                grad[:, j * 128:(j + 1) * 128].reshape(32, 8, 128)
            )
    virt = dot_nt_exact(jnp.broadcast_to(vkey, (8, D)), wk) + dot_nt_exact(
        jnp.broadcast_to(vvalue, (8, D)), wv
    )
    high = virt.astype(BF).astype(F32)
    virt_ref[0:8] = high
    virt_ref[8:16] = virt - high


def attend(count, core, x, partners, wq, wk, wv, wo, vn, cot, mask):
    vmem = pl.BlockSpec(memory_space=pltpu.VMEM)
    sds = jax.ShapeDtypeStruct
    return pl.pallas_call(
        attend_kernel,
        out_shape=(
            sds((BN, D), BF), sds((BN, D), F32), sds((BN, D), BF), sds((BN, D), BF),
            sds((BN, D), BF), sds((BN, D), BF), sds((2, 128, 8, 128), F32), sds((16, D), F32),
        ),
        in_specs=[pl.BlockSpec(memory_space=pltpu.SMEM)] * 2 + [vmem] * 12,
        out_specs=[vmem] * 8,
        scratch_shapes=[
            pltpu.VMEM((HEADS, 128, BN), BF),
            pltpu.VMEM((HEADS, BN, 128), BF),
            pltpu.VMEM((HEADS, HD, BN), BF),
            pltpu.VMEM((2, KEYS, 128), BF),
            pltpu.VMEM((2, KEYS, 128), BF),
            pltpu.VMEM((HEADS, HD + 16, KEYS), BF),
            pltpu.VMEM((HEADS, HD, KEYS), BF),
            pltpu.VMEM((CHUNKS, D, BN), BF),
            pltpu.VMEM((BN, BN), F32),
            pltpu.VMEM((KEYS, BN), F32),
            pltpu.VMEM((KEYS, BN), F32),
            pltpu.VMEM((KEYS, BN), BF),
            pltpu.VMEM((KEYS, BN), BF),
            pltpu.VMEM((128, BN), BF),
            pltpu.VMEM((128, BN), BF),
            pltpu.VMEM((BN, 128), BF),
            pltpu.VMEM((BN, 128), BF),
            pltpu.VMEM((2, KEYS, 128), F32),
            pltpu.VMEM((2, KEYS, 128), F32),
            pltpu.VMEM((HEADS, HD, BN), BF),
            pltpu.VMEM((HEADS, HD, BN), BF),
            pltpu.VMEM((HEADS, 1, BN), F32),
            pltpu.VMEM((HEADS, 1, BN), F32),
            pltpu.VMEM((HEADS, 1, BN), F32),
            pltpu.VMEM((HEADS, 1, BN), F32),
            pltpu.VMEM((HEADS, 1, BN), F32),
            pltpu.VMEM((HEADS, 1, BN), F32),
            pltpu.VMEM((HEADS, HD, 128), F32),
            pltpu.VMEM((HEADS, HD, 128), F32),
        ],
        compiler_params=pltpu.CompilerParams(vmem_limit_bytes=56 * 1024 * 1024),
        cost_estimate=pl.CostEstimate(flops=8 * 10**9, bytes_accessed=4 * 10**6, transcendentals=10**7),
        name="attend",
    )(count, core, x, *partners, wq, wk, wv, wo, vn, cot, mask)


def exchange(array, distance):
    return lax.ppermute(array, "blk", [(i, i ^ distance) for i in range(lax.axis_size("blk"))])


def exchange_by(array, distance):
    size = lax.axis_size("blk")
    branches = [functools.partial(exchange, distance=d) for d in range(2, size - 1)]
    return lax.switch(distance - 2, branches, array)


def body(
    features, w_query, key_weight, value_weight, w_output, virtual_node, cotangent, local_mask,
    counts, shifts,
):
    largest = lax.axis_size("blk") - 1
    low = jnp.min(jnp.where(shifts == 1, largest + 1, shifts))
    high = jnp.max(jnp.where(shifts == largest, 0, shifts))
    own = counts[0]
    halves = jnp.stack([own & 255, own >> 8]).astype(BF)
    tail = jnp.zeros((SENT - BN, D), BF).at[:2].set(jnp.broadcast_to(halves[:, None], (2, D)))
    sent = jnp.concatenate([features, tail], axis=0)
    partners = [exchange(sent, largest), exchange(sent, 1), exchange_by(sent, low), exchange_by(sent, high)]
    layer_out, own_grad, back_far, back_near, back_low, back_high, weights, virt = attend(
        counts, (lax.axis_index("sub") % 2)[None].astype(jnp.int32), features, partners, w_query, key_weight, value_weight, w_output,
        virtual_node[None, :], cotangent, local_mask,
    )
    everyone = ("blk", "sub")
    count_sub = lax.axis_size("sub")
    devices = lax.axis_size("blk") * count_sub
    same_core = [[i for i in range(devices) if i % 2 == core] for core in range(2)]
    siblings = [(i, i ^ 1) for i in range(count_sub)]
    far, near = exchange(back_far, largest), exchange(back_near, 1)

    mine, other = weights[0], weights[1]
    virt_rows = jnp.concatenate(
        [virt[0:1].reshape(2, 128), virt[8:9].reshape(2, 128), jnp.zeros((4, 128), F32)]
    )[None]
    fresh = lax.ppermute(
        jnp.concatenate([other, virt_rows]).astype(BF), "sub", siblings
    ).astype(F32)
    half = (mine + fresh[:-1]).astype(BF)
    virt_pair = virt_rows[0, :2] + virt_rows[0, 2:4] + fresh[-1, :2] + fresh[-1, 2:4]
    scattered = lax.all_to_all(half, everyone, 0, 0, axis_index_groups=same_core)
    low_part = exchange_by(back_low, low)
    scattered, low_part, far, near = lax.optimization_barrier((scattered, low_part, far, near))
    chunk = jnp.sum(scattered.astype(F32), axis=0)
    back_high, chunk = lax.optimization_barrier((back_high, chunk))
    virt_high = lax.reduce_precision(virt_pair, 8, 7)
    packed = jnp.concatenate(
        [chunk, virt_high, virt_pair - virt_high, jnp.zeros((4, 128), F32)]
    ).astype(BF)
    summed = lax.all_to_all(
        jnp.broadcast_to(packed, (devices // 2, 16, 128)), everyone, 0, 0,
        axis_index_groups=same_core,
    )
    high_part = exchange_by(back_high, high)
    kept = summed[:, :8]
    given = lax.ppermute(kept, "sub", siblings)
    core = lax.axis_index("sub") % 2
    halves = jnp.stack([jnp.where(core == 0, kept, given), jnp.where(core == 0, given, kept)], axis=1)
    grads = halves.astype(F32).transpose(0, 2, 1, 3).reshape(4, D, D)
    grad_virtual = jnp.sum(summed[:, 8:12].astype(F32), axis=0)
    grad_virtual = (grad_virtual[:2] + grad_virtual[2:]).reshape(D)
    returned = (far, near, low_part, high_part)
    total = own_grad
    for part in returned:
        total = total + part.astype(F32)
    return (
        layer_out, total.astype(BF), grads[0], grads[1], grads[2], grads[3], grad_virtual,
    )


def solution(mesh):
    return jax.shard_map(
        body,
        mesh=mesh,
        in_specs=(
            P(("blk", "sub"), None), P(), P(), P(), P(), P(), P(("blk", "sub"), None),
            P(("blk", "sub"), None), P(("blk", "sub")), P(),
        ),
        out_specs=(P(("blk", "sub"), None), P(("blk", "sub"), None), P(), P(), P(), P(), P()),
        check_vma=False,
    )
```

```python
import functools
import math

import jax
import jax.numpy as jnp
from jax import lax
from jax.experimental import pallas as pl
from jax.experimental.pallas import tpu as pltpu
from jax.sharding import PartitionSpec as P

D = 256
HEADS = 8
HD = D // HEADS
GROUP = 128 // HD
CHUNKS = 5
BN = 512
KEYS = CHUNKS * BN
SENT = BN + 16
NEG_FILL = -1000000000.0
SCALE = 1.0 / math.sqrt(HD)
LOG2E = 1.0 / math.log(2.0)
LN2 = math.log(2.0)
TILE = 512
DISTANT = 4
BF = jnp.bfloat16
F32 = jnp.float32


def dot(a, b):
    return jnp.dot(a, b, preferred_element_type=F32)


def dot_nt(a, b):
    return lax.dot_general(a, b, (((1,), (1,)), ((), ())), preferred_element_type=F32)


def dot_nt_exact(a, b):
    return lax.dot_general(
        a, b.astype(F32), (((1,), (1,)), ((), ())), precision=lax.Precision.HIGHEST,
        preferred_element_type=F32,
    )


def attend_kernel(
    count_ref, core_ref, x_ref, p0_ref, p1_ref, p2_ref, p3_ref, wq_ref, wk_ref, wv_ref, wo_ref, vn_ref,
    cot_ref, mask_ref,
    layer_ref, own_ref, b0_ref, b1_ref, b2_ref, b3_ref, weight_ref, virt_ref,
    qmt, qm, gt, ks, vs, vta, k0t, xt, bias, s_even, s_odd, p_even, p_odd, gmt_even, gmt_odd,
    gm_even, gm_odd, dk_acc, dv_acc, attn_t, dq_t, sv, dpv, dsv, pvn, tops, deltas, vk_cols, vv_cols,
):
    parts = (x_ref, p0_ref, p1_ref, p2_ref, p3_ref)
    x = x_ref[...]
    wq, wk, wv, wo = wq_ref[...], wk_ref[...], wv_ref[...], wo_ref[...]
    vn = jnp.broadcast_to(vn_ref[...], (16, D))
    vk = dot(vn, wk).astype(BF)
    vv = dot(vn, wv).astype(BF)

    q32 = dot(x, wq) * (SCALE * LOG2E)
    qs = q32.astype(BF)
    qt = q32.T.astype(BF)
    cot = cot_ref[...]
    g32 = dot_nt(cot, wo)
    g = g32.astype(BF)
    gt_all = g32.T.astype(BF)
    gt[...] = gt_all.reshape(HEADS, HD, BN)
    qmt[...] = jnp.zeros_like(qmt)
    lane_head = lax.broadcasted_iota(jnp.int32, (BN, 128), 1) // HD
    for h in range(HEADS):
        r = h % GROUP
        lo = (h // GROUP) * 128
        qmt[h, r * HD:(r + 1) * HD, :] = qt[h * HD:(h + 1) * HD]
        qm[h] = jnp.where(lane_head == r, qs[:, lo:lo + 128], jnp.zeros((), BF))

    head_of = lax.broadcasted_iota(jnp.int32, (16, D), 1) // HD
    diag = head_of == lax.broadcasted_iota(jnp.int32, (16, D), 0)
    sv[...] = dot(jnp.where(diag, vk, jnp.zeros((), BF)), qt)[:HEADS].reshape(HEADS, 1, BN) + math.log2(BN)
    dpv[...] = dot(jnp.where(diag, vv, jnp.zeros((), BF)), gt_all)[:HEADS].reshape(HEADS, 1, BN)
    vk_cols[...] = jnp.broadcast_to(vk[:1].astype(F32), (128, D)).T.reshape(HEADS, HD, 128)
    vv_cols[...] = jnp.broadcast_to(vv[:1].astype(F32), (128, D)).T.reshape(HEADS, HD, 128)

    key_row = lax.broadcasted_iota(jnp.int32, (BN, BN), 0)
    query_col = lax.broadcasted_iota(jnp.int32, (BN, BN), 1)
    linked = mask_ref[...].astype(F32).T
    ok = ((linked != 0.0) | (key_row == query_col)) & (key_row < count_ref[0])
    bias[...] = jnp.where(ok, 0.0, NEG_FILL)

    row_no = lax.broadcasted_iota(jnp.int32, (BN, D), 0).astype(F32)
    lane_no = lax.broadcasted_iota(jnp.int32, (16, BN), 1).astype(F32)
    for c in range(CHUNKS):
        rows = slice(c * BN, (c + 1) * BN)
        xc = parts[c][:BN, :]
        k32 = dot(xc, wk)
        v32 = dot(xc, wv)
        k = k32.astype(BF)
        live_row = jnp.ones((16, BN), BF)
        if c:
            tail = parts[c][BN:, :].astype(F32)
            count = tail[0:1, 0:1] + 256.0 * tail[1:2, 0:1]
            live = row_no < count
            k = jnp.where(live, k, jnp.broadcast_to(vk[:1], (BN, D)))
            k32 = jnp.where(live, k32, 0.0)
            v32 = jnp.where(live, v32, 0.0)
            live_row = jnp.where(lane_no < count, 1.0, 0.0).astype(BF)
        v = v32.astype(BF)
        for gi in range(2):
            ks[gi, rows, :] = k[:, gi * 128:(gi + 1) * 128]
            vs[gi, rows, :] = v[:, gi * 128:(gi + 1) * 128]
        vt = v32.T.astype(BF)
        k0t[:, :, rows] = k32.T.astype(BF).reshape(HEADS, HD, BN)
        xt[c] = xc.astype(F32).T.astype(BF)
        for h in range(HEADS):
            vta[h, :HD, rows] = vt[h * HD:(h + 1) * HD]
            vta[h, HD:, rows] = live_row

    dk_acc[...] = jnp.zeros_like(dk_acc)
    dv_acc[...] = jnp.zeros_like(dv_acc)
    row_head = lax.broadcasted_iota(jnp.int32, (128, BN), 0) // HD
    s_bufs, p_bufs = (s_even, s_odd), (p_even, p_odd)
    gmt_bufs, gm_bufs = (gmt_even, gmt_odd), (gm_even, gm_odd)

    def step(first, second, third, parity):
        peak = jnp.full((8, BN), -jnp.inf, F32)
        out = jnp.zeros((HD + 16, BN), F32)
        if second is not None:
            top2 = tops[second]
        if third is not None:
            delta3 = deltas[third]
            gi3 = third // GROUP
            dq = vk_cols[third][:, :1] * dsv[third]
        for t in range(KEYS // TILE):
            rows = pl.ds(t * TILE, TILE)
            if first is not None:
                s = dot(ks[first // GROUP, rows, :], qmt[first])
                if (t + 1) * TILE <= BN:
                    s = s + bias[rows, :]
                s_bufs[parity][rows, :] = s
                peak = jnp.maximum(peak, jnp.max(s.reshape(TILE // 8, 8, BN), axis=0))
            if third is not None:
                p3 = p_bufs[parity][rows, :]
                ds = (dot(vs[gi3, rows, :], gmt_bufs[parity][...]) - delta3).astype(BF) * p3
            if second is not None:
                p = jnp.exp2(s_bufs[1 - parity][rows, :] - top2).astype(BF)
                p_bufs[1 - parity][rows, :] = p
                out = out + dot(vta[second, :, rows], p)
            if third is not None:
                dv_acc[gi3, rows, :] += dot(p3, gm_bufs[parity][...])
                dk_acc[gi3, rows, :] += dot(ds, qm[third])
                dq = dq + dot(k0t[third, :, rows], ds)
        if first is not None:
            tops[first] = jnp.maximum(sv[first], jnp.max(peak, axis=0, keepdims=True))
        if second is not None:
            pv = jnp.exp2(sv[second] - top2)
            inv = 1.0 / (out[HD:HD + 1] + pv)
            attn_h = ((out[:HD] + vv_cols[second][:, :1] * pv) * inv).astype(BF)
            attn_t[second] = attn_h
            g_h = gt[second].astype(F32)
            delta = jnp.sum(g_h * attn_h.astype(F32), axis=0, keepdims=True) * inv
            deltas[second] = delta
            g_n = g_h * inv
            gmt32 = jnp.where(
                row_head == second % GROUP, jnp.concatenate([g_n] * GROUP, axis=0), 0.0
            )
            gmt_bufs[1 - parity][...] = gmt32.astype(BF)
            gm_bufs[1 - parity][...] = gmt32.T.astype(BF)
            dsv[second] = pv * (dpv[second] * inv - delta)
            pvn[second] = pv * inv
        if third is not None:
            dq_t[third] = (dq * SCALE).astype(BF)

    step(0, None, None, 0)
    step(1, 0, None, 1)

    @pl.loop(1, HEADS // 2)
    def _(pair):
        h = 2 * pair
        step(h, h - 1, h - 2, 0)
        step(h + 1, h, h - 1, 1)

    step(None, HEADS - 1, HEADS - 2, 0)
    step(None, None, HEADS - 1, 1)

    at = attn_t[...].reshape(D, BN)
    attn = at.astype(F32).T.astype(BF)
    layer_ref[...] = (x.astype(F32) + dot(attn, wo)).astype(BF)
    dqt = dq_t[...].reshape(D, BN)
    dqm = dqt.astype(F32).T.astype(BF)

    grad_query = dot(xt[0], dqm)
    grad_output = dot(at, cot)
    keep = diag[:HEADS]
    dsv_all = dsv[...].reshape(HEADS, BN)
    pvn_all = pvn[...].reshape(HEADS, BN)
    vkey = jnp.sum(jnp.where(keep, dot(dsv_all.astype(BF), qs), 0.0), axis=0, keepdims=True) * LN2
    vvalue = jnp.sum(jnp.where(keep, dot(pvn_all.astype(BF), g), 0.0), axis=0, keepdims=True)
    vn_col = jnp.broadcast_to(vn_ref[...].astype(F32), (128, D)).T[:, :1]
    grad_key = vn_col * vkey
    grad_value = vn_col * vvalue
    backs = (None, b0_ref, b1_ref, b2_ref, b3_ref)
    for c in range(CHUNKS):
        rows = slice(c * BN, (c + 1) * BN)
        dk = jnp.concatenate([dk_acc[0, rows, :], dk_acc[1, rows, :]], axis=1) * LN2
        dv = jnp.concatenate([dv_acc[0, rows, :], dv_acc[1, rows, :]], axis=1)
        if c:
            tail = parts[c][BN:, :].astype(F32)
            live = row_no < tail[0:1, 0:1] + 256.0 * tail[1:2, 0:1]
            dk = jnp.where(live, dk, 0.0)
            dv = jnp.where(live, dv, 0.0)
        dk = dk.astype(BF)
        dv = dv.astype(BF)
        grad_key = grad_key + dot(xt[c], dk)
        grad_value = grad_value + dot(xt[c], dv)
        back = dot_nt(dk, wk) + dot_nt(dv, wv)
        if c:
            backs[c][...] = back.astype(BF)
        else:
            own_ref[...] = back + dot_nt(dqm, wq) + cot.astype(F32)
    for n, grad in enumerate((grad_query, grad_key, grad_value, grad_output)):
        for j in range(2):
            weight_ref[(j + core_ref[0]) % 2, n * 32:(n + 1) * 32] = (
                grad[:, j * 128:(j + 1) * 128].reshape(32, 8, 128)
            )
    virt = dot_nt_exact(jnp.broadcast_to(vkey, (8, D)), wk) + dot_nt_exact(
        jnp.broadcast_to(vvalue, (8, D)), wv
    )
    high = virt.astype(BF).astype(F32)
    virt_ref[0:8] = high
    virt_ref[8:16] = virt - high


def attend(count, core, x, partners, wq, wk, wv, wo, vn, cot, mask):
    vmem = pl.BlockSpec(memory_space=pltpu.VMEM)
    sds = jax.ShapeDtypeStruct
    return pl.pallas_call(
        attend_kernel,
        out_shape=(
            sds((BN, D), BF), sds((BN, D), F32), sds((BN, D), BF), sds((BN, D), BF),
            sds((BN, D), BF), sds((BN, D), BF), sds((2, 128, 8, 128), F32), sds((16, D), F32),
        ),
        in_specs=[pl.BlockSpec(memory_space=pltpu.SMEM)] * 2 + [vmem] * 12,
        out_specs=[vmem] * 8,
        scratch_shapes=[
            pltpu.VMEM((HEADS, 128, BN), BF),
            pltpu.VMEM((HEADS, BN, 128), BF),
            pltpu.VMEM((HEADS, HD, BN), BF),
            pltpu.VMEM((2, KEYS, 128), BF),
            pltpu.VMEM((2, KEYS, 128), BF),
            pltpu.VMEM((HEADS, HD + 16, KEYS), BF),
            pltpu.VMEM((HEADS, HD, KEYS), BF),
            pltpu.VMEM((CHUNKS, D, BN), BF),
            pltpu.VMEM((BN, BN), F32),
            pltpu.VMEM((KEYS, BN), F32),
            pltpu.VMEM((KEYS, BN), F32),
            pltpu.VMEM((KEYS, BN), BF),
            pltpu.VMEM((KEYS, BN), BF),
            pltpu.VMEM((128, BN), BF),
            pltpu.VMEM((128, BN), BF),
            pltpu.VMEM((BN, 128), BF),
            pltpu.VMEM((BN, 128), BF),
            pltpu.VMEM((2, KEYS, 128), F32),
            pltpu.VMEM((2, KEYS, 128), F32),
            pltpu.VMEM((HEADS, HD, BN), BF),
            pltpu.VMEM((HEADS, HD, BN), BF),
            pltpu.VMEM((HEADS, 1, BN), F32),
            pltpu.VMEM((HEADS, 1, BN), F32),
            pltpu.VMEM((HEADS, 1, BN), F32),
            pltpu.VMEM((HEADS, 1, BN), F32),
            pltpu.VMEM((HEADS, 1, BN), F32),
            pltpu.VMEM((HEADS, 1, BN), F32),
            pltpu.VMEM((HEADS, HD, 128), F32),
            pltpu.VMEM((HEADS, HD, 128), F32),
        ],
        compiler_params=pltpu.CompilerParams(vmem_limit_bytes=56 * 1024 * 1024),
        cost_estimate=pl.CostEstimate(flops=8 * 10**9, bytes_accessed=4 * 10**6, transcendentals=10**7),
        name="attend",
    )(count, core, x, *partners, wq, wk, wv, wo, vn, cot, mask)


def exchange(array, distance):
    return lax.ppermute(array, "blk", [(i, i ^ distance) for i in range(lax.axis_size("blk"))])


def exchange_by(array, step):
    near_bits = DISTANT - 1
    steps = [d for d in range(1, lax.axis_size("blk")) if not d & DISTANT]
    branches = [functools.partial(exchange, distance=d) for d in steps]
    place = (step // (2 * DISTANT)) * DISTANT + (step & near_bits)
    return lax.switch(place - 1, branches, array)


def body(
    features, w_query, key_weight, value_weight, w_output, virtual_node, cotangent, local_mask,
    counts, shifts,
):
    largest = lax.axis_size("blk") - 1
    low = jnp.min(jnp.where(shifts == 1, largest + 1, shifts))
    high = jnp.max(jnp.where(shifts == largest, 0, shifts))
    own = counts[0]
    halves = jnp.stack([own & 255, own >> 8]).astype(BF)
    tail = jnp.zeros((SENT - BN, D), BF).at[:2].set(jnp.broadcast_to(halves[:, None], (2, D)))
    sent = jnp.concatenate([features, tail], axis=0)
    far_copy, near_copy = exchange(sent, largest), exchange(sent, 1)
    low_far, high_far = low & DISTANT != 0, high & DISTANT != 0
    low_step = jnp.where(low_far, low ^ largest, low)
    high_step = jnp.where(high_far, high ^ largest, high)
    partners = [
        far_copy, near_copy,
        exchange_by(jnp.where(low_far, far_copy, sent), low_step),
        exchange_by(jnp.where(high_far, far_copy, sent), high_step),
    ]
    layer_out, own_grad, back_far, back_near, back_low, back_high, weights, virt = attend(
        counts, (lax.axis_index("sub") % 2)[None].astype(jnp.int32), features, partners, w_query, key_weight, value_weight, w_output,
        virtual_node[None, :], cotangent, local_mask,
    )
    everyone = ("blk", "sub")
    count_sub = lax.axis_size("sub")
    devices = lax.axis_size("blk") * count_sub
    same_core = [[i for i in range(devices) if i % 2 == core] for core in range(2)]
    siblings = [(i, i ^ 1) for i in range(count_sub)]
    near = exchange(back_near, 1)

    mine, other = weights[0], weights[1]
    virt_rows = jnp.concatenate(
        [virt[0:1].reshape(2, 128), virt[8:9].reshape(2, 128), jnp.zeros((4, 128), F32)]
    )[None]
    fresh = lax.ppermute(
        jnp.concatenate([other, virt_rows]).astype(BF), "sub", siblings
    ).astype(F32)
    half = (mine + fresh[:-1]).astype(BF)
    virt_pair = virt_rows[0, :2] + virt_rows[0, 2:4] + fresh[-1, :2] + fresh[-1, 2:4]
    scattered = lax.all_to_all(half, everyone, 0, 0, axis_index_groups=same_core)
    back_low, back_high, half = lax.optimization_barrier((back_low, back_high, half))
    low_part = exchange_by(back_low, low_step)
    high_part = exchange_by(back_high, high_step)
    scattered, low_part, high_part, near = lax.optimization_barrier(
        (scattered, low_part, high_part, near)
    )
    low_part, high_part = low_part.astype(F32), high_part.astype(F32)
    onward = back_far.astype(F32) + jnp.where(low_far, low_part, 0.0) + jnp.where(high_far, high_part, 0.0)
    far = exchange(onward.astype(BF), largest)
    chunk = jnp.sum(scattered.astype(F32), axis=0)
    virt_high = lax.reduce_precision(virt_pair, 8, 7)
    packed = jnp.concatenate(
        [chunk, virt_high, virt_pair - virt_high, jnp.zeros((4, 128), F32)]
    ).astype(BF)
    summed = lax.all_to_all(
        jnp.broadcast_to(packed, (devices // 2, 16, 128)), everyone, 0, 0,
        axis_index_groups=same_core,
    )
    summed, far = lax.optimization_barrier((summed, far))
    kept = summed[:, :8]
    given = lax.ppermute(kept, "sub", siblings)
    core = lax.axis_index("sub") % 2
    halves = jnp.stack([jnp.where(core == 0, kept, given), jnp.where(core == 0, given, kept)], axis=1)
    grads = halves.astype(F32).transpose(0, 2, 1, 3).reshape(4, D, D)
    grad_virtual = jnp.sum(summed[:, 8:12].astype(F32), axis=0)
    grad_virtual = (grad_virtual[:2] + grad_virtual[2:]).reshape(D)
    total = own_grad + near.astype(F32)
    total = total + jnp.where(low_far, 0.0, low_part) + jnp.where(high_far, 0.0, high_part)
    total = total + far.astype(F32)
    return (
        layer_out, total.astype(BF), grads[0], grads[1], grads[2], grads[3], grad_virtual,
    )


def solution(mesh):
    return jax.shard_map(
        body,
        mesh=mesh,
        in_specs=(
            P(("blk", "sub"), None), P(), P(), P(), P(), P(), P(("blk", "sub"), None),
            P(("blk", "sub"), None), P(("blk", "sub")), P(),
        ),
        out_specs=(P(("blk", "sub"), None), P(("blk", "sub"), None), P(), P(), P(), P(), P()),
        check_vma=False,
    )
```

```python
import functools
import math

import jax
import jax.numpy as jnp
from jax import lax
from jax.experimental import pallas as pl
from jax.experimental.pallas import tpu as pltpu
from jax.sharding import PartitionSpec as P

D = 256
HEADS = 8
HD = D // HEADS
GROUP = 128 // HD
CHUNKS = 5
BN = 512
KEYS = CHUNKS * BN
SENT = BN + 16
NEG_FILL = -1000000000.0
SCALE = 1.0 / math.sqrt(HD)
LOG2E = 1.0 / math.log(2.0)
LN2 = math.log(2.0)
TILE = 512
DISTANT = 4
BF = jnp.bfloat16
F32 = jnp.float32


def dot(a, b):
    return jnp.dot(a, b, preferred_element_type=F32)


def dot_nt(a, b):
    return lax.dot_general(a, b, (((1,), (1,)), ((), ())), preferred_element_type=F32)


def dot_nt_exact(a, b):
    return lax.dot_general(
        a, b.astype(F32), (((1,), (1,)), ((), ())), precision=lax.Precision.HIGHEST,
        preferred_element_type=F32,
    )


def attend_kernel(
    count_ref, x_ref, p0_ref, p1_ref, p2_ref, p3_ref, wq_ref, wk_ref, wv_ref, wo_ref, vn_ref,
    cot_ref, mask_ref,
    layer_ref, own_ref, b0_ref, b1_ref, b2_ref, b3_ref, weight_ref, virt_ref,
    qmt, qm, gt, ks, vs, vta, k0t, xt, bias, s_even, s_odd, p_even, p_odd, gmt_even, gmt_odd,
    gm_even, gm_odd, dk_acc, dv_acc, attn_t, dq_t, sv, dpv, dsv, pvn, tops, deltas, vk_cols, vv_cols,
):
    parts = (x_ref, p0_ref, p1_ref, p2_ref, p3_ref)
    x = x_ref[...]
    wq, wk, wv, wo = wq_ref[...], wk_ref[...], wv_ref[...], wo_ref[...]
    vn = jnp.broadcast_to(vn_ref[...], (16, D))
    vk = dot(vn, wk).astype(BF)
    vv = dot(vn, wv).astype(BF)

    q32 = dot(x, wq) * (SCALE * LOG2E)
    qs = q32.astype(BF)
    qt = q32.T.astype(BF)
    cot = cot_ref[...]
    g32 = dot_nt(cot, wo)
    g = g32.astype(BF)
    gt_all = g32.T.astype(BF)
    gt[...] = gt_all.reshape(HEADS, HD, BN)
    qmt[...] = jnp.zeros_like(qmt)
    lane_head = lax.broadcasted_iota(jnp.int32, (BN, 128), 1) // HD
    for h in range(HEADS):
        r = h % GROUP
        lo = (h // GROUP) * 128
        qmt[h, r * HD:(r + 1) * HD, :] = qt[h * HD:(h + 1) * HD]
        qm[h] = jnp.where(lane_head == r, qs[:, lo:lo + 128], jnp.zeros((), BF))

    head_of = lax.broadcasted_iota(jnp.int32, (16, D), 1) // HD
    diag = head_of == lax.broadcasted_iota(jnp.int32, (16, D), 0)
    sv[...] = dot(jnp.where(diag, vk, jnp.zeros((), BF)), qt)[:HEADS].reshape(HEADS, 1, BN) + math.log2(BN)
    dpv[...] = dot(jnp.where(diag, vv, jnp.zeros((), BF)), gt_all)[:HEADS].reshape(HEADS, 1, BN)
    vk_cols[...] = jnp.broadcast_to(vk[:1].astype(F32), (128, D)).T.reshape(HEADS, HD, 128)
    vv_cols[...] = jnp.broadcast_to(vv[:1].astype(F32), (128, D)).T.reshape(HEADS, HD, 128)

    key_row = lax.broadcasted_iota(jnp.int32, (BN, BN), 0)
    query_col = lax.broadcasted_iota(jnp.int32, (BN, BN), 1)
    linked = mask_ref[...].astype(F32).T
    ok = ((linked != 0.0) | (key_row == query_col)) & (key_row < count_ref[0])
    bias[...] = jnp.where(ok, 0.0, NEG_FILL)

    row_no = lax.broadcasted_iota(jnp.int32, (BN, D), 0).astype(F32)
    lane_no = lax.broadcasted_iota(jnp.int32, (16, BN), 1).astype(F32)
    for c in range(CHUNKS):
        rows = slice(c * BN, (c + 1) * BN)
        xc = parts[c][:BN, :]
        k32 = dot(xc, wk)
        v32 = dot(xc, wv)
        k = k32.astype(BF)
        live_row = jnp.ones((16, BN), BF)
        if c:
            tail = parts[c][BN:, :].astype(F32)
            count = tail[0:1, 0:1] + 256.0 * tail[1:2, 0:1]
            live = row_no < count
            k = jnp.where(live, k, jnp.broadcast_to(vk[:1], (BN, D)))
            k32 = jnp.where(live, k32, 0.0)
            v32 = jnp.where(live, v32, 0.0)
            live_row = jnp.where(lane_no < count, 1.0, 0.0).astype(BF)
        v = v32.astype(BF)
        for gi in range(2):
            ks[gi, rows, :] = k[:, gi * 128:(gi + 1) * 128]
            vs[gi, rows, :] = v[:, gi * 128:(gi + 1) * 128]
        vt = v32.T.astype(BF)
        k0t[:, :, rows] = k32.T.astype(BF).reshape(HEADS, HD, BN)
        xt[c] = xc.astype(F32).T.astype(BF)
        for h in range(HEADS):
            vta[h, :HD, rows] = vt[h * HD:(h + 1) * HD]
            vta[h, HD:, rows] = live_row

    dk_acc[...] = jnp.zeros_like(dk_acc)
    dv_acc[...] = jnp.zeros_like(dv_acc)
    row_head = lax.broadcasted_iota(jnp.int32, (128, BN), 0) // HD
    s_bufs, p_bufs = (s_even, s_odd), (p_even, p_odd)
    gmt_bufs, gm_bufs = (gmt_even, gmt_odd), (gm_even, gm_odd)

    def step(first, second, third, parity):
        peak = jnp.full((8, BN), -jnp.inf, F32)
        out = jnp.zeros((HD + 16, BN), F32)
        if second is not None:
            top2 = tops[second]
        if third is not None:
            delta3 = deltas[third]
            gi3 = third // GROUP
            dq = vk_cols[third][:, :1] * dsv[third]
        for t in range(KEYS // TILE):
            rows = pl.ds(t * TILE, TILE)
            if first is not None:
                s = dot(ks[first // GROUP, rows, :], qmt[first])
                if (t + 1) * TILE <= BN:
                    s = s + bias[rows, :]
                s_bufs[parity][rows, :] = s
                peak = jnp.maximum(peak, jnp.max(s.reshape(TILE // 8, 8, BN), axis=0))
            if third is not None:
                p3 = p_bufs[parity][rows, :]
                ds = (dot(vs[gi3, rows, :], gmt_bufs[parity][...]) - delta3).astype(BF) * p3
            if second is not None:
                p = jnp.exp2(s_bufs[1 - parity][rows, :] - top2).astype(BF)
                p_bufs[1 - parity][rows, :] = p
                out = out + dot(vta[second, :, rows], p)
            if third is not None:
                dv_acc[gi3, rows, :] += dot(p3, gm_bufs[parity][...])
                dk_acc[gi3, rows, :] += dot(ds, qm[third])
                dq = dq + dot(k0t[third, :, rows], ds)
        if first is not None:
            tops[first] = jnp.maximum(sv[first], jnp.max(peak, axis=0, keepdims=True))
        if second is not None:
            pv = jnp.exp2(sv[second] - top2)
            inv = 1.0 / (out[HD:HD + 1] + pv)
            attn_h = ((out[:HD] + vv_cols[second][:, :1] * pv) * inv).astype(BF)
            attn_t[second] = attn_h
            g_h = gt[second].astype(F32)
            delta = jnp.sum(g_h * attn_h.astype(F32), axis=0, keepdims=True) * inv
            deltas[second] = delta
            g_n = g_h * inv
            gmt32 = jnp.where(
                row_head == second % GROUP, jnp.concatenate([g_n] * GROUP, axis=0), 0.0
            )
            gmt_bufs[1 - parity][...] = gmt32.astype(BF)
            gm_bufs[1 - parity][...] = gmt32.T.astype(BF)
            dsv[second] = pv * (dpv[second] * inv - delta)
            pvn[second] = pv * inv
        if third is not None:
            dq_t[third] = (dq * SCALE).astype(BF)

    step(0, None, None, 0)
    step(1, 0, None, 1)

    @pl.loop(1, HEADS // 2)
    def _(pair):
        h = 2 * pair
        step(h, h - 1, h - 2, 0)
        step(h + 1, h, h - 1, 1)

    step(None, HEADS - 1, HEADS - 2, 0)
    step(None, None, HEADS - 1, 1)

    at = attn_t[...].reshape(D, BN)
    attn = at.astype(F32).T.astype(BF)
    layer_ref[...] = (x.astype(F32) + dot(attn, wo)).astype(BF)
    dqt = dq_t[...].reshape(D, BN)
    dqm = dqt.astype(F32).T.astype(BF)

    grad_query = dot(xt[0], dqm)
    grad_output = dot(at, cot)
    keep = diag[:HEADS]
    dsv_all = dsv[...].reshape(HEADS, BN)
    pvn_all = pvn[...].reshape(HEADS, BN)
    vkey = jnp.sum(jnp.where(keep, dot(dsv_all.astype(BF), qs), 0.0), axis=0, keepdims=True) * LN2
    vvalue = jnp.sum(jnp.where(keep, dot(pvn_all.astype(BF), g), 0.0), axis=0, keepdims=True)
    vn_col = jnp.broadcast_to(vn_ref[...].astype(F32), (128, D)).T[:, :1]
    grad_key = vn_col * vkey
    grad_value = vn_col * vvalue
    backs = (None, b0_ref, b1_ref, b2_ref, b3_ref)
    for c in range(CHUNKS):
        rows = slice(c * BN, (c + 1) * BN)
        dk = jnp.concatenate([dk_acc[0, rows, :], dk_acc[1, rows, :]], axis=1) * LN2
        dv = jnp.concatenate([dv_acc[0, rows, :], dv_acc[1, rows, :]], axis=1)
        if c:
            tail = parts[c][BN:, :].astype(F32)
            live = row_no < tail[0:1, 0:1] + 256.0 * tail[1:2, 0:1]
            dk = jnp.where(live, dk, 0.0)
            dv = jnp.where(live, dv, 0.0)
        dk = dk.astype(BF)
        dv = dv.astype(BF)
        grad_key = grad_key + dot(xt[c], dk)
        grad_value = grad_value + dot(xt[c], dv)
        back = dot_nt(dk, wk) + dot_nt(dv, wv)
        if c:
            backs[c][...] = back.astype(BF)
        else:
            own_ref[...] = back + dot_nt(dqm, wq) + cot.astype(F32)
    for n, grad in enumerate((grad_query, grad_key, grad_value, grad_output)):
        for j in range(2):
            weight_ref[n * 32:(n + 1) * 32, j] = grad[:, j * 128:(j + 1) * 128].reshape(32, 8, 128).astype(BF)
    virt = dot_nt_exact(jnp.broadcast_to(vkey, (8, D)), wk) + dot_nt_exact(
        jnp.broadcast_to(vvalue, (8, D)), wv
    )
    high = virt.astype(BF).astype(F32)
    virt_ref[0:8] = high
    virt_ref[8:16] = virt - high


def attend(count, x, partners, wq, wk, wv, wo, vn, cot, mask):
    vmem = pl.BlockSpec(memory_space=pltpu.VMEM)
    sds = jax.ShapeDtypeStruct
    return pl.pallas_call(
        attend_kernel,
        out_shape=(
            sds((BN, D), BF), sds((BN, D), F32), sds((BN, D), BF), sds((BN, D), BF),
            sds((BN, D), BF), sds((BN, D), BF), sds((128, 2, 8, 128), BF), sds((16, D), F32),
        ),
        in_specs=[pl.BlockSpec(memory_space=pltpu.SMEM)] + [vmem] * 12,
        out_specs=[vmem] * 8,
        scratch_shapes=[
            pltpu.VMEM((HEADS, 128, BN), BF),
            pltpu.VMEM((HEADS, BN, 128), BF),
            pltpu.VMEM((HEADS, HD, BN), BF),
            pltpu.VMEM((2, KEYS, 128), BF),
            pltpu.VMEM((2, KEYS, 128), BF),
            pltpu.VMEM((HEADS, HD + 16, KEYS), BF),
            pltpu.VMEM((HEADS, HD, KEYS), BF),
            pltpu.VMEM((CHUNKS, D, BN), BF),
            pltpu.VMEM((BN, BN), F32),
            pltpu.VMEM((KEYS, BN), F32),
            pltpu.VMEM((KEYS, BN), F32),
            pltpu.VMEM((KEYS, BN), BF),
            pltpu.VMEM((KEYS, BN), BF),
            pltpu.VMEM((128, BN), BF),
            pltpu.VMEM((128, BN), BF),
            pltpu.VMEM((BN, 128), BF),
            pltpu.VMEM((BN, 128), BF),
            pltpu.VMEM((2, KEYS, 128), F32),
            pltpu.VMEM((2, KEYS, 128), F32),
            pltpu.VMEM((HEADS, HD, BN), BF),
            pltpu.VMEM((HEADS, HD, BN), BF),
            pltpu.VMEM((HEADS, 1, BN), F32),
            pltpu.VMEM((HEADS, 1, BN), F32),
            pltpu.VMEM((HEADS, 1, BN), F32),
            pltpu.VMEM((HEADS, 1, BN), F32),
            pltpu.VMEM((HEADS, 1, BN), F32),
            pltpu.VMEM((HEADS, 1, BN), F32),
            pltpu.VMEM((HEADS, HD, 128), F32),
            pltpu.VMEM((HEADS, HD, 128), F32),
        ],
        compiler_params=pltpu.CompilerParams(vmem_limit_bytes=56 * 1024 * 1024),
        cost_estimate=pl.CostEstimate(flops=8 * 10**9, bytes_accessed=4 * 10**6, transcendentals=10**7),
        name="attend",
    )(count, x, *partners, wq, wk, wv, wo, vn, cot, mask)


def finish_kernel(flags_ref, own_ref, near_ref, far_ref, low_ref, high_ref, out_ref):
    total = own_ref[...] + near_ref[...].astype(F32) + far_ref[...].astype(F32)
    total = total + jnp.where(flags_ref[0] != 0, 0.0, low_ref[...].astype(F32))
    total = total + jnp.where(flags_ref[1] != 0, 0.0, high_ref[...].astype(F32))
    out_ref[...] = total.astype(BF)


def finish(flags, own, near, far, low, high):
    vmem = pl.BlockSpec(memory_space=pltpu.VMEM)
    return pl.pallas_call(
        finish_kernel,
        out_shape=jax.ShapeDtypeStruct((BN, D), BF),
        in_specs=[pl.BlockSpec(memory_space=pltpu.SMEM)] + [vmem] * 5,
        out_specs=vmem,
        cost_estimate=pl.CostEstimate(flops=10**8, bytes_accessed=10**8, transcendentals=0),
        name="finish",
    )(flags, own, near, far, low, high)


def exchange(array, distance):
    return lax.ppermute(array, "blk", [(i, i ^ distance) for i in range(lax.axis_size("blk"))])


def exchange_by(array, step):
    near_bits = DISTANT - 1
    steps = [d for d in range(1, lax.axis_size("blk")) if not d & DISTANT]
    branches = [functools.partial(exchange, distance=d) for d in steps]
    place = (step // (2 * DISTANT)) * DISTANT + (step & near_bits)
    return lax.switch(place - 1, branches, array)


def body(
    features, w_query, key_weight, value_weight, w_output, virtual_node, cotangent, local_mask,
    counts, shifts,
):
    largest = lax.axis_size("blk") - 1
    low = jnp.min(jnp.where(shifts == 1, largest + 1, shifts))
    high = jnp.max(jnp.where(shifts == largest, 0, shifts))
    own = counts[0]
    halves = jnp.stack([own & 255, own >> 8]).astype(BF)
    tail = jnp.zeros((SENT - BN, D), BF).at[:2].set(jnp.broadcast_to(halves[:, None], (2, D)))
    sent = jnp.concatenate([features, tail], axis=0)
    far_copy, near_copy = exchange(sent, largest), exchange(sent, 1)
    low_far, high_far = low & DISTANT != 0, high & DISTANT != 0
    low_step = jnp.where(low_far, low ^ largest, low)
    high_step = jnp.where(high_far, high ^ largest, high)
    partners = [
        far_copy, near_copy,
        exchange_by(jnp.where(low_far, far_copy, sent), low_step),
        exchange_by(jnp.where(high_far, far_copy, sent), high_step),
    ]
    layer_out, own_grad, back_far, back_near, back_low, back_high, weights, virt = attend(
        counts, features, partners, w_query, key_weight, value_weight, w_output,
        virtual_node[None, :], cotangent, local_mask,
    )
    everyone = ("blk", "sub")
    count_sub = lax.axis_size("sub")
    devices = lax.axis_size("blk") * count_sub
    same_core = [[i for i in range(devices) if i % 2 == core] for core in range(2)]
    siblings = [(i, i ^ 1) for i in range(count_sub)]

    scattered = lax.all_to_all(weights.reshape(devices, 8, 128), everyone, 0, 0)
    near = exchange(back_near, 1)
    low_part = exchange_by(back_low, low_step)
    high_part = exchange_by(back_high, high_step)
    scattered, low_part, high_part, near = lax.optimization_barrier(
        (scattered, low_part, high_part, near)
    )
    onward = (
        back_far.astype(F32)
        + jnp.where(low_far, low_part.astype(F32), 0.0)
        + jnp.where(high_far, high_part.astype(F32), 0.0)
    ).astype(BF)
    onward, scattered = lax.optimization_barrier((onward, scattered))
    far = exchange(onward, largest)
    chunk = jnp.sum(scattered.astype(F32), axis=0)
    packed = jnp.concatenate(
        [chunk, virt[0:1].reshape(2, 128), virt[8:9].reshape(2, 128), jnp.zeros((4, 128), F32)]
    ).astype(BF)
    summed = lax.all_to_all(
        jnp.broadcast_to(packed, (devices // 2, 16, 128)), everyone, 0, 0,
        axis_index_groups=same_core,
    )
    flags = jnp.stack([low_far, high_far]).astype(jnp.int32)
    total = finish(flags, own_grad, near, far, low_part, high_part)
    summed, total = lax.optimization_barrier((summed, total))
    given = lax.ppermute(summed, "sub", siblings)
    core = lax.axis_index("sub") % 2
    pair = jnp.stack([jnp.where(core == 0, summed, given), jnp.where(core == 0, given, summed)], axis=1)
    grads = pair[:, :, :8].astype(F32).transpose(0, 2, 1, 3).reshape(4, D, D)
    grad_virtual = jnp.sum(summed[:, 8:12].astype(F32), axis=0) + jnp.sum(given[:, 8:12].astype(F32), axis=0)
    grad_virtual = (grad_virtual[:2] + grad_virtual[2:]).reshape(D)
    return (
        layer_out, total, grads[0], grads[1], grads[2], grads[3], grad_virtual,
    )


def solution(mesh):
    return jax.shard_map(
        body,
        mesh=mesh,
        in_specs=(
            P(("blk", "sub"), None), P(), P(), P(), P(), P(), P(("blk", "sub"), None),
            P(("blk", "sub"), None), P(("blk", "sub")), P(),
        ),
        out_specs=(P(("blk", "sub"), None), P(("blk", "sub"), None), P(), P(), P(), P(), P()),
        check_vma=False,
    )
```

```python
import functools
import math

import jax
import jax.numpy as jnp
from jax import lax
from jax.experimental import pallas as pl
from jax.experimental.pallas import tpu as pltpu
from jax.sharding import PartitionSpec as P

D = 256
HEADS = 8
HD = D // HEADS
GROUP = 128 // HD
CHUNKS = 5
BN = 512
KEYS = CHUNKS * BN
SENT = BN + 16
NEG_FILL = -1000000000.0
SCALE = 1.0 / math.sqrt(HD)
LOG2E = 1.0 / math.log(2.0)
LN2 = math.log(2.0)
TILE = 512
DISTANT = 4
BF = jnp.bfloat16
F32 = jnp.float32


def dot(a, b):
    return jnp.dot(a, b, preferred_element_type=F32)


def dot_nt(a, b):
    return lax.dot_general(a, b, (((1,), (1,)), ((), ())), preferred_element_type=F32)


def identity(size):
    row = lax.broadcasted_iota(jnp.int32, (size, size), 0)
    return jnp.where(row == lax.broadcasted_iota(jnp.int32, (size, size), 1), 1.0, 0.0).astype(BF)


def dot_nt_exact(a, b):
    return lax.dot_general(
        a, b.astype(F32), (((1,), (1,)), ((), ())), precision=lax.Precision.HIGHEST,
        preferred_element_type=F32,
    )


def attend_kernel(
    count_ref, x_ref, p0_ref, p1_ref, p2_ref, p3_ref, wq_ref, wk_ref, wv_ref, wo_ref, vn_ref,
    cot_ref, mask_ref,
    layer_ref, own_ref, b0_ref, b1_ref, b2_ref, b3_ref, weight_ref, virt_ref,
    qmt, qm, gt, ks, vs, vta, k0t, xt, bias, s_even, s_odd, p_even, p_odd, gmt_even, gmt_odd,
    gm_even, gm_odd, dk_acc, dv_acc, attn_t, dq_t, sv, dpv, dsv, pvn, tops, deltas, vk_cols, vv_cols,
):
    parts = (x_ref, p0_ref, p1_ref, p2_ref, p3_ref)
    x = x_ref[...]
    wq, wk, wv, wo = wq_ref[...], wk_ref[...], wv_ref[...], wo_ref[...]
    vn = jnp.broadcast_to(vn_ref[...], (16, D))
    vk = dot(vn, wk).astype(BF)
    vv = dot(vn, wv).astype(BF)

    wide, tall = identity(BN), identity(D)
    wq_t, wk_t, wv_t = (dot_nt(tall, w).astype(BF) for w in (wq, wk, wv))

    qs = (dot(x, wq) * (SCALE * LOG2E)).astype(BF)
    qt = (dot_nt(wq_t, x) * (SCALE * LOG2E)).astype(BF)
    cot = cot_ref[...]
    g = dot_nt(cot, wo).astype(BF)
    gt_all = dot_nt(wo, cot).astype(BF)
    gt[...] = gt_all.reshape(HEADS, HD, BN)
    qmt[...] = jnp.zeros_like(qmt)
    lane_head = lax.broadcasted_iota(jnp.int32, (BN, 128), 1) // HD
    for h in range(HEADS):
        r = h % GROUP
        lo = (h // GROUP) * 128
        qmt[h, r * HD:(r + 1) * HD, :] = qt[h * HD:(h + 1) * HD]
        qm[h] = jnp.where(lane_head == r, qs[:, lo:lo + 128], jnp.zeros((), BF))

    head_of = lax.broadcasted_iota(jnp.int32, (16, D), 1) // HD
    diag = head_of == lax.broadcasted_iota(jnp.int32, (16, D), 0)
    sv[...] = dot(jnp.where(diag, vk, jnp.zeros((), BF)), qt)[:HEADS].reshape(HEADS, 1, BN) + math.log2(BN)
    dpv[...] = dot(jnp.where(diag, vv, jnp.zeros((), BF)), gt_all)[:HEADS].reshape(HEADS, 1, BN)
    vk_cols[...] = jnp.broadcast_to(vk[:1].astype(F32), (128, D)).T.reshape(HEADS, HD, 128)
    vv_cols[...] = jnp.broadcast_to(vv[:1].astype(F32), (128, D)).T.reshape(HEADS, HD, 128)

    key_row = lax.broadcasted_iota(jnp.int32, (BN, BN), 0)
    query_col = lax.broadcasted_iota(jnp.int32, (BN, BN), 1)
    linked = dot_nt(wide, jnp.where(mask_ref[...] != 0, 1.0, 0.0).astype(BF))
    ok = ((linked != 0.0) | (key_row == query_col)) & (key_row < count_ref[0])
    bias[...] = jnp.where(ok, 0.0, NEG_FILL)

    row_no = lax.broadcasted_iota(jnp.int32, (BN, D), 0).astype(F32)
    lane_no = lax.broadcasted_iota(jnp.int32, (D, BN), 1).astype(F32)
    for c in range(CHUNKS):
        rows = slice(c * BN, (c + 1) * BN)
        xc = parts[c][:BN, :]
        k = dot(xc, wk).astype(BF)
        v = dot(xc, wv).astype(BF)
        kt = dot_nt(wk_t, xc)
        vt = dot_nt(wv_t, xc)
        live_row = jnp.ones((16, BN), BF)
        if c:
            tail = parts[c][BN:, :].astype(F32)
            count = tail[0:1, 0:1] + 256.0 * tail[1:2, 0:1]
            live = row_no < count
            k = jnp.where(live, k, jnp.broadcast_to(vk[:1], (BN, D)))
            v = jnp.where(live, v, jnp.zeros((), BF))
            live_lane = lane_no < count
            kt = jnp.where(live_lane, kt, 0.0)
            vt = jnp.where(live_lane, vt, 0.0)
            live_row = jnp.where(live_lane[:16], 1.0, 0.0).astype(BF)
        for gi in range(2):
            ks[gi, rows, :] = k[:, gi * 128:(gi + 1) * 128]
            vs[gi, rows, :] = v[:, gi * 128:(gi + 1) * 128]
        vt = vt.astype(BF)
        k0t[:, :, rows] = kt.astype(BF).reshape(HEADS, HD, BN)
        xt[c] = dot_nt(tall, xc).astype(BF)
        for h in range(HEADS):
            vta[h, :HD, rows] = vt[h * HD:(h + 1) * HD]
            vta[h, HD:, rows] = live_row

    dk_acc[...] = jnp.zeros_like(dk_acc)
    dv_acc[...] = jnp.zeros_like(dv_acc)
    row_head = lax.broadcasted_iota(jnp.int32, (128, BN), 0) // HD
    s_bufs, p_bufs = (s_even, s_odd), (p_even, p_odd)
    gmt_bufs, gm_bufs = (gmt_even, gmt_odd), (gm_even, gm_odd)

    def step(first, second, third, parity):
        peak = jnp.full((8, BN), -jnp.inf, F32)
        out = jnp.zeros((HD + 16, BN), F32)
        if second is not None:
            top2 = tops[second]
        if third is not None:
            delta3 = deltas[third]
            gi3 = third // GROUP
            dq = vk_cols[third][:, :1] * dsv[third]
        for t in range(KEYS // TILE):
            rows = pl.ds(t * TILE, TILE)
            if first is not None:
                s = dot(ks[first // GROUP, rows, :], qmt[first])
                if (t + 1) * TILE <= BN:
                    s = s + bias[rows, :]
                s_bufs[parity][rows, :] = s
                peak = jnp.maximum(peak, jnp.max(s.reshape(TILE // 8, 8, BN), axis=0))
            if third is not None:
                p3 = p_bufs[parity][rows, :]
                ds = (dot(vs[gi3, rows, :], gmt_bufs[parity][...]) - delta3).astype(BF) * p3
            if second is not None:
                p = jnp.exp2(s_bufs[1 - parity][rows, :] - top2).astype(BF)
                p_bufs[1 - parity][rows, :] = p
                out = out + dot(vta[second, :, rows], p)
            if third is not None:
                dv_acc[gi3, rows, :] += dot(p3, gm_bufs[parity][...])
                dk_acc[gi3, rows, :] += dot(ds, qm[third])
                dq = dq + dot(k0t[third, :, rows], ds)
        if first is not None:
            tops[first] = jnp.maximum(sv[first], jnp.max(peak, axis=0, keepdims=True))
        if second is not None:
            pv = jnp.exp2(sv[second] - top2)
            inv = 1.0 / (out[HD:HD + 1] + pv)
            attn_h = ((out[:HD] + vv_cols[second][:, :1] * pv) * inv).astype(BF)
            attn_t[second] = attn_h
            g_h = gt[second].astype(F32)
            delta = jnp.sum(g_h * attn_h.astype(F32), axis=0, keepdims=True) * inv
            deltas[second] = delta
            g_n = g_h * inv
            gmt32 = jnp.where(
                row_head == second % GROUP, jnp.concatenate([g_n] * GROUP, axis=0), 0.0
            )
            gmt_bufs[1 - parity][...] = gmt32.astype(BF)
            gm_bufs[1 - parity][...] = gmt32.T.astype(BF)
            dsv[second] = pv * (dpv[second] * inv - delta)
            pvn[second] = pv * inv
        if third is not None:
            dq_t[third] = (dq * SCALE).astype(BF)

    step(0, None, None, 0)
    step(1, 0, None, 1)

    @pl.loop(1, HEADS // 2)
    def _(pair):
        h = 2 * pair
        step(h, h - 1, h - 2, 0)
        step(h + 1, h, h - 1, 1)

    step(None, HEADS - 1, HEADS - 2, 0)
    step(None, None, HEADS - 1, 1)

    at = attn_t[...].reshape(D, BN)
    attn = dot_nt(wide, at).astype(BF)
    layer_ref[...] = (x.astype(F32) + dot(attn, wo)).astype(BF)
    dqt = dq_t[...].reshape(D, BN)
    dqm = dot_nt(wide, dqt).astype(BF)

    grad_query = dot(xt[0], dqm)
    grad_output = dot(at, cot)
    keep = diag[:HEADS]
    dsv_all = dsv[...].reshape(HEADS, BN)
    pvn_all = pvn[...].reshape(HEADS, BN)
    vkey = jnp.sum(jnp.where(keep, dot(dsv_all.astype(BF), qs), 0.0), axis=0, keepdims=True) * LN2
    vvalue = jnp.sum(jnp.where(keep, dot(pvn_all.astype(BF), g), 0.0), axis=0, keepdims=True)
    vn_col = jnp.broadcast_to(vn_ref[...].astype(F32), (128, D)).T[:, :1]
    grad_key = vn_col * vkey
    grad_value = vn_col * vvalue
    backs = (None, b0_ref, b1_ref, b2_ref, b3_ref)
    for c in range(CHUNKS):
        rows = slice(c * BN, (c + 1) * BN)
        dk = jnp.concatenate([dk_acc[0, rows, :], dk_acc[1, rows, :]], axis=1) * LN2
        dv = jnp.concatenate([dv_acc[0, rows, :], dv_acc[1, rows, :]], axis=1)
        if c:
            tail = parts[c][BN:, :].astype(F32)
            live = row_no < tail[0:1, 0:1] + 256.0 * tail[1:2, 0:1]
            dk = jnp.where(live, dk, 0.0)
            dv = jnp.where(live, dv, 0.0)
        dk = dk.astype(BF)
        dv = dv.astype(BF)
        grad_key = grad_key + dot(xt[c], dk)
        grad_value = grad_value + dot(xt[c], dv)
        back = dot_nt(dk, wk) + dot_nt(dv, wv)
        if c:
            backs[c][...] = back.astype(BF)
        else:
            own_ref[...] = back + dot_nt(dqm, wq) + cot.astype(F32)
    for n, grad in enumerate((grad_query, grad_key, grad_value, grad_output)):
        for j in range(2):
            weight_ref[n * 32:(n + 1) * 32, j] = grad[:, j * 128:(j + 1) * 128].reshape(32, 8, 128).astype(BF)
    virt = dot_nt_exact(jnp.broadcast_to(vkey, (8, D)), wk) + dot_nt_exact(
        jnp.broadcast_to(vvalue, (8, D)), wv
    )
    high = virt.astype(BF).astype(F32)
    virt_ref[0:8] = high
    virt_ref[8:16] = virt - high


def attend(count, x, partners, wq, wk, wv, wo, vn, cot, mask):
    vmem = pl.BlockSpec(memory_space=pltpu.VMEM)
    sds = jax.ShapeDtypeStruct
    return pl.pallas_call(
        attend_kernel,
        out_shape=(
            sds((BN, D), BF), sds((BN, D), F32), sds((BN, D), BF), sds((BN, D), BF),
            sds((BN, D), BF), sds((BN, D), BF), sds((128, 2, 8, 128), BF), sds((16, D), F32),
        ),
        in_specs=[pl.BlockSpec(memory_space=pltpu.SMEM)] + [vmem] * 12,
        out_specs=[vmem] * 8,
        scratch_shapes=[
            pltpu.VMEM((HEADS, 128, BN), BF),
            pltpu.VMEM((HEADS, BN, 128), BF),
            pltpu.VMEM((HEADS, HD, BN), BF),
            pltpu.VMEM((2, KEYS, 128), BF),
            pltpu.VMEM((2, KEYS, 128), BF),
            pltpu.VMEM((HEADS, HD + 16, KEYS), BF),
            pltpu.VMEM((HEADS, HD, KEYS), BF),
            pltpu.VMEM((CHUNKS, D, BN), BF),
            pltpu.VMEM((BN, BN), F32),
            pltpu.VMEM((KEYS, BN), F32),
            pltpu.VMEM((KEYS, BN), F32),
            pltpu.VMEM((KEYS, BN), BF),
            pltpu.VMEM((KEYS, BN), BF),
            pltpu.VMEM((128, BN), BF),
            pltpu.VMEM((128, BN), BF),
            pltpu.VMEM((BN, 128), BF),
            pltpu.VMEM((BN, 128), BF),
            pltpu.VMEM((2, KEYS, 128), F32),
            pltpu.VMEM((2, KEYS, 128), F32),
            pltpu.VMEM((HEADS, HD, BN), BF),
            pltpu.VMEM((HEADS, HD, BN), BF),
            pltpu.VMEM((HEADS, 1, BN), F32),
            pltpu.VMEM((HEADS, 1, BN), F32),
            pltpu.VMEM((HEADS, 1, BN), F32),
            pltpu.VMEM((HEADS, 1, BN), F32),
            pltpu.VMEM((HEADS, 1, BN), F32),
            pltpu.VMEM((HEADS, 1, BN), F32),
            pltpu.VMEM((HEADS, HD, 128), F32),
            pltpu.VMEM((HEADS, HD, 128), F32),
        ],
        compiler_params=pltpu.CompilerParams(vmem_limit_bytes=56 * 1024 * 1024),
        cost_estimate=pl.CostEstimate(flops=8 * 10**9, bytes_accessed=4 * 10**6, transcendentals=10**7),
        name="attend",
    )(count, x, *partners, wq, wk, wv, wo, vn, cot, mask)


def finish_kernel(flags_ref, own_ref, near_ref, far_ref, low_ref, high_ref, out_ref):
    total = own_ref[...] + near_ref[...].astype(F32) + far_ref[...].astype(F32)
    total = total + jnp.where(flags_ref[0] != 0, 0.0, low_ref[...].astype(F32))
    total = total + jnp.where(flags_ref[1] != 0, 0.0, high_ref[...].astype(F32))
    out_ref[...] = total.astype(BF)


def finish(flags, own, near, far, low, high):
    vmem = pl.BlockSpec(memory_space=pltpu.VMEM)
    return pl.pallas_call(
        finish_kernel,
        out_shape=jax.ShapeDtypeStruct((BN, D), BF),
        in_specs=[pl.BlockSpec(memory_space=pltpu.SMEM)] + [vmem] * 5,
        out_specs=vmem,
        cost_estimate=pl.CostEstimate(flops=10**6, bytes_accessed=2 * 10**6, transcendentals=0),
        name="finish",
    )(flags, own, near, far, low, high)


def exchange(array, distance):
    return lax.ppermute(array, "blk", [(i, i ^ distance) for i in range(lax.axis_size("blk"))])


def exchange_by(array, step):
    near_bits = DISTANT - 1
    steps = [d for d in range(1, lax.axis_size("blk")) if not d & DISTANT]
    branches = [functools.partial(exchange, distance=d) for d in steps]
    place = (step // (2 * DISTANT)) * DISTANT + (step & near_bits)
    return lax.switch(place - 1, branches, array)


def body(
    features, w_query, key_weight, value_weight, w_output, virtual_node, cotangent, local_mask,
    counts, shifts,
):
    largest = lax.axis_size("blk") - 1
    low = jnp.min(jnp.where(shifts == 1, largest + 1, shifts))
    high = jnp.max(jnp.where(shifts == largest, 0, shifts))
    own = counts[0]
    halves = jnp.stack([own & 255, own >> 8]).astype(BF)
    tail = jnp.zeros((SENT - BN, D), BF).at[:2].set(jnp.broadcast_to(halves[:, None], (2, D)))
    sent = jnp.concatenate([features, tail], axis=0)
    far_copy, near_copy = exchange(sent, largest), exchange(sent, 1)
    low_far, high_far = low & DISTANT != 0, high & DISTANT != 0
    low_step = jnp.where(low_far, low ^ largest, low)
    high_step = jnp.where(high_far, high ^ largest, high)
    partners = [
        far_copy, near_copy,
        exchange_by(jnp.where(low_far, far_copy, sent), low_step),
        exchange_by(jnp.where(high_far, far_copy, sent), high_step),
    ]
    layer_out, own_grad, back_far, back_near, back_low, back_high, weights, virt = attend(
        counts, features, partners, w_query, key_weight, value_weight, w_output,
        virtual_node[None, :], cotangent, local_mask,
    )
    everyone = ("blk", "sub")
    count_sub = lax.axis_size("sub")
    devices = lax.axis_size("blk") * count_sub
    same_core = [[i for i in range(devices) if i % 2 == core] for core in range(2)]
    siblings = [(i, i ^ 1) for i in range(count_sub)]

    scattered = lax.all_to_all(weights.reshape(devices, 8, 128), everyone, 0, 0)
    near = exchange(back_near, 1)
    low_part = exchange_by(back_low, low_step)
    scattered, low_part, near = lax.optimization_barrier((scattered, low_part, near))
    chunk = jnp.sum(scattered.astype(F32), axis=0)
    packed = jnp.concatenate(
        [chunk, virt[0:1].reshape(2, 128), virt[8:9].reshape(2, 128), jnp.zeros((4, 128), F32)]
    ).astype(BF)
    packed, back_high = lax.optimization_barrier((packed, back_high))
    summed = lax.all_to_all(
        jnp.broadcast_to(packed, (devices // 2, 16, 128)), everyone, 0, 0,
        axis_index_groups=same_core,
    )
    high_part = exchange_by(back_high, high_step)
    onward = (
        back_far.astype(F32)
        + jnp.where(low_far, low_part.astype(F32), 0.0)
        + jnp.where(high_far, high_part.astype(F32), 0.0)
    ).astype(BF)
    summed, onward = lax.optimization_barrier((summed, onward))
    far = exchange(onward, largest)
    given = lax.ppermute(summed, "sub", siblings)
    flags = jnp.stack([low_far, high_far]).astype(jnp.int32)
    total = finish(flags, own_grad, near, far, low_part, high_part)
    core = lax.axis_index("sub") % 2
    pair = jnp.stack([jnp.where(core == 0, summed, given), jnp.where(core == 0, given, summed)], axis=1)
    grads = pair[:, :, :8].astype(F32).transpose(0, 2, 1, 3).reshape(4, D, D)
    grad_virtual = jnp.sum(summed[:, 8:12].astype(F32), axis=0) + jnp.sum(given[:, 8:12].astype(F32), axis=0)
    grad_virtual = (grad_virtual[:2] + grad_virtual[2:]).reshape(D)
    return (
        layer_out, total, grads[0], grads[1], grads[2], grads[3], grad_virtual,
    )


def solution(mesh):
    return jax.shard_map(
        body,
        mesh=mesh,
        in_specs=(
            P(("blk", "sub"), None), P(), P(), P(), P(), P(), P(("blk", "sub"), None),
            P(("blk", "sub"), None), P(("blk", "sub")), P(),
        ),
        out_specs=(P(("blk", "sub"), None), P(("blk", "sub"), None), P(), P(), P(), P(), P()),
        check_vma=False,
    )
```

```python
import functools
import math

import jax
import jax.numpy as jnp
from jax import lax
from jax.experimental import pallas as pl
from jax.experimental.pallas import tpu as pltpu
from jax.sharding import PartitionSpec as P

D = 256
HEADS = 8
HD = D // HEADS
GROUP = 128 // HD
CHUNKS = 5
BN = 512
KEYS = CHUNKS * BN
SENT = BN + 16
NEG_FILL = -1000000000.0
SCALE = 1.0 / math.sqrt(HD)
LOG2E = 1.0 / math.log(2.0)
LN2 = math.log(2.0)
TILE = 512
DISTANT = 4
BF = jnp.bfloat16
F32 = jnp.float32


def dot(a, b):
    return jnp.dot(a, b, preferred_element_type=F32)


def dot_nt(a, b):
    return lax.dot_general(a, b, (((1,), (1,)), ((), ())), preferred_element_type=F32)


def dot_nt_exact(a, b):
    return lax.dot_general(
        a, b.astype(F32), (((1,), (1,)), ((), ())), precision=lax.Precision.HIGHEST,
        preferred_element_type=F32,
    )


def attend_kernel(
    count_ref, x_ref, p0_ref, p1_ref, p2_ref, p3_ref, wq_ref, wk_ref, wv_ref, wo_ref, vn_ref,
    cot_ref, mask_ref,
    layer_ref, own_ref, b0_ref, b1_ref, b2_ref, b3_ref, weight_ref, virt_ref,
    qmt, qm, gt, ks, vs, vta, k0t, xt, bias, s_even, s_odd, p_even, p_odd, gmt_even, gmt_odd,
    gm_even, gm_odd, dk_acc, dv_acc, attn_t, dq_t, sv, dpv, dsv, pvn, tops, deltas, vk_cols, vv_cols,
):
    parts = (x_ref, p0_ref, p1_ref, p2_ref, p3_ref)
    x = x_ref[...]
    wq, wk, wv, wo = wq_ref[...], wk_ref[...], wv_ref[...], wo_ref[...]
    vn = jnp.broadcast_to(vn_ref[...], (16, D))
    vk = dot(vn, wk).astype(BF)
    vv = dot(vn, wv).astype(BF)

    q32 = dot(x, wq) * (SCALE * LOG2E)
    qs = q32.astype(BF)
    qt = qs.T
    cot = cot_ref[...]
    g32 = dot_nt(cot, wo)
    g = g32.astype(BF)
    gt_all = g.T
    gt[...] = gt_all.reshape(HEADS, HD, BN)
    qmt[...] = jnp.zeros_like(qmt)
    lane_head = lax.broadcasted_iota(jnp.int32, (BN, 128), 1) // HD
    for h in range(HEADS):
        r = h % GROUP
        lo = (h // GROUP) * 128
        qmt[h, r * HD:(r + 1) * HD, :] = qt[h * HD:(h + 1) * HD]
        qm[h] = jnp.where(lane_head == r, qs[:, lo:lo + 128], jnp.zeros((), BF))

    head_of = lax.broadcasted_iota(jnp.int32, (16, D), 1) // HD
    diag = head_of == lax.broadcasted_iota(jnp.int32, (16, D), 0)
    sv[...] = dot(jnp.where(diag, vk, jnp.zeros((), BF)), qt)[:HEADS].reshape(HEADS, 1, BN) + math.log2(BN)
    dpv[...] = dot(jnp.where(diag, vv, jnp.zeros((), BF)), gt_all)[:HEADS].reshape(HEADS, 1, BN)
    vk_cols[...] = jnp.broadcast_to(vk[:1].astype(F32), (128, D)).T.reshape(HEADS, HD, 128)
    vv_cols[...] = jnp.broadcast_to(vv[:1].astype(F32), (128, D)).T.reshape(HEADS, HD, 128)

    key_row = lax.broadcasted_iota(jnp.int32, (BN, BN), 0)
    query_col = lax.broadcasted_iota(jnp.int32, (BN, BN), 1)
    linked = jnp.where(mask_ref[...] != 0, 1.0, 0.0).astype(BF).T.astype(F32)
    ok = ((linked != 0.0) | (key_row == query_col)) & (key_row < count_ref[0])
    bias[...] = jnp.where(ok, 0.0, NEG_FILL)

    row_no = lax.broadcasted_iota(jnp.int32, (BN, D), 0).astype(F32)
    lane_no = lax.broadcasted_iota(jnp.int32, (16, BN), 1).astype(F32)
    for c in range(CHUNKS):
        rows = slice(c * BN, (c + 1) * BN)
        xc = parts[c][:BN, :]
        k32 = dot(xc, wk)
        v32 = dot(xc, wv)
        k = k32.astype(BF)
        live_row = jnp.ones((16, BN), BF)
        if c:
            tail = parts[c][BN:, :].astype(F32)
            count = tail[0:1, 0:1] + 256.0 * tail[1:2, 0:1]
            live = row_no < count
            k = jnp.where(live, k, jnp.broadcast_to(vk[:1], (BN, D)))
            k32 = jnp.where(live, k32, 0.0)
            v32 = jnp.where(live, v32, 0.0)
            live_row = jnp.where(lane_no < count, 1.0, 0.0).astype(BF)
        v = v32.astype(BF)
        for gi in range(2):
            ks[gi, rows, :] = k[:, gi * 128:(gi + 1) * 128]
            vs[gi, rows, :] = v[:, gi * 128:(gi + 1) * 128]
        vt = v.T
        k0t[:, :, rows] = k32.astype(BF).T.reshape(HEADS, HD, BN)
        xt[c] = xc.T
        for h in range(HEADS):
            vta[h, :HD, rows] = vt[h * HD:(h + 1) * HD]
            vta[h, HD:, rows] = live_row

    dk_acc[...] = jnp.zeros_like(dk_acc)
    dv_acc[...] = jnp.zeros_like(dv_acc)
    row_head = lax.broadcasted_iota(jnp.int32, (128, BN), 0) // HD
    s_bufs, p_bufs = (s_even, s_odd), (p_even, p_odd)
    gmt_bufs, gm_bufs = (gmt_even, gmt_odd), (gm_even, gm_odd)

    def step(first, second, third, parity):
        peak = jnp.full((8, BN), -jnp.inf, F32)
        out = jnp.zeros((HD + 16, BN), F32)
        if second is not None:
            top2 = tops[second]
        if third is not None:
            delta3 = deltas[third]
            gi3 = third // GROUP
            dq = vk_cols[third][:, :1] * dsv[third]
        for t in range(KEYS // TILE):
            rows = pl.ds(t * TILE, TILE)
            if first is not None:
                s = dot(ks[first // GROUP, rows, :], qmt[first])
                if (t + 1) * TILE <= BN:
                    s = s + bias[rows, :]
                s_bufs[parity][rows, :] = s
                peak = jnp.maximum(peak, jnp.max(s.reshape(TILE // 8, 8, BN), axis=0))
            if third is not None:
                p3 = p_bufs[parity][rows, :]
                ds = (dot(vs[gi3, rows, :], gmt_bufs[parity][...]) - delta3).astype(BF) * p3
            if second is not None:
                p = jnp.exp2(s_bufs[1 - parity][rows, :] - top2).astype(BF)
                p_bufs[1 - parity][rows, :] = p
                out = out + dot(vta[second, :, rows], p)
            if third is not None:
                dv_acc[gi3, rows, :] += dot(p3, gm_bufs[parity][...])
                dk_acc[gi3, rows, :] += dot(ds, qm[third])
                dq = dq + dot(k0t[third, :, rows], ds)
        if first is not None:
            tops[first] = jnp.maximum(sv[first], jnp.max(peak, axis=0, keepdims=True))
        if second is not None:
            pv = jnp.exp2(sv[second] - top2)
            inv = 1.0 / (out[HD:HD + 1] + pv)
            attn_h = ((out[:HD] + vv_cols[second][:, :1] * pv) * inv).astype(BF)
            attn_t[second] = attn_h
            g_h = gt[second].astype(F32)
            delta = jnp.sum(g_h * attn_h.astype(F32), axis=0, keepdims=True) * inv
            deltas[second] = delta
            g_n = g_h * inv
            gmt32 = jnp.where(
                row_head == second % GROUP, jnp.concatenate([g_n] * GROUP, axis=0), 0.0
            )
            gmt_bufs[1 - parity][...] = gmt32.astype(BF)
            gm_bufs[1 - parity][...] = gmt32.astype(BF).T
            dsv[second] = pv * (dpv[second] * inv - delta)
            pvn[second] = pv * inv
        if third is not None:
            dq_t[third] = (dq * SCALE).astype(BF)

    step(0, None, None, 0)
    step(1, 0, None, 1)

    @pl.loop(1, HEADS // 2)
    def _(pair):
        h = 2 * pair
        step(h, h - 1, h - 2, 0)
        step(h + 1, h, h - 1, 1)

    step(None, HEADS - 1, HEADS - 2, 0)
    step(None, None, HEADS - 1, 1)

    at = attn_t[...].reshape(D, BN)
    attn = at.T
    layer_ref[...] = (x.astype(F32) + dot(attn, wo)).astype(BF)
    dqt = dq_t[...].reshape(D, BN)
    dqm = dqt.T

    grad_query = dot(xt[0], dqm)
    grad_output = dot(at, cot)
    keep = diag[:HEADS]
    dsv_all = dsv[...].reshape(HEADS, BN)
    pvn_all = pvn[...].reshape(HEADS, BN)
    vkey = jnp.sum(jnp.where(keep, dot(dsv_all.astype(BF), qs), 0.0), axis=0, keepdims=True) * LN2
    vvalue = jnp.sum(jnp.where(keep, dot(pvn_all.astype(BF), g), 0.0), axis=0, keepdims=True)
    vn_col = jnp.broadcast_to(vn_ref[...].astype(F32), (128, D)).T[:, :1]
    grad_key = vn_col * vkey
    grad_value = vn_col * vvalue
    backs = (None, b0_ref, b1_ref, b2_ref, b3_ref)
    for c in range(CHUNKS):
        rows = slice(c * BN, (c + 1) * BN)
        dk = jnp.concatenate([dk_acc[0, rows, :], dk_acc[1, rows, :]], axis=1) * LN2
        dv = jnp.concatenate([dv_acc[0, rows, :], dv_acc[1, rows, :]], axis=1)
        if c:
            tail = parts[c][BN:, :].astype(F32)
            live = row_no < tail[0:1, 0:1] + 256.0 * tail[1:2, 0:1]
            dk = jnp.where(live, dk, 0.0)
            dv = jnp.where(live, dv, 0.0)
        dk = dk.astype(BF)
        dv = dv.astype(BF)
        grad_key = grad_key + dot(xt[c], dk)
        grad_value = grad_value + dot(xt[c], dv)
        back = dot_nt(dk, wk) + dot_nt(dv, wv)
        if c:
            backs[c][...] = back.astype(BF)
        else:
            own_ref[...] = back + dot_nt(dqm, wq) + cot.astype(F32)
    for n, grad in enumerate((grad_query, grad_key, grad_value, grad_output)):
        for j in range(2):
            weight_ref[n * 32:(n + 1) * 32, j] = grad[:, j * 128:(j + 1) * 128].reshape(32, 8, 128).astype(BF)
    virt = dot_nt_exact(jnp.broadcast_to(vkey, (8, D)), wk) + dot_nt_exact(
        jnp.broadcast_to(vvalue, (8, D)), wv
    )
    high = virt.astype(BF).astype(F32)
    virt_ref[0:8] = high
    virt_ref[8:16] = virt - high


def attend(count, x, partners, wq, wk, wv, wo, vn, cot, mask):
    vmem = pl.BlockSpec(memory_space=pltpu.VMEM)
    sds = jax.ShapeDtypeStruct
    return pl.pallas_call(
        attend_kernel,
        out_shape=(
            sds((BN, D), BF), sds((BN, D), F32), sds((BN, D), BF), sds((BN, D), BF),
            sds((BN, D), BF), sds((BN, D), BF), sds((128, 2, 8, 128), BF), sds((16, D), F32),
        ),
        in_specs=[pl.BlockSpec(memory_space=pltpu.SMEM)] + [vmem] * 12,
        out_specs=[vmem] * 8,
        scratch_shapes=[
            pltpu.VMEM((HEADS, 128, BN), BF),
            pltpu.VMEM((HEADS, BN, 128), BF),
            pltpu.VMEM((HEADS, HD, BN), BF),
            pltpu.VMEM((2, KEYS, 128), BF),
            pltpu.VMEM((2, KEYS, 128), BF),
            pltpu.VMEM((HEADS, HD + 16, KEYS), BF),
            pltpu.VMEM((HEADS, HD, KEYS), BF),
            pltpu.VMEM((CHUNKS, D, BN), BF),
            pltpu.VMEM((BN, BN), F32),
            pltpu.VMEM((KEYS, BN), F32),
            pltpu.VMEM((KEYS, BN), F32),
            pltpu.VMEM((KEYS, BN), BF),
            pltpu.VMEM((KEYS, BN), BF),
            pltpu.VMEM((128, BN), BF),
            pltpu.VMEM((128, BN), BF),
            pltpu.VMEM((BN, 128), BF),
            pltpu.VMEM((BN, 128), BF),
            pltpu.VMEM((2, KEYS, 128), F32),
            pltpu.VMEM((2, KEYS, 128), F32),
            pltpu.VMEM((HEADS, HD, BN), BF),
            pltpu.VMEM((HEADS, HD, BN), BF),
            pltpu.VMEM((HEADS, 1, BN), F32),
            pltpu.VMEM((HEADS, 1, BN), F32),
            pltpu.VMEM((HEADS, 1, BN), F32),
            pltpu.VMEM((HEADS, 1, BN), F32),
            pltpu.VMEM((HEADS, 1, BN), F32),
            pltpu.VMEM((HEADS, 1, BN), F32),
            pltpu.VMEM((HEADS, HD, 128), F32),
            pltpu.VMEM((HEADS, HD, 128), F32),
        ],
        compiler_params=pltpu.CompilerParams(vmem_limit_bytes=44 * 1024 * 1024),
        cost_estimate=pl.CostEstimate(flops=8 * 10**9, bytes_accessed=4 * 10**6, transcendentals=10**7),
        name="attend",
    )(count, x, *partners, wq, wk, wv, wo, vn, cot, mask)


def finish_kernel(flags_ref, own_ref, near_ref, far_ref, low_ref, high_ref, out_ref):
    total = own_ref[...] + near_ref[...].astype(F32) + far_ref[...].astype(F32)
    total = total + jnp.where(flags_ref[0] != 0, 0.0, low_ref[...].astype(F32))
    total = total + jnp.where(flags_ref[1] != 0, 0.0, high_ref[...].astype(F32))
    out_ref[...] = total.astype(BF)


def finish(flags, own, near, far, low, high):
    vmem = pl.BlockSpec(memory_space=pltpu.VMEM)
    return pl.pallas_call(
        finish_kernel,
        out_shape=jax.ShapeDtypeStruct((BN, D), BF),
        in_specs=[pl.BlockSpec(memory_space=pltpu.SMEM)] + [vmem] * 5,
        out_specs=vmem,
        cost_estimate=pl.CostEstimate(flops=10**6, bytes_accessed=2 * 10**6, transcendentals=0),
        name="finish",
    )(flags, own, near, far, low, high)


def exchange(array, distance):
    return lax.ppermute(array, "blk", [(i, i ^ distance) for i in range(lax.axis_size("blk"))])


def exchange_by(array, step):
    near_bits = DISTANT - 1
    steps = [d for d in range(1, lax.axis_size("blk")) if not d & DISTANT]
    branches = [functools.partial(exchange, distance=d) for d in steps]
    place = (step // (2 * DISTANT)) * DISTANT + (step & near_bits)
    return lax.switch(place - 1, branches, array)


def body(
    features, w_query, key_weight, value_weight, w_output, virtual_node, cotangent, local_mask,
    counts, shifts,
):
    largest = lax.axis_size("blk") - 1
    low = jnp.min(jnp.where(shifts == 1, largest + 1, shifts))
    high = jnp.max(jnp.where(shifts == largest, 0, shifts))
    own = counts[0]
    halves = jnp.stack([own & 255, own >> 8]).astype(BF)
    tail = jnp.zeros((SENT - BN, D), BF).at[:2].set(jnp.broadcast_to(halves[:, None], (2, D)))
    sent = jnp.concatenate([features, tail], axis=0)
    far_copy, near_copy = exchange(sent, largest), exchange(sent, 1)
    low_far, high_far = low & DISTANT != 0, high & DISTANT != 0
    low_step = jnp.where(low_far, low ^ largest, low)
    high_step = jnp.where(high_far, high ^ largest, high)
    partners = [
        far_copy, near_copy,
        exchange_by(jnp.where(low_far, far_copy, sent), low_step),
        exchange_by(jnp.where(high_far, far_copy, sent), high_step),
    ]
    layer_out, own_grad, back_far, back_near, back_low, back_high, weights, virt = attend(
        counts, features, partners, w_query, key_weight, value_weight, w_output,
        virtual_node[None, :], cotangent, local_mask,
    )
    everyone = ("blk", "sub")
    count_sub = lax.axis_size("sub")
    devices = lax.axis_size("blk") * count_sub
    same_core = [[i for i in range(devices) if i % 2 == core] for core in range(2)]
    siblings = [(i, i ^ 1) for i in range(count_sub)]

    scattered = lax.all_to_all(weights.reshape(devices, 8, 128), everyone, 0, 0)
    near = exchange(back_near, 1)
    low_part = exchange_by(back_low, low_step)
    high_part = exchange_by(back_high, high_step)
    scattered, low_part, high_part, near = lax.optimization_barrier(
        (scattered, low_part, high_part, near)
    )
    onward = (
        back_far.astype(F32)
        + jnp.where(low_far, low_part.astype(F32), 0.0)
        + jnp.where(high_far, high_part.astype(F32), 0.0)
    ).astype(BF)
    onward, scattered = lax.optimization_barrier((onward, scattered))
    far = exchange(onward, largest)
    chunk = jnp.sum(scattered.astype(F32), axis=0)
    packed = jnp.concatenate(
        [chunk, virt[0:1].reshape(2, 128), virt[8:9].reshape(2, 128), jnp.zeros((4, 128), F32)]
    ).astype(BF)

    def gather(tiles):
        summed = lax.all_to_all(tiles, everyone, 0, 0, axis_index_groups=same_core)
        return summed, lax.ppermute(summed, "sub", siblings)

    summed, given = lax.cond(
        shifts[0] > 0, gather, lambda tiles: (tiles, tiles),
        jnp.broadcast_to(packed, (devices // 2, 16, 128)),
    )
    flags = jnp.stack([low_far, high_far]).astype(jnp.int32)
    total = finish(flags, own_grad, near, far, low_part, high_part)
    core = lax.axis_index("sub") % 2
    pair = jnp.stack([jnp.where(core == 0, summed, given), jnp.where(core == 0, given, summed)], axis=1)
    grads = pair[:, :, :8].astype(F32).transpose(0, 2, 1, 3).reshape(4, D, D)
    grad_virtual = jnp.sum(summed[:, 8:12].astype(F32), axis=0) + jnp.sum(given[:, 8:12].astype(F32), axis=0)
    grad_virtual = (grad_virtual[:2] + grad_virtual[2:]).reshape(D)
    return (
        layer_out, total, grads[0], grads[1], grads[2], grads[3], grad_virtual,
    )


def solution(mesh):
    return jax.shard_map(
        body,
        mesh=mesh,
        in_specs=(
            P(("blk", "sub"), None), P(), P(), P(), P(), P(), P(("blk", "sub"), None),
            P(("blk", "sub"), None), P(("blk", "sub")), P(),
        ),
        out_specs=(P(("blk", "sub"), None), P(("blk", "sub"), None), P(), P(), P(), P(), P()),
        check_vma=False,
    )
```

```python
import functools
import math

import jax
import jax.numpy as jnp
from jax import lax
from jax.experimental import pallas as pl
from jax.experimental.pallas import tpu as pltpu
from jax.sharding import PartitionSpec as P

D = 256
HEADS = 8
HD = D // HEADS
GROUP = 128 // HD
CHUNKS = 5
BN = 512
KEYS = CHUNKS * BN
SENT = BN + 16
NEG_FILL = -1000000000.0
SCALE = 1.0 / math.sqrt(HD)
LOG2E = 1.0 / math.log(2.0)
LN2 = math.log(2.0)
TILE = 512
DISTANT = 4
BF = jnp.bfloat16
F32 = jnp.float32


def dot(a, b):
    return jnp.dot(a, b, preferred_element_type=F32)


def dot_nt(a, b):
    return lax.dot_general(a, b, (((1,), (1,)), ((), ())), preferred_element_type=F32)


def dot_nt_exact(a, b):
    return lax.dot_general(
        a, b.astype(F32), (((1,), (1,)), ((), ())), precision=lax.Precision.HIGHEST,
        preferred_element_type=F32,
    )


def attend_kernel(
    count_ref, x_ref, p0_ref, p1_ref, p2_ref, p3_ref, wq_ref, wk_ref, wv_ref, wo_ref, vn_ref,
    cot_ref, mask_ref,
    layer_ref, own_ref, b0_ref, b1_ref, b2_ref, b3_ref, weight_ref,
    qmt, qm, gt, ks, vs, vta, k0t, xt, bias, s_even, s_odd, p_even, p_odd, gmt_even, gmt_odd,
    gm_even, gm_odd, dk_acc, dv_acc, attn_t, dq_t, sv, dpv, dsv, pvn, tops, deltas, vk_cols, vv_cols,
):
    parts = (x_ref, p0_ref, p1_ref, p2_ref, p3_ref)
    x = x_ref[...]
    wq, wk, wv, wo = wq_ref[...], wk_ref[...], wv_ref[...], wo_ref[...]
    vn = jnp.broadcast_to(vn_ref[...], (16, D))
    vk = dot(vn, wk).astype(BF)
    vv = dot(vn, wv).astype(BF)

    q32 = dot(x, wq) * (SCALE * LOG2E)
    qs = q32.astype(BF)
    qt = qs.T
    cot = cot_ref[...]
    g32 = dot_nt(cot, wo)
    g = g32.astype(BF)
    gt_all = g.T
    gt[...] = gt_all.reshape(HEADS, HD, BN)
    qmt[...] = jnp.zeros_like(qmt)
    lane_head = lax.broadcasted_iota(jnp.int32, (BN, 128), 1) // HD
    for h in range(HEADS):
        r = h % GROUP
        lo = (h // GROUP) * 128
        qmt[h, r * HD:(r + 1) * HD, :] = qt[h * HD:(h + 1) * HD]
        qm[h] = jnp.where(lane_head == r, qs[:, lo:lo + 128], jnp.zeros((), BF))

    head_of = lax.broadcasted_iota(jnp.int32, (16, D), 1) // HD
    diag = head_of == lax.broadcasted_iota(jnp.int32, (16, D), 0)
    sv[...] = dot(jnp.where(diag, vk, jnp.zeros((), BF)), qt)[:HEADS].reshape(HEADS, 1, BN) + math.log2(BN)
    dpv[...] = dot(jnp.where(diag, vv, jnp.zeros((), BF)), gt_all)[:HEADS].reshape(HEADS, 1, BN)
    vk_cols[...] = jnp.broadcast_to(vk[:1].astype(F32), (128, D)).T.reshape(HEADS, HD, 128)
    vv_cols[...] = jnp.broadcast_to(vv[:1].astype(F32), (128, D)).T.reshape(HEADS, HD, 128)

    key_row = lax.broadcasted_iota(jnp.int32, (BN, BN), 0)
    query_col = lax.broadcasted_iota(jnp.int32, (BN, BN), 1)
    linked = jnp.where(mask_ref[...] != 0, 1.0, 0.0).astype(BF).T.astype(F32)
    ok = ((linked != 0.0) | (key_row == query_col)) & (key_row < count_ref[0])
    bias[...] = jnp.where(ok, 0.0, NEG_FILL)

    row_no = lax.broadcasted_iota(jnp.int32, (BN, D), 0).astype(F32)
    lane_no = lax.broadcasted_iota(jnp.int32, (16, BN), 1).astype(F32)
    for c in range(CHUNKS):
        rows = slice(c * BN, (c + 1) * BN)
        xc = parts[c][:BN, :]
        k32 = dot(xc, wk)
        v32 = dot(xc, wv)
        k = k32.astype(BF)
        live_row = jnp.ones((16, BN), BF)
        if c:
            tail = parts[c][BN:, :].astype(F32)
            count = tail[0:1, 0:1] + 256.0 * tail[1:2, 0:1]
            live = row_no < count
            k = jnp.where(live, k, jnp.broadcast_to(vk[:1], (BN, D)))
            k32 = jnp.where(live, k32, 0.0)
            v32 = jnp.where(live, v32, 0.0)
            live_row = jnp.where(lane_no < count, 1.0, 0.0).astype(BF)
        v = v32.astype(BF)
        for gi in range(2):
            ks[gi, rows, :] = k[:, gi * 128:(gi + 1) * 128]
            vs[gi, rows, :] = v[:, gi * 128:(gi + 1) * 128]
        vt = v.T
        k0t[:, :, rows] = k32.astype(BF).T.reshape(HEADS, HD, BN)
        xt[c] = xc.T
        for h in range(HEADS):
            vta[h, :HD, rows] = vt[h * HD:(h + 1) * HD]
            vta[h, HD:, rows] = live_row

    dk_acc[...] = jnp.zeros_like(dk_acc)
    dv_acc[...] = jnp.zeros_like(dv_acc)
    row_head = lax.broadcasted_iota(jnp.int32, (128, BN), 0) // HD
    s_bufs, p_bufs = (s_even, s_odd), (p_even, p_odd)
    gmt_bufs, gm_bufs = (gmt_even, gmt_odd), (gm_even, gm_odd)

    def step(first, second, third, parity):
        peak = jnp.full((8, BN), -jnp.inf, F32)
        out = jnp.zeros((HD + 16, BN), F32)
        if second is not None:
            top2 = tops[second]
        if third is not None:
            delta3 = deltas[third]
            gi3 = third // GROUP
            dq = vk_cols[third][:, :1] * dsv[third]
        for t in range(KEYS // TILE):
            rows = pl.ds(t * TILE, TILE)
            if first is not None:
                s = dot(ks[first // GROUP, rows, :], qmt[first])
                if (t + 1) * TILE <= BN:
                    s = s + bias[rows, :]
                s_bufs[parity][rows, :] = s
                peak = jnp.maximum(peak, jnp.max(s.reshape(TILE // 8, 8, BN), axis=0))
            if third is not None:
                p3 = p_bufs[parity][rows, :]
                ds = (dot(vs[gi3, rows, :], gmt_bufs[parity][...]) - delta3).astype(BF) * p3
            if second is not None:
                p = jnp.exp2(s_bufs[1 - parity][rows, :] - top2).astype(BF)
                p_bufs[1 - parity][rows, :] = p
                out = out + dot(vta[second, :, rows], p)
            if third is not None:
                dv_acc[gi3, rows, :] += dot(p3, gm_bufs[parity][...])
                dk_acc[gi3, rows, :] += dot(ds, qm[third])
                dq = dq + dot(k0t[third, :, rows], ds)
        if first is not None:
            tops[first] = jnp.maximum(sv[first], jnp.max(peak, axis=0, keepdims=True))
        if second is not None:
            pv = jnp.exp2(sv[second] - top2)
            inv = 1.0 / (out[HD:HD + 1] + pv)
            attn_h = ((out[:HD] + vv_cols[second][:, :1] * pv) * inv).astype(BF)
            attn_t[second] = attn_h
            g_h = gt[second].astype(F32)
            delta = jnp.sum(g_h * attn_h.astype(F32), axis=0, keepdims=True) * inv
            deltas[second] = delta
            g_n = g_h * inv
            gmt32 = jnp.where(
                row_head == second % GROUP, jnp.concatenate([g_n] * GROUP, axis=0), 0.0
            )
            gmt_bufs[1 - parity][...] = gmt32.astype(BF)
            gm_bufs[1 - parity][...] = gmt32.astype(BF).T
            dsv[second] = pv * (dpv[second] * inv - delta)
            pvn[second] = pv * inv
        if third is not None:
            dq_t[third] = (dq * SCALE).astype(BF)

    step(0, None, None, 0)
    step(1, 0, None, 1)

    @pl.loop(1, HEADS // 2)
    def _(pair):
        h = 2 * pair
        step(h, h - 1, h - 2, 0)
        step(h + 1, h, h - 1, 1)

    step(None, HEADS - 1, HEADS - 2, 0)
    step(None, None, HEADS - 1, 1)

    at = attn_t[...].reshape(D, BN)
    attn = at.T
    layer_ref[...] = (x.astype(F32) + dot(attn, wo)).astype(BF)
    dqt = dq_t[...].reshape(D, BN)
    dqm = dqt.T

    grad_query = dot(xt[0], dqm)
    grad_output = dot(at, cot)
    keep = diag[:HEADS]
    dsv_all = dsv[...].reshape(HEADS, BN)
    pvn_all = pvn[...].reshape(HEADS, BN)
    vkey = jnp.sum(jnp.where(keep, dot(dsv_all.astype(BF), qs), 0.0), axis=0, keepdims=True) * LN2
    vvalue = jnp.sum(jnp.where(keep, dot(pvn_all.astype(BF), g), 0.0), axis=0, keepdims=True)
    vn_col = jnp.broadcast_to(vn_ref[...].astype(F32), (128, D)).T[:, :1]
    grad_key = vn_col * vkey
    grad_value = vn_col * vvalue
    backs = (None, b0_ref, b1_ref, b2_ref, b3_ref)
    for c in range(CHUNKS):
        rows = slice(c * BN, (c + 1) * BN)
        dk = jnp.concatenate([dk_acc[0, rows, :], dk_acc[1, rows, :]], axis=1) * LN2
        dv = jnp.concatenate([dv_acc[0, rows, :], dv_acc[1, rows, :]], axis=1)
        if c:
            tail = parts[c][BN:, :].astype(F32)
            live = row_no < tail[0:1, 0:1] + 256.0 * tail[1:2, 0:1]
            dk = jnp.where(live, dk, 0.0)
            dv = jnp.where(live, dv, 0.0)
        dk = dk.astype(BF)
        dv = dv.astype(BF)
        grad_key = grad_key + dot(xt[c], dk)
        grad_value = grad_value + dot(xt[c], dv)
        back = dot_nt(dk, wk) + dot_nt(dv, wv)
        if c:
            backs[c][...] = back.astype(BF)
        else:
            own_ref[...] = back + dot_nt(dqm, wq) + cot.astype(F32)
    virt = dot_nt_exact(jnp.broadcast_to(vkey, (8, D)), wk) + dot_nt_exact(
        jnp.broadcast_to(vvalue, (8, D)), wv
    )
    high = virt.astype(BF).astype(F32)
    rest = virt - high
    extra = jnp.concatenate(
        [high[:1, :128], high[:1, 128:], rest[:1, :128], rest[:1, 128:], jnp.zeros((4, 128), F32)], axis=0
    )
    extra = jnp.broadcast_to(extra[None], (32, 8, 128))
    for n, grad in enumerate((grad_query, grad_key, grad_value, grad_output)):
        for j in range(2):
            tiles = grad[:, j * 128:(j + 1) * 128].reshape(32, 8, 128)
            weight_ref[n * 32:(n + 1) * 32, j] = jnp.concatenate([tiles, extra], axis=1).astype(BF)


def attend(count, x, partners, wq, wk, wv, wo, vn, cot, mask):
    vmem = pl.BlockSpec(memory_space=pltpu.VMEM)
    sds = jax.ShapeDtypeStruct
    return pl.pallas_call(
        attend_kernel,
        out_shape=(
            sds((BN, D), BF), sds((BN, D), F32), sds((BN, D), BF), sds((BN, D), BF),
            sds((BN, D), BF), sds((BN, D), BF), sds((128, 2, 16, 128), BF),
        ),
        in_specs=[pl.BlockSpec(memory_space=pltpu.SMEM)] + [vmem] * 12,
        out_specs=[vmem] * 7,
        scratch_shapes=[
            pltpu.VMEM((HEADS, 128, BN), BF),
            pltpu.VMEM((HEADS, BN, 128), BF),
            pltpu.VMEM((HEADS, HD, BN), BF),
            pltpu.VMEM((2, KEYS, 128), BF),
            pltpu.VMEM((2, KEYS, 128), BF),
            pltpu.VMEM((HEADS, HD + 16, KEYS), BF),
            pltpu.VMEM((HEADS, HD, KEYS), BF),
            pltpu.VMEM((CHUNKS, D, BN), BF),
            pltpu.VMEM((BN, BN), F32),
            pltpu.VMEM((KEYS, BN), F32),
            pltpu.VMEM((KEYS, BN), F32),
            pltpu.VMEM((KEYS, BN), BF),
            pltpu.VMEM((KEYS, BN), BF),
            pltpu.VMEM((128, BN), BF),
            pltpu.VMEM((128, BN), BF),
            pltpu.VMEM((BN, 128), BF),
            pltpu.VMEM((BN, 128), BF),
            pltpu.VMEM((2, KEYS, 128), F32),
            pltpu.VMEM((2, KEYS, 128), F32),
            pltpu.VMEM((HEADS, HD, BN), BF),
            pltpu.VMEM((HEADS, HD, BN), BF),
            pltpu.VMEM((HEADS, 1, BN), F32),
            pltpu.VMEM((HEADS, 1, BN), F32),
            pltpu.VMEM((HEADS, 1, BN), F32),
            pltpu.VMEM((HEADS, 1, BN), F32),
            pltpu.VMEM((HEADS, 1, BN), F32),
            pltpu.VMEM((HEADS, 1, BN), F32),
            pltpu.VMEM((HEADS, HD, 128), F32),
            pltpu.VMEM((HEADS, HD, 128), F32),
        ],
        compiler_params=pltpu.CompilerParams(vmem_limit_bytes=56 * 1024 * 1024),
        cost_estimate=pl.CostEstimate(flops=8 * 10**9, bytes_accessed=4 * 10**6, transcendentals=10**7),
        name="attend",
    )(count, x, *partners, wq, wk, wv, wo, vn, cot, mask)


def finish_kernel(
    flags_ref, own_ref, near_ref, far_ref, low_ref, high_ref, mine_ref, given_ref,
    out_ref, *grad_refs,
):
    total = own_ref[...] + near_ref[...].astype(F32) + far_ref[...].astype(F32)
    total = total + jnp.where(flags_ref[0] != 0, 0.0, low_ref[...].astype(F32))
    total = total + jnp.where(flags_ref[1] != 0, 0.0, high_ref[...].astype(F32))
    out_ref[...] = total.astype(BF)
    mine, given = mine_ref[...].astype(F32), given_ref[...].astype(F32)
    left = jnp.where(flags_ref[2] == 0, mine, given).reshape(4, D, 128)
    right = jnp.where(flags_ref[2] == 0, given, mine).reshape(4, D, 128)
    for n, grad_ref in enumerate(grad_refs):
        grad_ref[:, :128] = left[n]
        grad_ref[:, 128:] = right[n]


def finish(flags, own, near, far, low, high, mine, given):
    vmem = pl.BlockSpec(memory_space=pltpu.VMEM)
    return pl.pallas_call(
        finish_kernel,
        out_shape=[jax.ShapeDtypeStruct((BN, D), BF)] + [jax.ShapeDtypeStruct((D, D), F32)] * 4,
        in_specs=[pl.BlockSpec(memory_space=pltpu.SMEM)] + [vmem] * 7,
        out_specs=[vmem] * 5,
        cost_estimate=pl.CostEstimate(flops=10**6, bytes_accessed=4 * 10**6, transcendentals=0),
        name="finish",
    )(flags, own, near, far, low, high, mine, given)


def exchange(array, distance):
    return lax.ppermute(array, "blk", [(i, i ^ distance) for i in range(lax.axis_size("blk"))])


def exchange_by(array, step):
    near_bits = DISTANT - 1
    steps = [d for d in range(1, lax.axis_size("blk")) if not d & DISTANT]
    branches = [functools.partial(exchange, distance=d) for d in steps]
    place = (step // (2 * DISTANT)) * DISTANT + (step & near_bits)
    return lax.switch(place - 1, branches, array)


def body(
    features, w_query, key_weight, value_weight, w_output, virtual_node, cotangent, local_mask,
    counts, shifts,
):
    largest = lax.axis_size("blk") - 1
    low = jnp.min(jnp.where(shifts == 1, largest + 1, shifts))
    high = jnp.max(jnp.where(shifts == largest, 0, shifts))
    own = counts[0]
    halves = jnp.stack([own & 255, own >> 8]).astype(BF)
    tail = jnp.zeros((SENT - BN, D), BF).at[:2].set(jnp.broadcast_to(halves[:, None], (2, D)))
    sent = jnp.concatenate([features, tail], axis=0)
    far_copy, near_copy = exchange(sent, largest), exchange(sent, 1)
    low_far, high_far = low & DISTANT != 0, high & DISTANT != 0
    low_step = jnp.where(low_far, low ^ largest, low)
    high_step = jnp.where(high_far, high ^ largest, high)
    partners = [
        far_copy, near_copy,
        exchange_by(jnp.where(low_far, far_copy, sent), low_step),
        exchange_by(jnp.where(high_far, far_copy, sent), high_step),
    ]
    layer_out, own_grad, back_far, back_near, back_low, back_high, weights = attend(
        counts, features, partners, w_query, key_weight, value_weight, w_output,
        virtual_node[None, :], cotangent, local_mask,
    )
    everyone = ("blk", "sub")
    count_sub = lax.axis_size("sub")
    devices = lax.axis_size("blk") * count_sub
    same_core = [[i for i in range(devices) if i % 2 == core] for core in range(2)]
    siblings = [(i, i ^ 1) for i in range(count_sub)]

    scattered = lax.all_to_all(weights.reshape(devices, 16, 128), everyone, 0, 0)
    near = exchange(back_near, 1)
    low_part = exchange_by(back_low, low_step)
    high_part = exchange_by(back_high, high_step)
    scattered, low_part, high_part, near = lax.optimization_barrier(
        (scattered, low_part, high_part, near)
    )
    onward = (
        back_far.astype(F32)
        + jnp.where(low_far, low_part.astype(F32), 0.0)
        + jnp.where(high_far, high_part.astype(F32), 0.0)
    ).astype(BF)
    onward, scattered = lax.optimization_barrier((onward, scattered))
    far = exchange(onward, largest)
    chunk = jnp.sum(scattered.astype(F32), axis=0)
    grad_virtual = (chunk[8:10] + chunk[10:12]).reshape(D)

    def gather(tiles):
        summed = lax.all_to_all(tiles, everyone, 0, 0, axis_index_groups=same_core)
        return summed, lax.ppermute(summed, "sub", siblings)

    summed, given = lax.cond(
        shifts[0] > 0, gather, lambda tiles: (tiles, tiles),
        jnp.broadcast_to(chunk[:8].astype(BF), (devices // 2, 8, 128)),
    )
    core = lax.axis_index("sub") % 2
    flags = jnp.stack([low_far.astype(jnp.int32), high_far.astype(jnp.int32), core.astype(jnp.int32)])
    total, *grads = finish(flags, own_grad, near, far, low_part, high_part, summed, given)
    return (
        layer_out, total, grads[0], grads[1], grads[2], grads[3], grad_virtual,
    )


def solution(mesh):
    return jax.shard_map(
        body,
        mesh=mesh,
        in_specs=(
            P(("blk", "sub"), None), P(), P(), P(), P(), P(), P(("blk", "sub"), None),
            P(("blk", "sub"), None), P(("blk", "sub")), P(),
        ),
        out_specs=(P(("blk", "sub"), None), P(("blk", "sub"), None), P(), P(), P(), P(), P()),
        check_vma=False,
    )
```

```python
import functools
import math

import jax
import jax.numpy as jnp
from jax import lax
from jax.experimental import pallas as pl
from jax.experimental.pallas import tpu as pltpu
from jax.sharding import PartitionSpec as P

D = 256
HEADS = 8
HD = D // HEADS
GROUP = 128 // HD
CHUNKS = 5
BN = 512
KEYS = CHUNKS * BN
SENT = BN + 16
NEG_FILL = -1000000000.0
SCALE = 1.0 / math.sqrt(HD)
LOG2E = 1.0 / math.log(2.0)
LN2 = math.log(2.0)
TILE = 512
HALF = BN // 2
DISTANT = 4
BF = jnp.bfloat16
F32 = jnp.float32


def dot(a, b):
    return jnp.dot(a, b, preferred_element_type=F32)


def dot_nt(a, b):
    return lax.dot_general(a, b, (((1,), (1,)), ((), ())), preferred_element_type=F32)


def dot_nt_exact(a, b):
    return lax.dot_general(
        a, b.astype(F32), (((1,), (1,)), ((), ())), precision=lax.Precision.HIGHEST,
        preferred_element_type=F32,
    )


def prepare_kernel(
    count_ref, x_ref, wq_ref, wk_ref, wv_ref, wo_ref, vn_ref, cot_ref, mask_ref,
    qmt, qm, gt, qs_ref, g_ref, bias, sv, dpv,
):
    vn = jnp.broadcast_to(vn_ref[...], (16, D))
    vk = dot(vn, wk_ref[...]).astype(BF)
    vv = dot(vn, wv_ref[...]).astype(BF)

    qs = (dot(x_ref[...], wq_ref[...]) * (SCALE * LOG2E)).astype(BF)
    qs_ref[...] = qs
    qt = qs.T
    g = dot_nt(cot_ref[...], wo_ref[...]).astype(BF)
    g_ref[...] = g
    gt_all = g.T
    gt[...] = gt_all.reshape(HEADS, HD, BN)
    qmt[...] = jnp.zeros_like(qmt)
    lane_head = lax.broadcasted_iota(jnp.int32, (BN, 128), 1) // HD
    for h in range(HEADS):
        r = h % GROUP
        lo = (h // GROUP) * 128
        qmt[h, r * HD:(r + 1) * HD, :] = qt[h * HD:(h + 1) * HD]
        qm[h] = jnp.where(lane_head == r, qs[:, lo:lo + 128], jnp.zeros((), BF))

    head_of = lax.broadcasted_iota(jnp.int32, (16, D), 1) // HD
    diag = head_of == lax.broadcasted_iota(jnp.int32, (16, D), 0)
    sv[...] = dot(jnp.where(diag, vk, jnp.zeros((), BF)), qt)[:HEADS].reshape(HEADS, 1, BN) + math.log2(BN)
    dpv[...] = dot(jnp.where(diag, vv, jnp.zeros((), BF)), gt_all)[:HEADS].reshape(HEADS, 1, BN)

    key_row = lax.broadcasted_iota(jnp.int32, (BN, BN), 0)
    query_col = lax.broadcasted_iota(jnp.int32, (BN, BN), 1)
    linked = jnp.where(mask_ref[...] != 0, 1.0, 0.0).astype(BF).T.astype(F32)
    ok = ((linked != 0.0) | (key_row == query_col)) & (key_row < count_ref[0])
    bias[...] = jnp.where(ok, 0.0, NEG_FILL).astype(BF)


def prepare(count, x, wq, wk, wv, wo, vn, cot, mask):
    vmem = pl.BlockSpec(memory_space=pltpu.VMEM)
    sds = jax.ShapeDtypeStruct
    return pl.pallas_call(
        prepare_kernel,
        out_shape=(
            sds((HEADS, 128, BN), BF), sds((HEADS, BN, 128), BF), sds((HEADS, HD, BN), BF),
            sds((BN, D), BF), sds((BN, D), BF), sds((BN, BN), BF),
            sds((HEADS, 1, BN), F32), sds((HEADS, 1, BN), F32),
        ),
        in_specs=[pl.BlockSpec(memory_space=pltpu.SMEM)] + [vmem] * 8,
        out_specs=[vmem] * 8,
        compiler_params=pltpu.CompilerParams(vmem_limit_bytes=32 * 1024 * 1024),
        cost_estimate=pl.CostEstimate(flops=2 * 10**9, bytes_accessed=6 * 10**6, transcendentals=0),
        name="prepare",
    )(count, x, wq, wk, wv, wo, vn, cot, mask)


def attend_kernel(
    x_ref, p0_ref, p1_ref, p2_ref, p3_ref, wk_ref, wv_ref, vn_ref, cot_ref,
    qmt, qm, gt, qs_ref, g_ref, bias, sv, dpv, wk_t_ref, wv_t_ref,
    at_ref, dqm_ref, dk0_ref, dv0_ref, b0_ref, b1_ref, b2_ref, b3_ref, weight_ref,
    ks, vs, vta, k0t, xt, s_even, s_odd, p_even, p_odd, ds_even, ds_odd, gmt_even, gmt_odd,
    gm_even, gm_odd, dk_acc, dv_acc, attn_t, dq_t, dsv, pvn, tops, deltas, vk_cols, vv_cols,
):
    parts = (x_ref, p0_ref, p1_ref, p2_ref, p3_ref)
    wk, wv = wk_ref[...], wv_ref[...]
    vn = jnp.broadcast_to(vn_ref[...], (16, D))
    vk = dot(vn, wk).astype(BF)
    vv = dot(vn, wv).astype(BF)
    head_of = lax.broadcasted_iota(jnp.int32, (16, D), 1) // HD
    diag = head_of == lax.broadcasted_iota(jnp.int32, (16, D), 0)
    vk_cols[...] = jnp.broadcast_to(vk[:1].astype(F32), (128, D)).T.reshape(HEADS, HD, 128)
    vv_cols[...] = jnp.broadcast_to(vv[:1].astype(F32), (128, D)).T.reshape(HEADS, HD, 128)

    row_no = lax.broadcasted_iota(jnp.int32, (BN, D), 0).astype(F32)
    lane_no = lax.broadcasted_iota(jnp.int32, (16, BN), 1).astype(F32)
    for c in range(CHUNKS):
        rows = slice(c * BN, (c + 1) * BN)
        xc = parts[c][:BN, :]
        k32 = dot(xc, wk)
        v32 = dot(xc, wv)
        k = k32.astype(BF)
        live_row = jnp.ones((16, BN), BF)
        if c:
            tail = parts[c][BN:, :].astype(F32)
            count = tail[0:1, 0:1] + 256.0 * tail[1:2, 0:1]
            live = row_no < count
            k = jnp.where(live, k, jnp.broadcast_to(vk[:1], (BN, D)))
            k32 = jnp.where(live, k32, 0.0)
            v32 = jnp.where(live, v32, 0.0)
            live_row = jnp.where(lane_no < count, 1.0, 0.0).astype(BF)
        v = v32.astype(BF)
        for gi in range(2):
            ks[gi, rows, :] = k[:, gi * 128:(gi + 1) * 128]
            vs[gi, rows, :] = v[:, gi * 128:(gi + 1) * 128]
        vt = v.T
        k0t[:, :, rows] = k32.astype(BF).T.reshape(HEADS, HD, BN)
        xt[c] = xc.T
        for h in range(HEADS):
            vta[h, :HD, rows] = vt[h * HD:(h + 1) * HD]
            vta[h, HD:, rows] = live_row

    dk_acc[...] = jnp.zeros_like(dk_acc)
    dv_acc[...] = jnp.zeros_like(dv_acc)
    row_head = lax.broadcasted_iota(jnp.int32, (128, BN), 0) // HD
    s_bufs, p_bufs = (s_even, s_odd), (p_even, p_odd)
    gmt_bufs, gm_bufs = (gmt_even, gmt_odd), (gm_even, gm_odd)

    halves = [slice(0, HALF), slice(HALF, BN)]

    def step(first, second, third, parity):
        peaks = [jnp.full((8, HALF), -jnp.inf, F32) for _ in halves]
        outs = [jnp.zeros((HD + 16, HALF), F32) for _ in halves]
        if second is not None:
            top2 = tops[second]
        if third is not None:
            delta3 = deltas[third]
            gi3 = third // GROUP
            dq = vk_cols[third][:, :1] * dsv[third]
        for t in range(KEYS // TILE):
            rows = pl.ds(t * TILE, TILE)
            ds_buf = (ds_even, ds_odd)[t % 2]
            for n, cols in enumerate(halves):
                if first is not None:
                    s = dot(ks[first // GROUP, rows, :], qmt[first, :, cols])
                    if (t + 1) * TILE <= BN:
                        s = s + bias[rows, cols].astype(F32)
                    s_bufs[parity][rows, cols] = s
                    peaks[n] = jnp.maximum(peaks[n], jnp.max(s.reshape(TILE // 8, 8, HALF), axis=0))
                if third is not None:
                    dp = dot(vs[gi3, rows, :], gmt_bufs[parity][:, cols]) - delta3[:, cols]
                    ds_buf[:, cols] = dp.astype(BF) * p_bufs[parity][rows, cols]
                if second is not None:
                    p = jnp.exp2(s_bufs[1 - parity][rows, cols] - top2[:, cols]).astype(BF)
                    p_bufs[1 - parity][rows, cols] = p
                    outs[n] = outs[n] + dot(vta[second, :, rows], p)
            if third is not None:
                ds = ds_buf[...]
                dv_acc[gi3, rows, :] += dot(p_bufs[parity][rows, :], gm_bufs[parity][...])
                dk_acc[gi3, rows, :] += dot(ds, qm[third])
                dq = dq + dot(k0t[third, :, rows], ds)
        peak = jnp.concatenate(peaks, axis=1)
        out = jnp.concatenate(outs, axis=1)
        if first is not None:
            tops[first] = jnp.maximum(sv[first], jnp.max(peak, axis=0, keepdims=True))
        if second is not None:
            pv = jnp.exp2(sv[second] - top2)
            inv = 1.0 / (out[HD:HD + 1] + pv)
            attn_h = ((out[:HD] + vv_cols[second][:, :1] * pv) * inv).astype(BF)
            attn_t[second] = attn_h
            g_h = gt[second].astype(F32)
            delta = jnp.sum(g_h * attn_h.astype(F32), axis=0, keepdims=True) * inv
            deltas[second] = delta
            g_n = g_h * inv
            gmt32 = jnp.where(
                row_head == second % GROUP, jnp.concatenate([g_n] * GROUP, axis=0), 0.0
            )
            gmt_bufs[1 - parity][...] = gmt32.astype(BF)
            gm_bufs[1 - parity][...] = gmt32.astype(BF).T
            dsv[second] = pv * (dpv[second] * inv - delta)
            pvn[second] = pv * inv
        if third is not None:
            dq_t[third] = (dq * SCALE).astype(BF)

    step(0, None, None, 0)
    step(1, 0, None, 1)

    @pl.loop(1, HEADS // 2)
    def _(pair):
        h = 2 * pair
        step(h, h - 1, h - 2, 0)
        step(h + 1, h, h - 1, 1)

    step(None, HEADS - 1, HEADS - 2, 0)
    step(None, None, HEADS - 1, 1)

    at = attn_t[...].reshape(D, BN)
    at_ref[...] = at
    dqm = dq_t[...].reshape(D, BN).T
    dqm_ref[...] = dqm

    grad_query = dot(xt[0], dqm)
    grad_output = dot(at, cot_ref[...])
    keep = diag[:HEADS]
    dsv_all = dsv[...].reshape(HEADS, BN)
    pvn_all = pvn[...].reshape(HEADS, BN)
    vkey = jnp.sum(jnp.where(keep, dot(dsv_all.astype(BF), qs_ref[...]), 0.0), axis=0, keepdims=True) * LN2
    vvalue = jnp.sum(jnp.where(keep, dot(pvn_all.astype(BF), g_ref[...]), 0.0), axis=0, keepdims=True)
    vn_col = jnp.broadcast_to(vn_ref[...].astype(F32), (128, D)).T[:, :1]
    grad_key = vn_col * vkey
    grad_value = vn_col * vvalue
    backs = (None, b0_ref, b1_ref, b2_ref, b3_ref)
    for c in range(CHUNKS):
        rows = slice(c * BN, (c + 1) * BN)
        dk = jnp.concatenate([dk_acc[0, rows, :], dk_acc[1, rows, :]], axis=1) * LN2
        dv = jnp.concatenate([dv_acc[0, rows, :], dv_acc[1, rows, :]], axis=1)
        if c:
            tail = parts[c][BN:, :].astype(F32)
            live = row_no < tail[0:1, 0:1] + 256.0 * tail[1:2, 0:1]
            dk = jnp.where(live, dk, 0.0)
            dv = jnp.where(live, dv, 0.0)
        dk = dk.astype(BF)
        dv = dv.astype(BF)
        grad_key = grad_key + dot(xt[c], dk)
        grad_value = grad_value + dot(xt[c], dv)
        if c:
            backs[c][...] = (dot(dk, wk_t_ref[...]) + dot(dv, wv_t_ref[...])).astype(BF)
        else:
            dk0_ref[...] = dk
            dv0_ref[...] = dv
    virt = dot_nt_exact(jnp.broadcast_to(vkey, (8, D)), wk) + dot_nt_exact(
        jnp.broadcast_to(vvalue, (8, D)), wv
    )
    high = virt.astype(BF).astype(F32)
    rest = virt - high
    extra = jnp.concatenate(
        [high[:1, :128], high[:1, 128:], rest[:1, :128], rest[:1, 128:], jnp.zeros((4, 128), F32)], axis=0
    )
    extra = jnp.broadcast_to(extra[None], (32, 8, 128))
    for n, grad in enumerate((grad_query, grad_key, grad_value, grad_output)):
        for j in range(2):
            tiles = grad[:, j * 128:(j + 1) * 128].reshape(32, 8, 128)
            weight_ref[n * 32:(n + 1) * 32, j] = jnp.concatenate([tiles, extra], axis=1).astype(BF)


def attend(x, partners, wk, wv, vn, cot, prepared):
    vmem = pl.BlockSpec(memory_space=pltpu.VMEM)
    sds = jax.ShapeDtypeStruct
    return pl.pallas_call(
        attend_kernel,
        out_shape=[sds((D, BN), BF)] + [sds((BN, D), BF)] * 7 + [sds((128, 2, 16, 128), BF)],
        in_specs=[vmem] * 19,
        out_specs=[vmem] * 9,
        scratch_shapes=[
            pltpu.VMEM((2, KEYS, 128), BF),
            pltpu.VMEM((2, KEYS, 128), BF),
            pltpu.VMEM((HEADS, HD + 16, KEYS), BF),
            pltpu.VMEM((HEADS, HD, KEYS), BF),
            pltpu.VMEM((CHUNKS, D, BN), BF),
            pltpu.VMEM((KEYS, BN), F32),
            pltpu.VMEM((KEYS, BN), F32),
            pltpu.VMEM((KEYS, BN), BF),
            pltpu.VMEM((KEYS, BN), BF),
            pltpu.VMEM((TILE, BN), BF),
            pltpu.VMEM((TILE, BN), BF),
            pltpu.VMEM((128, BN), BF),
            pltpu.VMEM((128, BN), BF),
            pltpu.VMEM((BN, 128), BF),
            pltpu.VMEM((BN, 128), BF),
            pltpu.VMEM((2, KEYS, 128), F32),
            pltpu.VMEM((2, KEYS, 128), F32),
            pltpu.VMEM((HEADS, HD, BN), BF),
            pltpu.VMEM((HEADS, HD, BN), BF),
            pltpu.VMEM((HEADS, 1, BN), F32),
            pltpu.VMEM((HEADS, 1, BN), F32),
            pltpu.VMEM((HEADS, 1, BN), F32),
            pltpu.VMEM((HEADS, 1, BN), F32),
            pltpu.VMEM((HEADS, HD, 128), F32),
            pltpu.VMEM((HEADS, HD, 128), F32),
        ],
        compiler_params=pltpu.CompilerParams(vmem_limit_bytes=56 * 1024 * 1024),
        cost_estimate=pl.CostEstimate(flops=8 * 10**9, bytes_accessed=4 * 10**6, transcendentals=10**7),
        name="attend",
    )(x, *partners, wk, wv, vn, cot, *prepared, wk.T, wv.T)


def late_kernel(
    flags_ref, x_ref, cot_ref, at_ref, dqm_ref, dk_ref, dv_ref, near_ref, low_ref, high_ref,
    wq_ref, wk_ref, wv_ref, wo_ref, layer_ref, part_ref,
):
    layer_ref[...] = (x_ref[...].astype(F32) + dot(at_ref[...].T, wo_ref[...])).astype(BF)
    part = cot_ref[...].astype(F32) + near_ref[...].astype(F32)
    part = part + dot_nt(dqm_ref[...], wq_ref[...])
    part = part + dot_nt(dk_ref[...], wk_ref[...]) + dot_nt(dv_ref[...], wv_ref[...])
    part = part + jnp.where(flags_ref[0] != 0, 0.0, low_ref[...].astype(F32))
    part_ref[...] = part + jnp.where(flags_ref[1] != 0, 0.0, high_ref[...].astype(F32))


def late(*operands):
    vmem = pl.BlockSpec(memory_space=pltpu.VMEM)
    return pl.pallas_call(
        late_kernel,
        out_shape=(jax.ShapeDtypeStruct((BN, D), BF), jax.ShapeDtypeStruct((BN, D), F32)),
        in_specs=[pl.BlockSpec(memory_space=pltpu.SMEM)] + [vmem] * 13,
        out_specs=[vmem] * 2,
        cost_estimate=pl.CostEstimate(flops=10**9, bytes_accessed=4 * 10**6, transcendentals=0),
        name="late",
    )(*operands)


def finish_kernel(core_ref, part_ref, far_ref, mine_ref, given_ref, out_ref, *grad_refs):
    out_ref[...] = (part_ref[...] + far_ref[...].astype(F32)).astype(BF)
    mine, given = mine_ref[...].astype(F32), given_ref[...].astype(F32)
    left = jnp.where(core_ref[0] == 0, mine, given).reshape(4, D, 128)
    right = jnp.where(core_ref[0] == 0, given, mine).reshape(4, D, 128)
    for n, grad_ref in enumerate(grad_refs):
        grad_ref[:, :128] = left[n]
        grad_ref[:, 128:] = right[n]


def finish(core, part, far, mine, given):
    vmem = pl.BlockSpec(memory_space=pltpu.VMEM)
    return pl.pallas_call(
        finish_kernel,
        out_shape=[jax.ShapeDtypeStruct((BN, D), BF)] + [jax.ShapeDtypeStruct((D, D), F32)] * 4,
        in_specs=[pl.BlockSpec(memory_space=pltpu.SMEM)] + [vmem] * 4,
        out_specs=[vmem] * 5,
        cost_estimate=pl.CostEstimate(flops=10**6, bytes_accessed=4 * 10**6, transcendentals=0),
        name="finish",
    )(core, part, far, mine, given)


def exchange(array, distance):
    return lax.ppermute(array, "blk", [(i, i ^ distance) for i in range(lax.axis_size("blk"))])


def exchange_by(array, step):
    near_bits = DISTANT - 1
    steps = [d for d in range(1, lax.axis_size("blk")) if not d & DISTANT]
    branches = [functools.partial(exchange, distance=d) for d in steps]
    place = (step // (2 * DISTANT)) * DISTANT + (step & near_bits)
    return lax.switch(place - 1, branches, array)


def body(
    features, w_query, key_weight, value_weight, w_output, virtual_node, cotangent, local_mask,
    counts, shifts,
):
    largest = lax.axis_size("blk") - 1
    low = jnp.min(jnp.where(shifts == 1, largest + 1, shifts))
    high = jnp.max(jnp.where(shifts == largest, 0, shifts))
    own = counts[0]
    halves = jnp.stack([own & 255, own >> 8]).astype(BF)
    tail = jnp.zeros((SENT - BN, D), BF).at[:2].set(jnp.broadcast_to(halves[:, None], (2, D)))
    sent = jnp.concatenate([features, tail], axis=0)
    far_copy, near_copy = exchange(sent, largest), exchange(sent, 1)
    low_far, high_far = low & DISTANT != 0, high & DISTANT != 0
    low_step = jnp.where(low_far, low ^ largest, low)
    high_step = jnp.where(high_far, high ^ largest, high)
    partners = [
        far_copy, near_copy,
        exchange_by(jnp.where(low_far, far_copy, sent), low_step),
        exchange_by(jnp.where(high_far, far_copy, sent), high_step),
    ]
    vn = virtual_node[None, :]
    prepared = prepare(
        counts, features, w_query, key_weight, value_weight, w_output, vn, cotangent, local_mask
    )
    attn_t, dquery, dkey, dvalue, back_far, back_near, back_low, back_high, weights = attend(
        features, partners, key_weight, value_weight, vn, cotangent, prepared
    )
    everyone = ("blk", "sub")
    count_sub = lax.axis_size("sub")
    devices = lax.axis_size("blk") * count_sub
    same_core = [[i for i in range(devices) if i % 2 == core] for core in range(2)]
    siblings = [(i, i ^ 1) for i in range(count_sub)]

    scattered = lax.all_to_all(weights.reshape(devices, 16, 128), everyone, 0, 0)
    near = exchange(back_near, 1)
    low_part = exchange_by(back_low, low_step)
    high_part = exchange_by(back_high, high_step)
    scattered, low_part, high_part, near = lax.optimization_barrier(
        (scattered, low_part, high_part, near)
    )
    onward = (
        back_far.astype(F32)
        + jnp.where(low_far, low_part.astype(F32), 0.0)
        + jnp.where(high_far, high_part.astype(F32), 0.0)
    ).astype(BF)
    onward, scattered = lax.optimization_barrier((onward, scattered))
    far = exchange(onward, largest)
    chunk = jnp.sum(scattered.astype(F32), axis=0)
    grad_virtual = (chunk[8:10] + chunk[10:12]).reshape(D)

    flags = jnp.stack([low_far, high_far]).astype(jnp.int32)

    def gather(tiles, *operands):
        summed = lax.all_to_all(tiles, everyone, 0, 0, axis_index_groups=same_core)
        layer_out, part = late(*operands)
        return summed, lax.ppermute(summed, "sub", siblings), layer_out, part

    def idle(tiles, *operands):
        return tiles, tiles, operands[1], jnp.zeros((BN, D), F32)

    summed, given, layer_out, part = lax.cond(
        shifts[0] > 0, gather, idle,
        jnp.broadcast_to(chunk[:8].astype(BF), (devices // 2, 8, 128)),
        flags, features, cotangent, attn_t, dquery, dkey, dvalue, near, low_part, high_part,
        w_query, key_weight, value_weight, w_output,
    )
    core = (lax.axis_index("sub") % 2).astype(jnp.int32)[None]
    total, *grads = finish(core, part, far, summed, given)
    return (
        layer_out, total, grads[0], grads[1], grads[2], grads[3], grad_virtual,
    )


def solution(mesh):
    return jax.shard_map(
        body,
        mesh=mesh,
        in_specs=(
            P(("blk", "sub"), None), P(), P(), P(), P(), P(), P(("blk", "sub"), None),
            P(("blk", "sub"), None), P(("blk", "sub")), P(),
        ),
        out_specs=(P(("blk", "sub"), None), P(("blk", "sub"), None), P(), P(), P(), P(), P()),
        check_vma=False,
    )
```

```python
import functools
import math

import jax
import jax.numpy as jnp
from jax import lax
from jax.experimental import pallas as pl
from jax.experimental.pallas import tpu as pltpu
from jax.sharding import PartitionSpec as P

D = 256
HEADS = 8
HD = D // HEADS
GROUP = 128 // HD
CHUNKS = 5
BN = 512
KEYS = CHUNKS * BN
SENT = BN + 16
NEG_FILL = -1000000000.0
SCALE = 1.0 / math.sqrt(HD)
LOG2E = 1.0 / math.log(2.0)
LN2 = math.log(2.0)
TILE = 512
HALF = BN // 2
DISTANT = 4
BF = jnp.bfloat16
F32 = jnp.float32


def dot(a, b):
    return jnp.dot(a, b, preferred_element_type=F32)


def dot_nt(a, b):
    return lax.dot_general(a, b, (((1,), (1,)), ((), ())), preferred_element_type=F32)


def dot_nt_exact(a, b):
    return lax.dot_general(
        a, b.astype(F32), (((1,), (1,)), ((), ())), precision=lax.Precision.HIGHEST,
        preferred_element_type=F32,
    )


def prepare_kernel(
    count_ref, x_ref, wq_ref, wk_ref, wv_ref, wo_ref, vn_ref, cot_ref, mask_ref,
    qmt, qm, gt, qs_ref, g_ref, bias, sv, dpv,
):
    vn = jnp.broadcast_to(vn_ref[...], (16, D))
    vk = dot(vn, wk_ref[...]).astype(BF)
    vv = dot(vn, wv_ref[...]).astype(BF)

    qs = (dot(x_ref[...], wq_ref[...]) * (SCALE * LOG2E)).astype(BF)
    qs_ref[...] = qs
    qt = qs.T
    g = dot_nt(cot_ref[...], wo_ref[...]).astype(BF)
    g_ref[...] = g
    gt_all = g.T
    gt[...] = gt_all.reshape(HEADS, HD, BN)
    qmt[...] = jnp.zeros_like(qmt)
    lane_head = lax.broadcasted_iota(jnp.int32, (BN, 128), 1) // HD
    for h in range(HEADS):
        r = h % GROUP
        lo = (h // GROUP) * 128
        qmt[h, r * HD:(r + 1) * HD, :] = qt[h * HD:(h + 1) * HD]
        qm[h] = jnp.where(lane_head == r, qs[:, lo:lo + 128], jnp.zeros((), BF))

    head_of = lax.broadcasted_iota(jnp.int32, (16, D), 1) // HD
    diag = head_of == lax.broadcasted_iota(jnp.int32, (16, D), 0)
    sv[...] = dot(jnp.where(diag, vk, jnp.zeros((), BF)), qt)[:HEADS].reshape(HEADS, 1, BN) + math.log2(BN)
    dpv[...] = dot(jnp.where(diag, vv, jnp.zeros((), BF)), gt_all)[:HEADS].reshape(HEADS, 1, BN)

    key_row = lax.broadcasted_iota(jnp.int32, (BN, BN), 0)
    query_col = lax.broadcasted_iota(jnp.int32, (BN, BN), 1)
    linked = jnp.where(mask_ref[...] != 0, 1.0, 0.0).astype(BF).T.astype(F32)
    ok = ((linked != 0.0) | (key_row == query_col)) & (key_row < count_ref[0])
    bias[...] = jnp.where(ok, 0.0, NEG_FILL).astype(BF)


def prepare(count, x, wq, wk, wv, wo, vn, cot, mask):
    vmem = pl.BlockSpec(memory_space=pltpu.VMEM)
    sds = jax.ShapeDtypeStruct
    return pl.pallas_call(
        prepare_kernel,
        out_shape=(
            sds((HEADS, 128, BN), BF), sds((HEADS, BN, 128), BF), sds((HEADS, HD, BN), BF),
            sds((BN, D), BF), sds((BN, D), BF), sds((BN, BN), BF),
            sds((HEADS, 1, BN), F32), sds((HEADS, 1, BN), F32),
        ),
        in_specs=[pl.BlockSpec(memory_space=pltpu.SMEM)] + [vmem] * 8,
        out_specs=[vmem] * 8,
        compiler_params=pltpu.CompilerParams(vmem_limit_bytes=60 * 1024 * 1024),
        cost_estimate=pl.CostEstimate(flops=2 * 10**9, bytes_accessed=6 * 10**6, transcendentals=0),
        name="prepare",
    )(count, x, wq, wk, wv, wo, vn, cot, mask)


def attend_kernel(
    x_ref, p0_ref, p1_ref, p2_ref, p3_ref, wk_ref, wv_ref, vn_ref, cot_ref,
    qmt, qm, gt, qs_ref, g_ref, bias, sv, dpv, wk_t_ref, wv_t_ref,
    at_ref, dqm_ref, dk0_ref, dv0_ref, b0_ref, b1_ref, b2_ref, b3_ref, weight_ref,
    ks, vs, vta, k0t, xt, s_even, s_odd, p_even, p_odd, ds_even, ds_odd, gmt_even, gmt_odd,
    gm_even, gm_odd, dk_acc, dv_acc, attn_t, dq_t, dsv, pvn, tops, deltas, vk_cols, vv_cols,
):
    parts = (x_ref, p0_ref, p1_ref, p2_ref, p3_ref)
    wk, wv = wk_ref[...], wv_ref[...]
    vn = jnp.broadcast_to(vn_ref[...], (16, D))
    vk = dot(vn, wk).astype(BF)
    vv = dot(vn, wv).astype(BF)
    head_of = lax.broadcasted_iota(jnp.int32, (16, D), 1) // HD
    diag = head_of == lax.broadcasted_iota(jnp.int32, (16, D), 0)
    vk_cols[...] = jnp.broadcast_to(vk[:1].astype(F32), (128, D)).T.reshape(HEADS, HD, 128)
    vv_cols[...] = jnp.broadcast_to(vv[:1].astype(F32), (128, D)).T.reshape(HEADS, HD, 128)

    row_no = lax.broadcasted_iota(jnp.int32, (BN, D), 0).astype(F32)
    lane_no = lax.broadcasted_iota(jnp.int32, (16, BN), 1).astype(F32)
    for c in range(CHUNKS):
        rows = slice(c * BN, (c + 1) * BN)
        xc = parts[c][:BN, :]
        k32 = dot(xc, wk)
        v32 = dot(xc, wv)
        k = k32.astype(BF)
        live_row = jnp.ones((16, BN), BF)
        if c:
            tail = parts[c][BN:, :].astype(F32)
            count = tail[0:1, 0:1] + 256.0 * tail[1:2, 0:1]
            live = row_no < count
            k = jnp.where(live, k, jnp.broadcast_to(vk[:1], (BN, D)))
            k32 = jnp.where(live, k32, 0.0)
            v32 = jnp.where(live, v32, 0.0)
            live_row = jnp.where(lane_no < count, 1.0, 0.0).astype(BF)
        v = v32.astype(BF)
        for gi in range(2):
            ks[gi, rows, :] = k[:, gi * 128:(gi + 1) * 128]
            vs[gi, rows, :] = v[:, gi * 128:(gi + 1) * 128]
        vt = v.T
        k0t[:, :, rows] = k32.astype(BF).T.reshape(HEADS, HD, BN)
        xt[c] = xc.T
        for h in range(HEADS):
            vta[h, :HD, rows] = vt[h * HD:(h + 1) * HD]
            vta[h, HD:, rows] = live_row

    dk_acc[...] = jnp.zeros_like(dk_acc)
    dv_acc[...] = jnp.zeros_like(dv_acc)
    row_head = lax.broadcasted_iota(jnp.int32, (128, BN), 0) // HD
    s_bufs, p_bufs = (s_even, s_odd), (p_even, p_odd)
    gmt_bufs, gm_bufs = (gmt_even, gmt_odd), (gm_even, gm_odd)

    halves = [slice(0, HALF), slice(HALF, BN)]

    def step(first, second, third, parity):
        peaks = [jnp.full((8, HALF), -jnp.inf, F32) for _ in halves]
        outs = [jnp.zeros((HD + 16, HALF), F32) for _ in halves]
        if second is not None:
            top2 = tops[second]
        if third is not None:
            delta3 = deltas[third]
            gi3 = third // GROUP
            dq = vk_cols[third][:, :1] * dsv[third]
        for t in range(KEYS // TILE):
            rows = pl.ds(t * TILE, TILE)
            ds_buf = (ds_even, ds_odd)[t % 2]
            for n, cols in enumerate(halves):
                if first is not None:
                    s = dot(ks[first // GROUP, rows, :], qmt[first, :, cols])
                    if (t + 1) * TILE <= BN:
                        s = s + bias[rows, cols].astype(F32)
                    s_bufs[parity][rows, cols] = s
                    peaks[n] = jnp.maximum(peaks[n], jnp.max(s.reshape(TILE // 8, 8, HALF), axis=0))
                if third is not None:
                    dp = dot(vs[gi3, rows, :], gmt_bufs[parity][:, cols]) - delta3[:, cols]
                    ds_buf[:, cols] = dp.astype(BF) * p_bufs[parity][rows, cols]
                if second is not None:
                    p = jnp.exp2(s_bufs[1 - parity][rows, cols] - top2[:, cols]).astype(BF)
                    p_bufs[1 - parity][rows, cols] = p
                    outs[n] = outs[n] + dot(vta[second, :, rows], p)
            if third is not None:
                ds = ds_buf[...]
                dv_acc[gi3, rows, :] += dot(p_bufs[parity][rows, :], gm_bufs[parity][...])
                dk_acc[gi3, rows, :] += dot(ds, qm[third])
                dq = dq + dot(k0t[third, :, rows], ds)
        peak = jnp.concatenate(peaks, axis=1)
        out = jnp.concatenate(outs, axis=1)
        if first is not None:
            tops[first] = jnp.maximum(sv[first], jnp.max(peak, axis=0, keepdims=True))
        if second is not None:
            pv = jnp.exp2(sv[second] - top2)
            inv = 1.0 / (out[HD:HD + 1] + pv)
            attn_h = ((out[:HD] + vv_cols[second][:, :1] * pv) * inv).astype(BF)
            attn_t[second] = attn_h
            g_h = gt[second].astype(F32)
            delta = jnp.sum(g_h * attn_h.astype(F32), axis=0, keepdims=True) * inv
            deltas[second] = delta
            g_n = g_h * inv
            gmt32 = jnp.where(
                row_head == second % GROUP, jnp.concatenate([g_n] * GROUP, axis=0), 0.0
            )
            gmt_bufs[1 - parity][...] = gmt32.astype(BF)
            gm_bufs[1 - parity][...] = gmt32.astype(BF).T
            dsv[second] = pv * (dpv[second] * inv - delta)
            pvn[second] = pv * inv
        if third is not None:
            dq_t[third] = (dq * SCALE).astype(BF)

    step(0, None, None, 0)
    step(1, 0, None, 1)

    @pl.loop(1, HEADS // 2)
    def _(pair):
        h = 2 * pair
        step(h, h - 1, h - 2, 0)
        step(h + 1, h, h - 1, 1)

    step(None, HEADS - 1, HEADS - 2, 0)
    step(None, None, HEADS - 1, 1)

    at = attn_t[...].reshape(D, BN)
    at_ref[...] = at
    dqm = dq_t[...].reshape(D, BN).T
    dqm_ref[...] = dqm

    grad_query = dot(xt[0], dqm)
    grad_output = dot(at, cot_ref[...])
    keep = diag[:HEADS]
    dsv_all = dsv[...].reshape(HEADS, BN)
    pvn_all = pvn[...].reshape(HEADS, BN)
    vkey = jnp.sum(jnp.where(keep, dot(dsv_all.astype(BF), qs_ref[...]), 0.0), axis=0, keepdims=True) * LN2
    vvalue = jnp.sum(jnp.where(keep, dot(pvn_all.astype(BF), g_ref[...]), 0.0), axis=0, keepdims=True)
    vn_col = jnp.broadcast_to(vn_ref[...].astype(F32), (128, D)).T[:, :1]
    grad_key = vn_col * vkey
    grad_value = vn_col * vvalue
    backs = (None, b0_ref, b1_ref, b2_ref, b3_ref)
    for c in range(CHUNKS):
        rows = slice(c * BN, (c + 1) * BN)
        dk = jnp.concatenate([dk_acc[0, rows, :], dk_acc[1, rows, :]], axis=1) * LN2
        dv = jnp.concatenate([dv_acc[0, rows, :], dv_acc[1, rows, :]], axis=1)
        if c:
            tail = parts[c][BN:, :].astype(F32)
            live = row_no < tail[0:1, 0:1] + 256.0 * tail[1:2, 0:1]
            dk = jnp.where(live, dk, 0.0)
            dv = jnp.where(live, dv, 0.0)
        dk = dk.astype(BF)
        dv = dv.astype(BF)
        grad_key = grad_key + dot(xt[c], dk)
        grad_value = grad_value + dot(xt[c], dv)
        if c:
            backs[c][...] = (dot(dk, wk_t_ref[...]) + dot(dv, wv_t_ref[...])).astype(BF)
        else:
            dk0_ref[...] = dk
            dv0_ref[...] = dv
    virt = dot_nt_exact(jnp.broadcast_to(vkey, (8, D)), wk) + dot_nt_exact(
        jnp.broadcast_to(vvalue, (8, D)), wv
    )
    high = virt.astype(BF).astype(F32)
    rest = virt - high
    extra = jnp.concatenate(
        [high[:1, :128], high[:1, 128:], rest[:1, :128], rest[:1, 128:], jnp.zeros((4, 128), F32)], axis=0
    )
    extra = jnp.broadcast_to(extra[None], (32, 8, 128))
    for n, grad in enumerate((grad_query, grad_key, grad_value, grad_output)):
        for j in range(2):
            tiles = grad[:, j * 128:(j + 1) * 128].reshape(32, 8, 128)
            weight_ref[n * 32:(n + 1) * 32, j] = jnp.concatenate([tiles, extra], axis=1).astype(BF)


def attend(x, partners, wk, wv, vn, cot, prepared):
    vmem = pl.BlockSpec(memory_space=pltpu.VMEM)
    sds = jax.ShapeDtypeStruct
    return pl.pallas_call(
        attend_kernel,
        out_shape=[sds((D, BN), BF)] + [sds((BN, D), BF)] * 7 + [sds((128, 2, 16, 128), BF)],
        in_specs=[vmem] * 19,
        out_specs=[vmem] * 9,
        scratch_shapes=[
            pltpu.VMEM((2, KEYS, 128), BF),
            pltpu.VMEM((2, KEYS, 128), BF),
            pltpu.VMEM((HEADS, HD + 16, KEYS), BF),
            pltpu.VMEM((HEADS, HD, KEYS), BF),
            pltpu.VMEM((CHUNKS, D, BN), BF),
            pltpu.VMEM((KEYS, BN), F32),
            pltpu.VMEM((KEYS, BN), F32),
            pltpu.VMEM((KEYS, BN), BF),
            pltpu.VMEM((KEYS, BN), BF),
            pltpu.VMEM((TILE, BN), BF),
            pltpu.VMEM((TILE, BN), BF),
            pltpu.VMEM((128, BN), BF),
            pltpu.VMEM((128, BN), BF),
            pltpu.VMEM((BN, 128), BF),
            pltpu.VMEM((BN, 128), BF),
            pltpu.VMEM((2, KEYS, 128), F32),
            pltpu.VMEM((2, KEYS, 128), F32),
            pltpu.VMEM((HEADS, HD, BN), BF),
            pltpu.VMEM((HEADS, HD, BN), BF),
            pltpu.VMEM((HEADS, 1, BN), F32),
            pltpu.VMEM((HEADS, 1, BN), F32),
            pltpu.VMEM((HEADS, 1, BN), F32),
            pltpu.VMEM((HEADS, 1, BN), F32),
            pltpu.VMEM((HEADS, HD, 128), F32),
            pltpu.VMEM((HEADS, HD, 128), F32),
        ],
        compiler_params=pltpu.CompilerParams(vmem_limit_bytes=56 * 1024 * 1024),
        cost_estimate=pl.CostEstimate(flops=8 * 10**9, bytes_accessed=4 * 10**6, transcendentals=10**7),
        name="attend",
    )(x, *partners, wk, wv, vn, cot, *prepared, wk.T, wv.T)


def late_kernel(
    flags_ref, x_ref, cot_ref, at_ref, dqm_ref, dk_ref, dv_ref, near_ref, low_ref, high_ref,
    wq_ref, wk_ref, wv_ref, wo_ref, layer_ref, part_ref,
):
    layer_ref[...] = (x_ref[...].astype(F32) + dot(at_ref[...].T, wo_ref[...])).astype(BF)
    part = cot_ref[...].astype(F32) + near_ref[...].astype(F32)
    part = part + dot_nt(dqm_ref[...], wq_ref[...])
    part = part + dot_nt(dk_ref[...], wk_ref[...]) + dot_nt(dv_ref[...], wv_ref[...])
    part = part + jnp.where(flags_ref[0] != 0, 0.0, low_ref[...].astype(F32))
    part_ref[...] = part + jnp.where(flags_ref[1] != 0, 0.0, high_ref[...].astype(F32))


def late(*operands):
    vmem = pl.BlockSpec(memory_space=pltpu.VMEM)
    return pl.pallas_call(
        late_kernel,
        out_shape=(jax.ShapeDtypeStruct((BN, D), BF), jax.ShapeDtypeStruct((BN, D), F32)),
        in_specs=[pl.BlockSpec(memory_space=pltpu.SMEM)] + [vmem] * 13,
        out_specs=[vmem] * 2,
        compiler_params=pltpu.CompilerParams(vmem_limit_bytes=60 * 1024 * 1024),
        cost_estimate=pl.CostEstimate(flops=3 * 10**9, bytes_accessed=8 * 10**6, transcendentals=0),
        name="late",
    )(*operands)


def finish_kernel(core_ref, part_ref, far_ref, mine_ref, given_ref, out_ref, *grad_refs):
    out_ref[...] = (part_ref[...] + far_ref[...].astype(F32)).astype(BF)
    mine, given = mine_ref[...].astype(F32), given_ref[...].astype(F32)
    left = jnp.where(core_ref[0] == 0, mine, given).reshape(4, D, 128)
    right = jnp.where(core_ref[0] == 0, given, mine).reshape(4, D, 128)
    for n, grad_ref in enumerate(grad_refs):
        grad_ref[:, :128] = left[n]
        grad_ref[:, 128:] = right[n]


def finish(core, part, far, mine, given):
    vmem = pl.BlockSpec(memory_space=pltpu.VMEM)
    return pl.pallas_call(
        finish_kernel,
        out_shape=[jax.ShapeDtypeStruct((BN, D), BF)] + [jax.ShapeDtypeStruct((D, D), F32)] * 4,
        in_specs=[pl.BlockSpec(memory_space=pltpu.SMEM)] + [vmem] * 4,
        out_specs=[vmem] * 5,
        compiler_params=pltpu.CompilerParams(vmem_limit_bytes=60 * 1024 * 1024),
        cost_estimate=pl.CostEstimate(flops=10**6, bytes_accessed=4 * 10**6, transcendentals=0),
        name="finish",
    )(core, part, far, mine, given)


def exchange(array, distance):
    return lax.ppermute(array, "blk", [(i, i ^ distance) for i in range(lax.axis_size("blk"))])


def exchange_by(array, step):
    near_bits = DISTANT - 1
    steps = [d for d in range(1, lax.axis_size("blk")) if not d & DISTANT]
    branches = [functools.partial(exchange, distance=d) for d in steps]
    place = (step // (2 * DISTANT)) * DISTANT + (step & near_bits)
    return lax.switch(place - 1, branches, array)


def body(
    features, w_query, key_weight, value_weight, w_output, virtual_node, cotangent, local_mask,
    counts, shifts,
):
    largest = lax.axis_size("blk") - 1
    low = jnp.min(jnp.where(shifts == 1, largest + 1, shifts))
    high = jnp.max(jnp.where(shifts == largest, 0, shifts))
    own = counts[0]
    halves = jnp.stack([own & 255, own >> 8]).astype(BF)
    tail = jnp.zeros((SENT - BN, D), BF).at[:2].set(jnp.broadcast_to(halves[:, None], (2, D)))
    sent = jnp.concatenate([features, tail], axis=0)
    far_copy, near_copy = exchange(sent, largest), exchange(sent, 1)
    low_far, high_far = low & DISTANT != 0, high & DISTANT != 0
    low_step = jnp.where(low_far, low ^ largest, low)
    high_step = jnp.where(high_far, high ^ largest, high)
    partners = [
        far_copy, near_copy,
        exchange_by(jnp.where(low_far, far_copy, sent), low_step),
        exchange_by(jnp.where(high_far, far_copy, sent), high_step),
    ]
    vn = virtual_node[None, :]
    prepared = prepare(
        counts, features, w_query, key_weight, value_weight, w_output, vn, cotangent, local_mask
    )
    attn_t, dquery, dkey, dvalue, back_far, back_near, back_low, back_high, weights = attend(
        features, partners, key_weight, value_weight, vn, cotangent, prepared
    )
    everyone = ("blk", "sub")
    count_sub = lax.axis_size("sub")
    devices = lax.axis_size("blk") * count_sub
    same_core = [[i for i in range(devices) if i % 2 == core] for core in range(2)]
    siblings = [(i, i ^ 1) for i in range(count_sub)]

    scattered = lax.all_to_all(weights.reshape(devices, 16, 128), everyone, 0, 0)
    near = exchange(back_near, 1)
    low_part = exchange_by(back_low, low_step)
    high_part = exchange_by(back_high, high_step)
    onward = (
        back_far.astype(F32)
        + jnp.where(low_far, low_part.astype(F32), 0.0)
        + jnp.where(high_far, high_part.astype(F32), 0.0)
    ).astype(BF)
    far = exchange(onward, largest)
    flags = jnp.stack([low_far, high_far]).astype(jnp.int32)
    layer_out, part = late(
        flags, features, cotangent, attn_t, dquery, dkey, dvalue, near, low_part, high_part,
        w_query, key_weight, value_weight, w_output,
    )
    scattered, layer_out, part = lax.optimization_barrier((scattered, layer_out, part))
    chunk = jnp.sum(scattered.astype(F32), axis=0)
    grad_virtual = (chunk[8:10] + chunk[10:12]).reshape(D)

    def gather(tiles):
        summed = lax.all_to_all(tiles, everyone, 0, 0, axis_index_groups=same_core)
        return summed, lax.ppermute(summed, "sub", siblings)

    summed, given = lax.cond(
        shifts[0] > 0, gather, lambda tiles: (tiles, tiles),
        jnp.broadcast_to(chunk[:8].astype(BF), (devices // 2, 8, 128)),
    )
    core = (lax.axis_index("sub") % 2).astype(jnp.int32)[None]
    total, *grads = finish(core, part, far, summed, given)
    return (
        layer_out, total, grads[0], grads[1], grads[2], grads[3], grad_virtual,
    )


def solution(mesh):
    return jax.shard_map(
        body,
        mesh=mesh,
        in_specs=(
            P(("blk", "sub"), None), P(), P(), P(), P(), P(), P(("blk", "sub"), None),
            P(("blk", "sub"), None), P(("blk", "sub")), P(),
        ),
        out_specs=(P(("blk", "sub"), None), P(("blk", "sub"), None), P(), P(), P(), P(), P()),
        check_vma=False,
    )
```

```python
import functools
import math

import jax
import jax.numpy as jnp
from jax import lax
from jax.experimental import pallas as pl
from jax.experimental.pallas import tpu as pltpu
from jax.sharding import PartitionSpec as P

D = 256
HEADS = 8
HD = D // HEADS
GROUP = 128 // HD
CHUNKS = 5
BN = 512
KEYS = CHUNKS * BN
SENT = BN + 16
NEG_FILL = -1000000000.0
SCALE = 1.0 / math.sqrt(HD)
LOG2E = 1.0 / math.log(2.0)
LN2 = math.log(2.0)
TILE = 512
DISTANT = 4
BF = jnp.bfloat16
F32 = jnp.float32


def dot(a, b):
    return jnp.dot(a, b, preferred_element_type=F32)


def dot_nt(a, b):
    return lax.dot_general(a, b, (((1,), (1,)), ((), ())), preferred_element_type=F32)


def dot_nt_exact(a, b):
    return lax.dot_general(
        a, b.astype(F32), (((1,), (1,)), ((), ())), precision=lax.Precision.HIGHEST,
        preferred_element_type=F32,
    )


def prepare_kernel(
    count_ref, x_ref, wq_ref, wk_ref, wv_ref, wo_ref, vn_ref, cot_ref, mask_ref,
    qmt, qm, gt, qs_ref, g_ref, bias, sv, dpv,
):
    vn = jnp.broadcast_to(vn_ref[...], (16, D))
    vk = dot(vn, wk_ref[...]).astype(BF)
    vv = dot(vn, wv_ref[...]).astype(BF)

    qs = (dot(x_ref[...], wq_ref[...]) * (SCALE * LOG2E)).astype(BF)
    qs_ref[...] = qs
    qt = qs.T
    g = dot_nt(cot_ref[...], wo_ref[...]).astype(BF)
    g_ref[...] = g
    gt_all = g.T
    gt[...] = gt_all.reshape(HEADS, HD, BN)
    qmt[...] = jnp.zeros_like(qmt)
    lane_head = lax.broadcasted_iota(jnp.int32, (BN, 128), 1) // HD
    for h in range(HEADS):
        r = h % GROUP
        lo = (h // GROUP) * 128
        qmt[h, r * HD:(r + 1) * HD, :] = qt[h * HD:(h + 1) * HD]
        qm[h] = jnp.where(lane_head == r, qs[:, lo:lo + 128], jnp.zeros((), BF))

    head_of = lax.broadcasted_iota(jnp.int32, (16, D), 1) // HD
    diag = head_of == lax.broadcasted_iota(jnp.int32, (16, D), 0)
    sv[...] = dot(jnp.where(diag, vk, jnp.zeros((), BF)), qt)[:HEADS].reshape(HEADS, 1, BN) + math.log2(BN)
    dpv[...] = dot(jnp.where(diag, vv, jnp.zeros((), BF)), gt_all)[:HEADS].reshape(HEADS, 1, BN)

    key_row = lax.broadcasted_iota(jnp.int32, (BN, BN), 0)
    query_col = lax.broadcasted_iota(jnp.int32, (BN, BN), 1)
    linked = jnp.where(mask_ref[...] != 0, 1.0, 0.0).astype(BF).T.astype(F32)
    ok = ((linked != 0.0) | (key_row == query_col)) & (key_row < count_ref[0])
    bias[...] = jnp.where(ok, 0.0, NEG_FILL).astype(BF)


def prepare(count, x, wq, wk, wv, wo, vn, cot, mask):
    vmem = pl.BlockSpec(memory_space=pltpu.VMEM)
    sds = jax.ShapeDtypeStruct
    return pl.pallas_call(
        prepare_kernel,
        out_shape=(
            sds((HEADS, 128, BN), BF), sds((HEADS, BN, 128), BF), sds((HEADS, HD, BN), BF),
            sds((BN, D), BF), sds((BN, D), BF), sds((BN, BN), BF),
            sds((HEADS, 1, BN), F32), sds((HEADS, 1, BN), F32),
        ),
        in_specs=[pl.BlockSpec(memory_space=pltpu.SMEM)] + [vmem] * 8,
        out_specs=[vmem] * 8,
        compiler_params=pltpu.CompilerParams(vmem_limit_bytes=60 * 1024 * 1024),
        cost_estimate=pl.CostEstimate(flops=2 * 10**9, bytes_accessed=6 * 10**6, transcendentals=0),
        name="prepare",
    )(count, x, wq, wk, wv, wo, vn, cot, mask)


def attend_kernel(
    x_ref, p0_ref, p1_ref, p2_ref, p3_ref, wk_ref, wv_ref, vn_ref, cot_ref,
    qmt, qm, gt, qs_ref, g_ref, bias, sv, dpv, wk_t_ref, wv_t_ref, wq_t_ref, wo_ref,
    layer_ref, own_ref, b0_ref, b1_ref, b2_ref, b3_ref, weight_ref,
    ks, vs, vta, k0t, xt, s_even, s_odd, p_even, p_odd, gmt_even, gmt_odd,
    gm_even, gm_odd, dk_acc, dv_acc, attn_t, dq_t, dsv, pvn, tops, deltas, vk_cols, vv_cols,
):
    parts = (x_ref, p0_ref, p1_ref, p2_ref, p3_ref)
    wk, wv = wk_ref[...], wv_ref[...]
    vn = jnp.broadcast_to(vn_ref[...], (16, D))
    vk = dot(vn, wk).astype(BF)
    vv = dot(vn, wv).astype(BF)
    head_of = lax.broadcasted_iota(jnp.int32, (16, D), 1) // HD
    diag = head_of == lax.broadcasted_iota(jnp.int32, (16, D), 0)
    vk_cols[...] = jnp.broadcast_to(vk[:1].astype(F32), (128, D)).T.reshape(HEADS, HD, 128)
    vv_cols[...] = jnp.broadcast_to(vv[:1].astype(F32), (128, D)).T.reshape(HEADS, HD, 128)

    row_no = lax.broadcasted_iota(jnp.int32, (BN, D), 0).astype(F32)
    lane_no = lax.broadcasted_iota(jnp.int32, (16, BN), 1).astype(F32)
    for c in range(CHUNKS):
        rows = slice(c * BN, (c + 1) * BN)
        xc = parts[c][:BN, :]
        k32 = dot(xc, wk)
        v32 = dot(xc, wv)
        k = k32.astype(BF)
        live_row = jnp.ones((16, BN), BF)
        if c:
            tail = parts[c][BN:, :].astype(F32)
            count = tail[0:1, 0:1] + 256.0 * tail[1:2, 0:1]
            live = row_no < count
            k = jnp.where(live, k, jnp.broadcast_to(vk[:1], (BN, D)))
            k32 = jnp.where(live, k32, 0.0)
            v32 = jnp.where(live, v32, 0.0)
            live_row = jnp.where(lane_no < count, 1.0, 0.0).astype(BF)
        v = v32.astype(BF)
        for gi in range(2):
            ks[gi, rows, :] = k[:, gi * 128:(gi + 1) * 128]
            vs[gi, rows, :] = v[:, gi * 128:(gi + 1) * 128]
        vt = v.T
        k0t[:, :, rows] = k32.astype(BF).T.reshape(HEADS, HD, BN)
        xt[c] = xc.T
        for h in range(HEADS):
            vta[h, :HD, rows] = vt[h * HD:(h + 1) * HD]
            vta[h, HD:, rows] = live_row

    dk_acc[...] = jnp.zeros_like(dk_acc)
    dv_acc[...] = jnp.zeros_like(dv_acc)
    row_head = lax.broadcasted_iota(jnp.int32, (128, BN), 0) // HD
    s_bufs, p_bufs = (s_even, s_odd), (p_even, p_odd)
    gmt_bufs, gm_bufs = (gmt_even, gmt_odd), (gm_even, gm_odd)

    def step(first, second, third, parity):
        peak = jnp.full((8, BN), -jnp.inf, F32)
        out = jnp.zeros((HD + 16, BN), F32)
        if second is not None:
            top2 = tops[second]
        if third is not None:
            delta3 = deltas[third]
            gi3 = third // GROUP
            dq = vk_cols[third][:, :1] * dsv[third]
        for t in range(KEYS // TILE):
            rows = pl.ds(t * TILE, TILE)
            if first is not None:
                s = dot(ks[first // GROUP, rows, :], qmt[first])
                if (t + 1) * TILE <= BN:
                    s = s + bias[rows, :].astype(F32)
                s_bufs[parity][rows, :] = s
                peak = jnp.maximum(peak, jnp.max(s.reshape(TILE // 8, 8, BN), axis=0))
            if third is not None:
                p3 = p_bufs[parity][rows, :]
                ds = (dot(vs[gi3, rows, :], gmt_bufs[parity][...]) - delta3).astype(BF) * p3
            if second is not None:
                p = jnp.exp2(s_bufs[1 - parity][rows, :] - top2).astype(BF)
                p_bufs[1 - parity][rows, :] = p
                out = out + dot(vta[second, :, rows], p)
            if third is not None:
                dv_acc[gi3, rows, :] += dot(p3, gm_bufs[parity][...])
                dk_acc[gi3, rows, :] += dot(ds, qm[third])
                dq = dq + dot(k0t[third, :, rows], ds)
        if first is not None:
            tops[first] = jnp.maximum(sv[first], jnp.max(peak, axis=0, keepdims=True))
        if second is not None:
            pv = jnp.exp2(sv[second] - top2)
            inv = 1.0 / (out[HD:HD + 1] + pv)
            attn_h = ((out[:HD] + vv_cols[second][:, :1] * pv) * inv).astype(BF)
            attn_t[second] = attn_h
            g_h = gt[second].astype(F32)
            delta = jnp.sum(g_h * attn_h.astype(F32), axis=0, keepdims=True) * inv
            deltas[second] = delta
            g_n = g_h * inv
            gmt32 = jnp.where(
                row_head == second % GROUP, jnp.concatenate([g_n] * GROUP, axis=0), 0.0
            )
            gmt_bufs[1 - parity][...] = gmt32.astype(BF)
            gm_bufs[1 - parity][...] = gmt32.astype(BF).T
            dsv[second] = pv * (dpv[second] * inv - delta)
            pvn[second] = pv * inv
        if third is not None:
            dq_t[third] = (dq * SCALE).astype(BF)

    step(0, None, None, 0)
    step(1, 0, None, 1)

    @pl.loop(1, HEADS // 2)
    def _(pair):
        h = 2 * pair
        step(h, h - 1, h - 2, 0)
        step(h + 1, h, h - 1, 1)

    step(None, HEADS - 1, HEADS - 2, 0)
    step(None, None, HEADS - 1, 1)

    at = attn_t[...].reshape(D, BN)
    layer_ref[...] = (x_ref[...].astype(F32) + dot(at.T, wo_ref[...])).astype(BF)
    dqm = dq_t[...].reshape(D, BN).T

    grad_query = dot(xt[0], dqm)
    grad_output = dot(at, cot_ref[...])
    keep = diag[:HEADS]
    dsv_all = dsv[...].reshape(HEADS, BN)
    pvn_all = pvn[...].reshape(HEADS, BN)
    vkey = jnp.sum(jnp.where(keep, dot(dsv_all.astype(BF), qs_ref[...]), 0.0), axis=0, keepdims=True) * LN2
    vvalue = jnp.sum(jnp.where(keep, dot(pvn_all.astype(BF), g_ref[...]), 0.0), axis=0, keepdims=True)
    vn_col = jnp.broadcast_to(vn_ref[...].astype(F32), (128, D)).T[:, :1]
    grad_key = vn_col * vkey
    grad_value = vn_col * vvalue
    backs = (None, b0_ref, b1_ref, b2_ref, b3_ref)
    for c in range(CHUNKS):
        rows = slice(c * BN, (c + 1) * BN)
        dk = jnp.concatenate([dk_acc[0, rows, :], dk_acc[1, rows, :]], axis=1) * LN2
        dv = jnp.concatenate([dv_acc[0, rows, :], dv_acc[1, rows, :]], axis=1)
        if c:
            tail = parts[c][BN:, :].astype(F32)
            live = row_no < tail[0:1, 0:1] + 256.0 * tail[1:2, 0:1]
            dk = jnp.where(live, dk, 0.0)
            dv = jnp.where(live, dv, 0.0)
        dk = dk.astype(BF)
        dv = dv.astype(BF)
        grad_key = grad_key + dot(xt[c], dk)
        grad_value = grad_value + dot(xt[c], dv)
        back = dot(dk, wk_t_ref[...]) + dot(dv, wv_t_ref[...])
        if c:
            backs[c][...] = back.astype(BF)
        else:
            own_ref[...] = back + dot(dqm, wq_t_ref[...]) + cot_ref[...].astype(F32)
    virt = dot_nt_exact(jnp.broadcast_to(vkey, (8, D)), wk) + dot_nt_exact(
        jnp.broadcast_to(vvalue, (8, D)), wv
    )
    high = virt.astype(BF).astype(F32)
    rest = virt - high
    extra = jnp.concatenate(
        [high[:1, :128], high[:1, 128:], rest[:1, :128], rest[:1, 128:], jnp.zeros((4, 128), F32)], axis=0
    )
    extra = jnp.broadcast_to(extra[None], (32, 8, 128))
    for n, grad in enumerate((grad_query, grad_key, grad_value, grad_output)):
        for j in range(2):
            tiles = grad[:, j * 128:(j + 1) * 128].reshape(32, 8, 128)
            weight_ref[n * 32:(n + 1) * 32, j] = jnp.concatenate([tiles, extra], axis=1).astype(BF)


def attend(x, partners, wq, wk, wv, wo, vn, cot, prepared):
    vmem = pl.BlockSpec(memory_space=pltpu.VMEM)
    sds = jax.ShapeDtypeStruct
    return pl.pallas_call(
        attend_kernel,
        out_shape=[sds((BN, D), BF), sds((BN, D), F32)] + [sds((BN, D), BF)] * 4 + [sds((128, 2, 16, 128), BF)],
        in_specs=[vmem] * 21,
        out_specs=[vmem] * 7,
        scratch_shapes=[
            pltpu.VMEM((2, KEYS, 128), BF),
            pltpu.VMEM((2, KEYS, 128), BF),
            pltpu.VMEM((HEADS, HD + 16, KEYS), BF),
            pltpu.VMEM((HEADS, HD, KEYS), BF),
            pltpu.VMEM((CHUNKS, D, BN), BF),
            pltpu.VMEM((KEYS, BN), F32),
            pltpu.VMEM((KEYS, BN), F32),
            pltpu.VMEM((KEYS, BN), BF),
            pltpu.VMEM((KEYS, BN), BF),
            pltpu.VMEM((128, BN), BF),
            pltpu.VMEM((128, BN), BF),
            pltpu.VMEM((BN, 128), BF),
            pltpu.VMEM((BN, 128), BF),
            pltpu.VMEM((2, KEYS, 128), F32),
            pltpu.VMEM((2, KEYS, 128), F32),
            pltpu.VMEM((HEADS, HD, BN), BF),
            pltpu.VMEM((HEADS, HD, BN), BF),
            pltpu.VMEM((HEADS, 1, BN), F32),
            pltpu.VMEM((HEADS, 1, BN), F32),
            pltpu.VMEM((HEADS, 1, BN), F32),
            pltpu.VMEM((HEADS, 1, BN), F32),
            pltpu.VMEM((HEADS, HD, 128), F32),
            pltpu.VMEM((HEADS, HD, 128), F32),
        ],
        compiler_params=pltpu.CompilerParams(vmem_limit_bytes=56 * 1024 * 1024),
        cost_estimate=pl.CostEstimate(flops=8 * 10**9, bytes_accessed=4 * 10**6, transcendentals=10**7),
        name="attend",
    )(x, *partners, wk, wv, vn, cot, *prepared, wk.T, wv.T, wq.T, wo)


def finish_kernel(
    flags_ref, own_ref, near_ref, far_ref, low_ref, high_ref, mine_ref, given_ref,
    out_ref, *grad_refs,
):
    total = own_ref[...] + near_ref[...].astype(F32) + far_ref[...].astype(F32)
    total = total + jnp.where(flags_ref[0] != 0, 0.0, low_ref[...].astype(F32))
    total = total + jnp.where(flags_ref[1] != 0, 0.0, high_ref[...].astype(F32))
    out_ref[...] = total.astype(BF)
    mine, given = mine_ref[...].astype(F32), given_ref[...].astype(F32)
    left = jnp.where(flags_ref[2] == 0, mine, given).reshape(4, D, 128)
    right = jnp.where(flags_ref[2] == 0, given, mine).reshape(4, D, 128)
    for n, grad_ref in enumerate(grad_refs):
        grad_ref[:, :128] = left[n]
        grad_ref[:, 128:] = right[n]


def finish(flags, own, near, far, low, high, mine, given):
    vmem = pl.BlockSpec(memory_space=pltpu.VMEM)
    return pl.pallas_call(
        finish_kernel,
        out_shape=[jax.ShapeDtypeStruct((BN, D), BF)] + [jax.ShapeDtypeStruct((D, D), F32)] * 4,
        in_specs=[pl.BlockSpec(memory_space=pltpu.SMEM)] + [vmem] * 7,
        out_specs=[vmem] * 5,
        compiler_params=pltpu.CompilerParams(vmem_limit_bytes=60 * 1024 * 1024),
        cost_estimate=pl.CostEstimate(flops=10**6, bytes_accessed=4 * 10**6, transcendentals=0),
        name="finish",
    )(flags, own, near, far, low, high, mine, given)


def exchange(array, distance):
    return lax.ppermute(array, "blk", [(i, i ^ distance) for i in range(lax.axis_size("blk"))])


def exchange_by(array, step):
    near_bits = DISTANT - 1
    steps = [d for d in range(1, lax.axis_size("blk")) if not d & DISTANT]
    branches = [functools.partial(exchange, distance=d) for d in steps]
    place = (step // (2 * DISTANT)) * DISTANT + (step & near_bits)
    return lax.switch(place - 1, branches, array)


def body(
    features, w_query, key_weight, value_weight, w_output, virtual_node, cotangent, local_mask,
    counts, shifts,
):
    largest = lax.axis_size("blk") - 1
    low = jnp.min(jnp.where(shifts == 1, largest + 1, shifts))
    high = jnp.max(jnp.where(shifts == largest, 0, shifts))
    own = counts[0]
    halves = jnp.stack([own & 255, own >> 8]).astype(BF)
    tail = jnp.zeros((SENT - BN, D), BF).at[:2].set(jnp.broadcast_to(halves[:, None], (2, D)))
    sent = jnp.concatenate([features, tail], axis=0)
    far_copy, near_copy = exchange(sent, largest), exchange(sent, 1)
    low_far, high_far = low & DISTANT != 0, high & DISTANT != 0
    low_step = jnp.where(low_far, low ^ largest, low)
    high_step = jnp.where(high_far, high ^ largest, high)
    partners = [
        far_copy, near_copy,
        exchange_by(jnp.where(low_far, far_copy, sent), low_step),
        exchange_by(jnp.where(high_far, far_copy, sent), high_step),
    ]
    vn = virtual_node[None, :]
    prepared = prepare(
        counts, features, w_query, key_weight, value_weight, w_output, vn, cotangent, local_mask
    )
    layer_out, own_grad, back_far, back_near, back_low, back_high, weights = attend(
        features, partners, w_query, key_weight, value_weight, w_output, vn, cotangent, prepared
    )
    everyone = ("blk", "sub")
    count_sub = lax.axis_size("sub")
    devices = lax.axis_size("blk") * count_sub
    same_core = [[i for i in range(devices) if i % 2 == core] for core in range(2)]
    siblings = [(i, i ^ 1) for i in range(count_sub)]

    scattered = lax.all_to_all(weights.reshape(devices, 16, 128), everyone, 0, 0)
    near = exchange(back_near, 1)
    low_part = exchange_by(back_low, low_step)
    high_part = exchange_by(back_high, high_step)
    onward = (
        back_far.astype(F32)
        + jnp.where(low_far, low_part.astype(F32), 0.0)
        + jnp.where(high_far, high_part.astype(F32), 0.0)
    ).astype(BF)
    far = exchange(onward, largest)
    scattered, onward, near = lax.optimization_barrier((scattered, onward, near))
    chunk = jnp.sum(scattered.astype(F32), axis=0)
    grad_virtual = (chunk[8:10] + chunk[10:12]).reshape(D)

    def gather(tiles):
        summed = lax.all_to_all(tiles, everyone, 0, 0, axis_index_groups=same_core)
        return summed, lax.ppermute(summed, "sub", siblings)

    summed, given = lax.cond(
        shifts[0] > 0, gather, lambda tiles: (tiles, tiles),
        jnp.broadcast_to(chunk[:8].astype(BF), (devices // 2, 8, 128)),
    )
    core = lax.axis_index("sub") % 2
    flags = jnp.stack([low_far.astype(jnp.int32), high_far.astype(jnp.int32), core.astype(jnp.int32)])
    total, *grads = finish(flags, own_grad, near, far, low_part, high_part, summed, given)
    return (
        layer_out, total, grads[0], grads[1], grads[2], grads[3], grad_virtual,
    )


def solution(mesh):
    return jax.shard_map(
        body,
        mesh=mesh,
        in_specs=(
            P(("blk", "sub"), None), P(), P(), P(), P(), P(), P(("blk", "sub"), None),
            P(("blk", "sub"), None), P(("blk", "sub")), P(),
        ),
        out_specs=(P(("blk", "sub"), None), P(("blk", "sub"), None), P(), P(), P(), P(), P()),
        check_vma=False,
    )
```
